128 devices in a mesh: batch: 8 (over z, y_lo), head: 4 (over x), blk: 4 (over y_hi, core).
Axes of the slice: x: 4, y: 4 (y_hi: 2, y_lo: 2; y = y_hi * 2 + y_lo), z: 4, core: 2. Of those that a mesh axis runs over, the one named last changes fastest.
Arguments:
- inputs: bfloat16 [8, 2048, 768], P('batch', ('head', 'blk')), may hold values from -4 to 4
- lengths: int32 [8], P('batch'), may hold values from 1025 to 2048, as said below
- joint_weight: bfloat16 [2, 768, 2304], P(None, ('batch', 'blk')), may hold values from -0.21875 to 0.21875
- query_bias: bfloat16 [2, 768], P(None, ('batch', 'blk')), may hold values from -1.1953125 to 1.1953125
- value_bias: bfloat16 [2, 768], P(None, ('batch', 'blk')), may hold values from -0.3984375 to 0.3984375
- output_weight: bfloat16 [2, 768, 768], P(None, ('batch', 'blk')), may hold values from -0.75 to 0.75
- output_bias: bfloat16 [2, 768], P(None, ('batch', 'blk')), may hold values from -0.3984375 to 0.3984375
- first_gain: bfloat16 [2, 768], P(None, ('batch', 'blk')), may hold values from 0.5 to 1.5
- first_shift: bfloat16 [2, 768], P(None, ('batch', 'blk')), may hold values from -0.3984375 to 0.3984375
- up_weight: bfloat16 [2, 768, 3072], P(None, ('batch', 'blk')), may hold values from -0.21875 to 0.21875
- up_bias: bfloat16 [2, 3072], P(None, ('batch', 'blk')), may hold values from -1.1953125 to 1.1953125
- down_weight: bfloat16 [2, 3072, 768], P(None, ('batch', 'blk')), may hold values from -0.15625 to 0.15625
- down_bias: bfloat16 [2, 768], P(None, ('batch', 'blk')), may hold values from -0.3984375 to 0.3984375
- second_gain: bfloat16 [2, 768], P(None, ('batch', 'blk')), may hold values from 0.5 to 1.5
- second_shift: bfloat16 [2, 768], P(None, ('batch', 'blk')), may hold values from -0.3984375 to 0.3984375
- cotangent: bfloat16 [8, 2048, 768], P('batch', ('head', 'blk')), may hold values from -4 to 4
Outputs:
- activations: bfloat16 [2, 8, 2048, 768], P(None, 'batch', ('head', 'blk'))
- input_grad: float32 [8, 2048, 768], P('batch', ('head', 'blk'))
- joint_weight_grad: float32 [2, 768, 2304], P(None, ('batch', 'blk'))
- query_bias_grad: float32 [2, 768], P(None, ('batch', 'blk'))
- value_bias_grad: float32 [2, 768], P(None, ('batch', 'blk'))
- output_weight_grad: float32 [2, 768, 768], P(None, ('batch', 'blk'))
- output_bias_grad: float32 [2, 768], P(None, ('batch', 'blk'))
- first_gain_grad: float32 [2, 768], P(None, ('batch', 'blk'))
- first_shift_grad: float32 [2, 768], P(None, ('batch', 'blk'))
- up_weight_grad: float32 [2, 768, 3072], P(None, ('batch', 'blk'))
- up_bias_grad: float32 [2, 3072], P(None, ('batch', 'blk'))
- down_weight_grad: float32 [2, 3072, 768], P(None, ('batch', 'blk'))
- down_bias_grad: float32 [2, 768], P(None, ('batch', 'blk'))
- second_gain_grad: float32 [2, 768], P(None, ('batch', 'blk'))
- second_shift_grad: float32 [2, 768], P(None, ('batch', 'blk'))
The draws below stay inside these ranges and needn't reach their ends.
Inputs may be any that keep to these rules, and one draw needn't show every extreme that they name: Positions lengths[b] and later of sequence b are padding, whose keys are masked.
All inputs are finite; a program needn't handle non-finite values.
Results may differ from the reference program's by a relative error of at most 0.025.
Values may be sent and summed in bfloat16 or wider, within the bound.
A program may use at most 256 MiB of HBM per device.

```python
import jax
import jax.numpy as jnp
from jax import lax

D = 768
HEADS = 12
HD = 64
FF = 3072
LAYERS = 2
BATCH = 8
SEQ = 2048


def draw_lengths(key, part):
    key = jax.random.fold_in(key, 7)
    range_key, order_key = jax.random.split(key)
    picked = jax.random.randint(range_key, (BATCH,), SEQ // 2 + 1, SEQ + 1, dtype=jnp.int32)
    shuffled = jax.random.permutation(order_key, BATCH)
    picked = picked.at[shuffled[0]].set(SEQ)
    if BATCH >= 3:
        picked = picked.at[shuffled[1]].set(SEQ // 2 + 1)
    return picked


def steps_of(own_key, dims, cuts, low, largest):
    level = 1.0
    for position, blocks in cuts:
        draws = jax.random.uniform(jax.random.fold_in(jax.random.fold_in(own_key, 6), position), (blocks,), jnp.float32, low / len(cuts), largest / len(cuts))
        level = level * jnp.repeat(jnp.exp(draws), dims[position] // blocks).reshape((-1,) + (1,) * (len(dims) - 1 - position))
    return level


def scatter_about(stream_key, shape, width, limit, cuts=(), held_as=jnp.bfloat16):
    array = width * jax.random.normal(stream_key, shape, jnp.float32)
    if cuts:
        array = array * steps_of(stream_key, shape, cuts, -0.22, 0.18)
    return jnp.clip(array, -limit, limit).astype(held_as)


def setup_inputs(seed: int = 0) -> dict:
    splits = jax.random.split(jax.random.key(seed), 17)
    return {
        "inputs": scatter_about(splits[0], (BATCH, SEQ, D), 1.0, 4.0, ((0, 8), (1, 16))),
        "lengths": draw_lengths(jax.random.fold_in(splits[16], 71), 0),
        "joint_weight": scatter_about(splits[2], (LAYERS, D, 3 * D), D ** -0.5, 0.21875, ((1, 32),)),
        "query_bias": scatter_about(splits[3], (LAYERS, D), 0.3, 1.1953125, ((1, 32),)),
        "value_bias": scatter_about(splits[4], (LAYERS, D), 0.1, 0.3984375, ((1, 32),)),
        "output_weight": scatter_about(splits[5], (LAYERS, D, D), HD ** -0.5, 0.75, ((1, 32),)),
        "output_bias": scatter_about(splits[6], (LAYERS, D), 0.1, 0.3984375, ((1, 32),)),
        "first_gain": jnp.clip(1.0 + 0.1 * jax.random.normal(splits[7], (LAYERS, D), jnp.float32), 0.5, 1.5).astype(jnp.bfloat16),
        "first_shift": scatter_about(splits[8], (LAYERS, D), 0.1, 0.3984375, ((1, 32),)),
        "up_weight": scatter_about(splits[9], (LAYERS, D, FF), D ** -0.5, 0.21875, ((1, 32),)),
        "up_bias": scatter_about(splits[10], (LAYERS, FF), 0.3, 1.1953125, ((1, 32),)),
        "down_weight": scatter_about(splits[11], (LAYERS, FF, D), (FF // 2) ** -0.5, 0.15625, ((1, 32),)),
        "down_bias": scatter_about(splits[12], (LAYERS, D), 0.1, 0.3984375, ((1, 32),)),
        "second_gain": jnp.clip(1.0 + 0.1 * jax.random.normal(splits[13], (LAYERS, D), jnp.float32), 0.5, 1.5).astype(jnp.bfloat16),
        "second_shift": scatter_about(splits[14], (LAYERS, D), 0.1, 0.3984375, ((1, 32),)),
        "cotangent": scatter_about(splits[15], (BATCH, SEQ, D), 1.0, 4.0, ((0, 8), (1, 16))),
    }


EPSILON = 1e-12
MASKED = -1e+30
HIGHEST = lax.Precision.HIGHEST

@jax.custom_vjp
def low(v):
    return lax.optimization_barrier(v.astype(jnp.bfloat16)).astype(jnp.float32)

@jax.custom_vjp
def low_back(v):
    return v

def low_keep(v):
    return (low(v), None)

def low_pass(kept, grad):
    return (grad,)

def back_keep(v):
    return (v, None)

def back_low(kept, grad):
    return (low(grad),)
low.defvjp(low_keep, low_pass)
low_back.defvjp(back_keep, back_low)

def matmul_high(operand, matrix):
    return jnp.dot(operand, matrix, precision=HIGHEST, preferred_element_type=jnp.float32)

def layer_norm(values, gain, shift):
    average = lax.optimization_barrier(jnp.mean(values, axis=-1, keepdims=True))
    centered = values - average
    variance = lax.optimization_barrier(jnp.mean(centered * centered, axis=-1, keepdims=True))
    return centered * lax.rsqrt(variance + EPSILON) * gain + shift

def to_heads(matrix):
    return matrix.reshape(SEQ, HEADS, HD).transpose(1, 0, 2)

def sequence_attention(sequence_items):
    queries, key_rows, value_rows, length = sequence_items
    key_valid = jnp.arange(SEQ, dtype=jnp.int32) < length
    score_scale = HD ** (-0.5)

    def one_head(pieces):
        query_head, key_head, value_head = pieces
        raw_scores = low_back(jnp.dot(query_head, key_head.T, precision=HIGHEST))
        scores = jnp.where(key_valid[None, :], raw_scores * score_scale, MASKED)
        row_peak = lax.optimization_barrier(jnp.max(scores, axis=-1, keepdims=True))
        shifted = jnp.exp(scores - row_peak)
        probabilities = shifted / lax.optimization_barrier(jnp.sum(shifted, axis=-1, keepdims=True))
        return jnp.dot(low(probabilities), value_head, precision=HIGHEST)
    mixed_heads = lax.map(jax.checkpoint(one_head), (to_heads(queries), to_heads(key_rows), to_heads(value_rows)))
    return mixed_heads.transpose(1, 0, 2).reshape(SEQ, D)

def forward_layers(start_rows, params, lengths):
    joint_weight, query_bias, value_bias, output_weight, output_bias, first_gain, first_shift, up_weight, up_bias, down_weight, down_bias, second_gain, second_shift = params
    hidden = start_rows.reshape(BATCH * SEQ, D)
    layer_outputs = []
    for layer_index in range(LAYERS):
        projected = matmul_high(hidden, joint_weight[layer_index])
        queries = low_back(low(projected[:, :D] + query_bias[layer_index]))
        key_rows = low_back(low(projected[:, D:2 * D]))
        value_rows = low_back(low(projected[:, 2 * D:] + value_bias[layer_index]))
        mixed = lax.map(sequence_attention, (queries.reshape(BATCH, SEQ, D), key_rows.reshape(BATCH, SEQ, D), value_rows.reshape(BATCH, SEQ, D), lengths))
        mixed = low_back(low(mixed.reshape(BATCH * SEQ, D)))
        branch = low_back(matmul_high(mixed, output_weight[layer_index]) + output_bias[layer_index])
        first_norm = layer_norm(hidden + branch, first_gain[layer_index], first_shift[layer_index])
        upward = low_back(matmul_high(low(first_norm), up_weight[layer_index]) + up_bias[layer_index])
        activated = low(jax.nn.gelu(upward, approximate=False))
        lowered = low_back(matmul_high(activated, down_weight[layer_index]) + down_bias[layer_index])
        result = layer_norm(first_norm + lowered, second_gain[layer_index], second_shift[layer_index])
        layer_outputs.append(result)
        hidden = low(result)
    return (result, jnp.stack(layer_outputs))

def reference(inputs, lengths, joint_weight, query_bias, value_bias, output_weight, output_bias, first_gain, first_shift, up_weight, up_bias, down_weight, down_bias, second_gain, second_shift, cotangent):
    params = tuple((member.astype(jnp.float32) for member in (joint_weight, query_bias, value_bias, output_weight, output_bias, first_gain, first_shift, up_weight, up_bias, down_weight, down_bias, second_gain, second_shift)))
    start_rows = inputs.astype(jnp.float32)

    def run_layers(start_values, weight_values):
        return forward_layers(start_values, weight_values, lengths)
    result, pullback, layer_outputs = jax.vjp(run_layers, start_rows, params, has_aux=True)
    grad_start, grad_params = pullback(cotangent.astype(jnp.float32).reshape(BATCH * SEQ, D))
    activations = layer_outputs.reshape(LAYERS, BATCH, SEQ, D).astype(jnp.bfloat16)
    return (activations, grad_start, grad_params[0], grad_params[1], grad_params[2], grad_params[3], grad_params[4], grad_params[5], grad_params[6], grad_params[7], grad_params[8], grad_params[9], grad_params[10], grad_params[11], grad_params[12])
```

```python
import jax
import jax.numpy as jnp
from jax import lax
from jax.experimental import pallas as pl
from jax.experimental.pallas import tpu as pltpu
from jax.sharding import PartitionSpec as P

HEADS = 12
HD = 64
LAYERS = 2


EPSILON = 1e-12
MASKED = -1e30


def sent_together(arrays, axis, split_dim, concat_dim, along):
    widths = [a.shape[along] for a in arrays]
    both = jnp.concatenate(arrays, axis=along)
    whole = lax.all_to_all(both, axis, split_axis=split_dim, concat_axis=concat_dim, tiled=True)
    return tuple(jnp.split(whole, [sum(widths[:k]) for k in range(1, len(widths))], axis=along))


def sent_together_2(arrays, axis, dim, along):
    widths = [a.shape[along] for a in arrays]
    both = jnp.concatenate(arrays, axis=along)
    whole = lax.all_gather(both, axis, axis=dim, tiled=True)
    return tuple(jnp.split(whole, [sum(widths[:k]) for k in range(1, len(widths))], axis=along))


def cut_along(array, dim, length):
    dims = array.shape
    blocks = array.reshape(*dims[:dim], length, dims[dim] // length, *dims[dim + 1 :])
    return jnp.moveaxis(blocks, dim, 0)


def sum_at_owner(array, axis, dim):
    length = lax.axis_size(axis)
    blocks = lax.all_to_all(cut_along(array, dim, length), axis, 0, 0, tiled=True)
    return jnp.sum(blocks.astype(jnp.float32), axis=0)


def layer_norm(values, gain, shift):
    average = jnp.mean(values, axis=-1, keepdims=True)
    centered = values - average
    variance = jnp.mean(centered * centered, axis=-1, keepdims=True)
    return centered * lax.rsqrt(variance + EPSILON) * gain + shift


def exact_gelu(values):
    return jax.nn.gelu(values, approximate=False)


def row_product(operand, matrix):
    return jnp.dot(operand, matrix, preferred_element_type=jnp.float32)


def inner_rows(operand, other):
    return lax.dot_general(
        operand, other, (((0,), (0,)), ((), ())), preferred_element_type=jnp.float32
    )


def times_transposed(operand, matrix):
    return lax.dot_general(
        operand, matrix, (((1,), (1,)), ((), ())), preferred_element_type=jnp.float32
    )


MESH = pl.DeviceIdType.MESH
ALL = slice(None)


def my_place():
    b, x, k = lax.axis_index("batch"), lax.axis_index("head"), lax.axis_index("blk")
    return {"z": b // 2, "y": (k // 2) * 2 + b % 2, "x": x, "c": k % 2}


def device_of(place):
    return (
        place["z"] * 2 + place["y"] % 2,
        place["x"],
        (place["y"] // 2) * 2 + place["c"],
    )


def peer_of(place, axis, step):
    other = dict(place)
    other[axis] = (place[axis] + step) % (2 if axis == "c" else 4)
    return other


def greet_all(place):
    barrier = pltpu.get_barrier_semaphore()
    peers = [peer_of(place, a, s) for a in ("x", "y", "z") for s in (1, 2, 3)]
    peers.append(peer_of(place, "c", 1))
    for p in peers:
        pl.semaphore_signal(barrier, inc=1, device_id=device_of(p), device_id_type=MESH)
    pl.semaphore_wait(barrier, len(peers))


def remote(src, dst, send, recv, place):
    return pltpu.make_async_remote_copy(
        src_ref=src,
        dst_ref=dst,
        send_sem=send,
        recv_sem=recv,
        device_id=device_of(place),
        device_id_type=MESH,
    )


PIECES = (
    (0, ("z", "y", "x")),
    (1, ("z", "y")),
    (2, ("y", "z")),
    (3, ("z", "y", "x")),
    (4, ("z", "y")),
    (5, ("y", "z")),
    (6, ("y", "z")),
)


def gather_kernel(*refs):
    n = len(PIECES)
    ins, outs = refs[:n], refs[n : 2 * n]
    send, recv, fsend, frecv, local = refs[2 * n :]
    me = my_place()
    partner = peer_of(me, "c", 1)

    def region(i, phase, place):
        array, order = PIECES[i]
        done = order[:phase]
        z = ALL if "z" in done else place["z"]
        y = (ALL, ALL) if "y" in done else (place["y"] % 2, place["y"] // 2)
        cols = ALL
        if "x" in order and "x" not in done:
            cols = pl.ds(pl.multiple_of(place["x"] * 768, 128), 768)
        return outs[i].at[z, y[0], y[1], place["c"], ALL, cols]

    def own(i):
        if "x" in PIECES[i][1]:
            return ins[i].at[ALL, pl.ds(pl.multiple_of(me["x"] * 768, 128), 768)]
        return ins[i]

    def step(i, phase, s):
        axis = PIECES[i][1][phase]
        src = own(i) if phase == 0 else region(i, phase, me)
        return remote(
            src,
            region(i, phase, me),
            send.at[i, phase, s - 1],
            recv.at[i, phase, s - 1],
            peer_of(me, axis, s),
        )

    def landed(i, phase, s):
        axis = PIECES[i][1][phase]
        place = peer_of(me, axis, 4 - s)
        r = region(i, phase, place)
        return remote(r, r, send.at[i, phase, s - 1], recv.at[i, phase, s - 1], place)

    def forward(i, phase, s):
        axis = PIECES[i][1][phase]
        r = region(i, phase, peer_of(me, axis, 4 - s))
        return remote(r, r, fsend.at[i, phase, s - 1], frecv.at[i, phase, s - 1], partner)

    def forwarded(i, phase, s):
        axis = PIECES[i][1][phase]
        r = region(i, phase, peer_of(partner, axis, 4 - s))
        return remote(r, r, fsend.at[i, phase, s - 1], frecv.at[i, phase, s - 1], partner)

    greet_all(me)
    copies, sends, fwds = [], [], []
    for i in range(n):
        for s in (2, 1, 3):
            c = step(i, 0, s)
            c.start()
            sends.append(c)
        c = pltpu.make_async_copy(own(i), region(i, 0, me), local.at[i])
        c.start()
        copies.append(c)
        c = remote(own(i), region(i, 0, me), fsend.at[i, 3, 0], frecv.at[i, 3, 0], partner)
        c.start()
        fwds.append(c)
    for c in copies:
        c.wait()
    for phase in range(3):
        for i in range(n):
            order = PIECES[i][1]
            if phase >= len(order):
                continue
            for s in (1, 3, 2):
                landed(i, phase, s).wait_recv()
                c = forward(i, phase, s)
                c.start()
                fwds.append(c)
            if phase + 1 < len(order):
                for s in (2, 1, 3):
                    c = step(i, phase + 1, s)
                    c.start()
                    sends.append(c)
    for i in range(n):
        r = region(i, 0, partner)
        remote(r, r, fsend.at[i, 3, 0], frecv.at[i, 3, 0], partner).wait_recv()
        for phase in range(len(PIECES[i][1])):
            for s in (1, 2, 3):
                forwarded(i, phase, s).wait_recv()
    for c in sends + fwds:
        c.wait_send()


def gather_weights(pieces):
    n = len(pieces)
    anyspace = pl.BlockSpec(memory_space=pl.ANY)
    return pl.pallas_call(
        gather_kernel,
        out_shape=[jax.ShapeDtypeStruct((4, 2, 2, 2, *p.shape), p.dtype) for p in pieces],
        in_specs=[anyspace] * n,
        out_specs=[anyspace] * n,
        scratch_shapes=[
            pltpu.SemaphoreType.DMA((n, 3, 3)),
            pltpu.SemaphoreType.DMA((n, 3, 3)),
            pltpu.SemaphoreType.DMA((n, 4, 3)),
            pltpu.SemaphoreType.DMA((n, 4, 3)),
            pltpu.SemaphoreType.DMA((n,)),
        ],
        compiler_params=pltpu.CompilerParams(collective_id=0, has_side_effects=True),
        name="gather_weights",
    )(*pieces)


THIRDS = (("x", "y", "z"), ("y", "z", "x"), ("z", "x", "y"))


def reduce_kernel(*refs):
    ins = refs[:11]
    joint_out, out_out, up_out, down_out, vec_out = refs[11:16]
    lhs, rhs, g, r1, s1, r2, s2, r3, last, vc, va = refs[16:27]
    csend, crecv, lsem, ps, pr, vs, vr = refs[27:]
    vec_in = ins[10]
    me = my_place()
    partner = peer_of(me, "c", 1)
    c = me["c"]
    greet_all(me)
    half = pl.ds(pl.multiple_of(c * 128, 128), 128)
    other_half = pl.ds(pl.multiple_of((1 - c) * 128, 128), 128)
    starts = (0, 3072, 3840, 6144)
    widths = (3072, 768, 2304, 768)
    layers = (1, 0)

    def exchanges(l):
        lhs_in, rhs_in = ins[5 * l], ins[5 * l + 1 : 5 * l + 5]
        away = [
            remote(
                lhs_in.at[1 - c],
                lhs.at[l, ALL, half],
                csend.at[l, 0],
                crecv.at[l, 0],
                partner,
            )
        ]
        here = [pltpu.make_async_copy(lhs_in.at[c], lhs.at[l, ALL, half], lsem.at[l, 0])]
        for j in range(4):
            dst = rhs.at[l, half, pl.ds(starts[j], widths[j])]
            away.append(remote(rhs_in[j], dst, csend.at[l, j + 1], crecv.at[l, j + 1], partner))
            here.append(pltpu.make_async_copy(rhs_in[j], dst, lsem.at[l, j + 1]))
        return away, here

    exchanged = {}
    for l in layers:
        exchanged[l] = exchanges(l)
        for copy in exchanged[l][0] + exchanged[l][1]:
            copy.start()

    vec_axes = ("c", "x", "y", "z")
    vec_sends = []

    def vec_slot(phase, place):
        if phase == 0:
            return vc.at[place["c"]]
        return va.at[phase - 1, place[vec_axes[phase]]]

    def vec_start(phase, value):
        vec_slot(phase, me)[...] = value.astype(jnp.bfloat16)
        for s in range(1, 2 if phase == 0 else 4):
            copy = remote(
                vec_slot(phase, me),
                vec_slot(phase, me),
                vs.at[phase, s - 1],
                vr.at[phase, s - 1],
                peer_of(me, vec_axes[phase], s),
            )
            copy.start()
            vec_sends.append(copy)

    def vec_finish(phase):
        count = 2 if phase == 0 else 4
        for s in range(1, count):
            src = peer_of(me, vec_axes[phase], count - s)
            slot = vec_slot(phase, src)
            remote(slot, slot, vs.at[phase, s - 1], vr.at[phase, s - 1], src).wait_recv()
        total = None
        for j in range(count):
            part = (vc[j] if phase == 0 else va[phase - 1, j]).astype(jnp.float32)
            total = part if total is None else total + part
        return total

    vec_start(0, vec_in[...])

    sends = []

    def send_chunks(phase, t, l, source, target):
        axis = THIRDS[t][phase] if phase < 3 else "x"
        for s in (2, 1, 3):
            peer = peer_of(me, axis, s)
            copy = remote(
                source(peer[axis]),
                target(s),
                ps.at[phase, t, l, s - 1],
                pr.at[phase, t, l, s - 1],
                peer,
            )
            copy.start()
            sends.append(copy)

    def await_chunks(phase, t, l, target):
        axis = THIRDS[t][phase] if phase < 3 else "x"
        for s in (1, 3, 2):
            slot = target(s)
            remote(
                slot,
                slot,
                ps.at[phase, t, l, s - 1],
                pr.at[phase, t, l, s - 1],
                peer_of(me, axis, s),
            ).wait_recv()

    dims = (((0,), (0,)), ((), ()))
    for l in layers:
        away, here = exchanged[l]
        for copy in here:
            copy.wait()
        for copy in away:
            copy.wait_recv()
        for t in range(3):
            for q in range(4):
                unit = (0, 1 + q, 5 if q < 3 else 6)[t]
                col = (q * 768, 3072, 3840 + q * 768)[t]
                block = jnp.dot(
                    lhs[l, 384 * unit : 384 * unit + 384, :],
                    rhs[l, :, col : col + 768],
                    preferred_element_type=jnp.float32,
                )
                for i in range(16):
                    z, y = i // 4, (i % 2) * 2 + (i // 2) % 2
                    at = ((q, y, z), (y, z, q), (z, q, y))[t]
                    g[t, l, at[0], at[1], at[2]] = block[24 * i : 24 * i + 24].astype(jnp.bfloat16)
            send_chunks(
                0, t, l, lambda a, t=t, l=l: g.at[t, l, a], lambda s, t=t, l=l: r1.at[t, l, s - 1]
            )
    vec_start(1, vec_finish(0))
    f32 = jnp.float32
    for l in layers:
        for t in range(3):
            mine = me[THIRDS[t][0]]
            await_chunks(0, t, l, lambda s, t=t, l=l: r1.at[t, l, s - 1])

            def add1(i, carry, t=t, l=l, mine=mine):
                a, b = i // 4, i % 4
                total = g[t, l, mine, a, b].astype(f32)
                for s in range(3):
                    total = total + r1[t, l, s, a, b].astype(f32)
                s1[t, l, a, b] = total.astype(jnp.bfloat16)
                return carry

            lax.fori_loop(0, 16, add1, 0)
            send_chunks(
                1, t, l, lambda a, t=t, l=l: s1.at[t, l, a], lambda s, t=t, l=l: r2.at[t, l, s - 1]
            )
    vec_start(2, vec_finish(1))
    for l in layers:
        for t in range(3):
            mine = me[THIRDS[t][1]]
            await_chunks(1, t, l, lambda s, t=t, l=l: r2.at[t, l, s - 1])
            for a in range(4):
                total = s1[t, l, mine, a].astype(f32)
                for s in range(3):
                    total = total + r2[t, l, s, a].astype(f32)
                s2[t, l, a] = total.astype(jnp.bfloat16)
            send_chunks(
                2, t, l, lambda a, t=t, l=l: s2.at[t, l, a], lambda s, t=t, l=l: r3.at[t, l, s - 1]
            )
    vec_start(3, vec_finish(2))
    for l in layers:
        for t in range(3):
            mine = me[THIRDS[t][2]]
            await_chunks(2, t, l, lambda s, t=t, l=l: r3.at[t, l, s - 1])
            total = s2[t, l, mine].astype(f32)
            for s in range(3):
                total = total + r3[t, l, s].astype(f32)
            last[t, l, me["x"]] = total.astype(jnp.bfloat16)
            send_chunks(
                3,
                t,
                l,
                lambda a, t=t, l=l: last.at[t, l, me["x"]],
                lambda s, t=t, l=l: last.at[t, l, me["x"]],
            )
    vec_out[...] = vec_finish(3)
    for l in layers:
        for t in range(3):
            await_chunks(3, t, l, lambda s, t=t, l=l: last.at[t, l, (me["x"] + 4 - s) % 4])
            for q in range(4):
                part = last[t, l, q].astype(f32)
                if t == 0:
                    up_out[l, :, 768 * q : 768 * q + 768] = part
                elif t == 1:
                    down_out[l, 24 * q : 24 * q + 24, :] = part
                elif q < 3:
                    joint_out[l, :, 768 * q : 768 * q + 768] = part
                else:
                    out_out[l] = part
    for copy in sends + vec_sends + [a for l in layers for a in exchanged[l][0]]:
        copy.wait_send()


def for_owner_cores(array):
    tokens, width = array.shape
    n = width // 768
    t = array.T.reshape(16, 2, n, 24, tokens).transpose(1, 2, 0, 3, 4)
    return t.reshape(2, n * 384, tokens)


def reduce_grads(per_layer, vectors):
    operands = []
    for hidden, mixed, first, acts, d_joint, d_branch, d_up, d_down in per_layer:
        operands.append(
            jnp.concatenate([for_owner_cores(a) for a in (first, acts, hidden, mixed)], axis=1)
        )
        operands += [d_up, d_down, d_joint, d_branch]
    anyspace = pl.BlockSpec(memory_space=pl.ANY)
    vmem = pl.BlockSpec(memory_space=pltpu.VMEM)
    bf, dma = jnp.bfloat16, pltpu.SemaphoreType.DMA
    return pl.pallas_call(
        reduce_kernel,
        out_shape=[
            jax.ShapeDtypeStruct((2, 24, 2304), jnp.float32),
            jax.ShapeDtypeStruct((2, 24, 768), jnp.float32),
            jax.ShapeDtypeStruct((2, 24, 3072), jnp.float32),
            jax.ShapeDtypeStruct((2, 96, 768), jnp.float32),
            jax.ShapeDtypeStruct((32, 768), jnp.float32),
        ],
        in_specs=[anyspace] * 10 + [vmem],
        out_specs=[vmem] * 5,
        scratch_shapes=[
            pltpu.VMEM((2, 2688, 256), bf),
            pltpu.VMEM((2, 256, 6912), bf),
            pltpu.VMEM((3, 2, 4, 4, 4, 24, 768), bf),
            pltpu.VMEM((3, 2, 3, 4, 4, 24, 768), bf),
            pltpu.VMEM((3, 2, 4, 4, 24, 768), bf),
            pltpu.VMEM((3, 2, 3, 4, 24, 768), bf),
            pltpu.VMEM((3, 2, 4, 24, 768), bf),
            pltpu.VMEM((3, 2, 3, 24, 768), bf),
            pltpu.VMEM((3, 2, 4, 24, 768), bf),
            pltpu.VMEM((2, 32, 768), bf),
            pltpu.VMEM((3, 4, 32, 768), bf),
            dma((2, 5)),
            dma((2, 5)),
            dma((2, 5)),
            dma((4, 3, 2, 3)),
            dma((4, 3, 2, 3)),
            dma((4, 3)),
            dma((4, 3)),
        ],
        compiler_params=pltpu.CompilerParams(
            collective_id=1, has_side_effects=True, vmem_limit_bytes=62 * 1024 * 1024
        ),
        name="reduce_grads",
    )(*operands, vectors)


def column_sums(values):
    return jnp.sum(values.astype(jnp.float32), axis=tuple(range(values.ndim - 1)))


def body(
    inputs,
    lengths,
    joint_weight,
    query_bias,
    value_bias,
    output_weight,
    output_bias,
    first_gain,
    first_shift,
    up_weight,
    up_bias,
    down_weight,
    down_bias,
    second_gain,
    second_shift,
    cotangent,
):
    vectors = jnp.stack(
        (
            query_bias,
            value_bias,
            output_bias,
            first_gain,
            first_shift,
            down_bias,
            second_gain,
            second_shift,
        ),
        axis=1,
    )
    vectors = jnp.concatenate([vectors, up_bias.reshape(LAYERS, 4, 24)], axis=1)
    vectors = jnp.pad(vectors.reshape(24, 24), ((0, 8), (0, 104)))
    joint_and_out = jnp.concatenate([joint_weight, output_weight], axis=-1)
    pieces = []
    for layer_index in range(LAYERS):
        pieces += [up_weight[layer_index], down_weight[layer_index], joint_and_out[layer_index]]
    *gathered, vectors_all = gather_weights((*pieces, vectors))
    vectors_all = vectors_all.reshape(32, 32, 128)[:, :24, :24].reshape(32, LAYERS, 12, 24)
    rows_all = vectors_all[:, :, :8].transpose(1, 2, 0, 3).reshape(LAYERS, 8, 768)
    up_adds = vectors_all[:, :, 8:].transpose(1, 0, 2, 3).reshape(LAYERS, 3072)
    weights_of = []
    for layer_index in range(LAYERS):
        up_full, down_full, joint_out = gathered[3 * layer_index : 3 * layer_index + 3]
        up_full = up_full.reshape(768, 3072)
        down_full = down_full.reshape(3072, 768)
        joint_out = joint_out.reshape(768, 3072)
        rows = rows_all[layer_index]
        weights_of.append(
            (
                joint_out[:, :2304],
                rows[0],
                rows[1],
                joint_out[:, 2304:],
                rows[2],
                rows[3],
                rows[4],
                up_full,
                up_adds[layer_index],
                down_full,
                rows[5],
                rows[6],
                rows[7],
            )
        )
    seq_count, tok_count, width = inputs.shape
    row_count = seq_count * tok_count
    head_devices = lax.axis_size("head")
    blk_devices = lax.axis_size("blk")
    group_heads = HEADS // head_devices
    score_scale = HD ** (-0.5)
    block_rows = head_devices * tok_count
    places = jnp.arange(blk_devices * block_rows, dtype=jnp.int32)
    block_index = places // block_rows
    within = places % block_rows
    key_places = (within // tok_count * blk_devices + block_index) * tok_count + within % tok_count

    def masked_scores(query, key_rows, length):
        query_heads = query.reshape(query.shape[0], group_heads, HD)
        key_heads = key_rows.reshape(key_rows.shape[0], group_heads, HD)
        raw_scores = jnp.einsum(
            "qhe,khe->hqk", query_heads, key_heads, preferred_element_type=jnp.float32
        )
        key_valid = key_places < length
        return jnp.where(key_valid[None, None, :], raw_scores * score_scale, MASKED)

    def attend_forward(sequence_items):
        query, key_rows, value_rows, length = sequence_items
        scores = masked_scores(query, key_rows, length)
        row_peak = jnp.max(scores, axis=-1, keepdims=True)
        shifted = jnp.exp(scores - row_peak)
        row_total = jnp.sum(shifted, axis=-1, keepdims=True)
        probabilities = (shifted / row_total).astype(jnp.bfloat16)
        value_heads = value_rows.reshape(value_rows.shape[0], group_heads, HD)
        mixed_heads = jnp.einsum(
            "hqk,khe->qhe", probabilities, value_heads, preferred_element_type=jnp.float32
        )
        log_total = row_peak[..., 0] + jnp.log(row_total[..., 0])
        return (mixed_heads.reshape(query.shape[0], -1).astype(jnp.bfloat16), log_total)

    def attend_backward(sequence_items):
        query, key_rows, value_rows, length, log_total, grad_mixed = sequence_items
        scores = masked_scores(query, key_rows, length)
        probabilities = jnp.exp(scores - log_total[..., None])
        query_heads = query.reshape(query.shape[0], group_heads, HD)
        key_heads = key_rows.reshape(key_rows.shape[0], group_heads, HD)
        value_heads = value_rows.reshape(value_rows.shape[0], group_heads, HD)
        grad_heads = grad_mixed.reshape(grad_mixed.shape[0], group_heads, HD)
        grad_probs = jnp.einsum(
            "qhe,khe->hqk", grad_heads, value_heads, preferred_element_type=jnp.float32
        )
        row_inner = jnp.sum(probabilities * grad_probs, axis=-1, keepdims=True)
        grad_scores = (probabilities * (grad_probs - row_inner) * score_scale).astype(jnp.bfloat16)
        grad_query = jnp.einsum(
            "hqk,khe->qhe", grad_scores, key_heads, preferred_element_type=jnp.float32
        )
        key_term = jnp.einsum(
            "hqk,qhe->khe", grad_scores, query_heads, preferred_element_type=jnp.float32
        )
        value_term = jnp.einsum(
            "hqk,qhe->khe",
            probabilities.astype(jnp.bfloat16),
            grad_heads,
            preferred_element_type=jnp.float32,
        )
        key_total = key_rows.shape[0]
        pair_term = jnp.concatenate(
            [key_term.reshape(key_total, -1), value_term.reshape(key_total, -1)], axis=-1
        )
        return (grad_query.reshape(query.shape[0], -1).astype(jnp.bfloat16), pair_term)

    hidden = inputs.reshape(row_count, width)
    kept = []
    outputs = []
    for layer_index in range(LAYERS):
        weights = weights_of[layer_index]
        (
            joint_full,
            query_add,
            value_add,
            out_full,
            out_add,
            gain_first,
            shift_first,
            up_full,
            up_add,
            down_full,
            down_add,
            gain_second,
            shift_second,
        ) = weights
        projected = row_product(hidden, joint_full)
        query = (
            (projected[:, :width] + query_add)
            .astype(jnp.bfloat16)
            .reshape(seq_count, tok_count, width)
        )
        key_rows = (
            projected[:, width : 2 * width]
            .astype(jnp.bfloat16)
            .reshape(seq_count, tok_count, width)
        )
        value_rows = (
            (projected[:, 2 * width :] + value_add)
            .astype(jnp.bfloat16)
            .reshape(seq_count, tok_count, width)
        )
        query_group, key_group, value_group = sent_together(
            (query, key_rows, value_rows), "head", 2, 1, 0
        )
        key_all, value_all = sent_together_2((key_group, value_group), "blk", 1, 0)
        mixed_group, log_total = lax.map(attend_forward, (query_group, key_all, value_all, lengths))
        mixed_rows = lax.all_to_all(
            mixed_group, "head", split_axis=1, concat_axis=2, tiled=True
        ).reshape(row_count, width)
        branch = row_product(mixed_rows, out_full) + out_add
        before_first = hidden.astype(jnp.float32) + branch
        first_norm = layer_norm(before_first, gain_first, shift_first)
        first_low = first_norm.astype(jnp.bfloat16)
        upward = row_product(first_low, up_full) + up_add
        activated = exact_gelu(upward).astype(jnp.bfloat16)
        before_second = first_norm + (row_product(activated, down_full) + down_add)
        result = layer_norm(before_second, gain_second, shift_second)
        result_low = result.astype(jnp.bfloat16)
        outputs.append(result_low.reshape(seq_count, tok_count, width))
        kept.append(
            (
                hidden,
                query_group,
                key_all,
                value_all,
                log_total,
                mixed_rows,
                before_first,
                first_low,
                upward,
                activated,
                before_second,
            )
        )
        hidden = result_low
    grad_rows = cotangent.reshape(row_count, width).astype(jnp.float32)
    layer_grads = [None] * LAYERS
    vector_grads = [None] * LAYERS
    for layer_index in reversed(range(LAYERS)):
        (
            hidden,
            query_group,
            key_all,
            value_all,
            log_total,
            mixed_rows,
            before_first,
            first_low,
            upward,
            activated,
            before_second,
        ) = kept[layer_index]
        weights = weights_of[layer_index]
        (
            joint_full,
            query_add,
            value_add,
            out_full,
            out_add,
            gain_first,
            shift_first,
            up_full,
            up_add,
            down_full,
            down_add,
            gain_second,
            shift_second,
        ) = weights
        _, second_pull = jax.vjp(
            layer_norm,
            before_second,
            gain_second.astype(jnp.float32),
            shift_second.astype(jnp.float32),
        )
        grad_second, grad_gain_second, grad_shift_second = second_pull(grad_rows)
        grad_down = grad_second.astype(jnp.bfloat16)
        grad_down_add = column_sums(grad_down)
        _, gelu_pull = jax.vjp(exact_gelu, upward)
        grad_up = gelu_pull(times_transposed(grad_down, down_full))[0].astype(jnp.bfloat16)
        grad_up_add = column_sums(grad_up)
        grad_first = grad_second + times_transposed(grad_up, up_full)
        _, first_pull = jax.vjp(
            layer_norm,
            before_first,
            gain_first.astype(jnp.float32),
            shift_first.astype(jnp.float32),
        )
        grad_before, grad_gain_first, grad_shift_first = first_pull(grad_first)
        grad_branch = grad_before.astype(jnp.bfloat16)
        grad_out_add = column_sums(grad_branch)
        grad_mixed = (
            times_transposed(grad_branch, out_full)
            .astype(jnp.bfloat16)
            .reshape(seq_count, tok_count, width)
        )
        grad_group = lax.all_to_all(grad_mixed, "head", split_axis=2, concat_axis=1, tiled=True)
        grad_query_group, pair_terms = lax.map(
            attend_backward, (query_group, key_all, value_all, lengths, log_total, grad_group)
        )
        pair_sums = sum_at_owner(pair_terms.astype(jnp.bfloat16), "blk", 1).astype(jnp.bfloat16)
        group_width = pair_sums.shape[-1] // 2
        grad_query, grad_key, grad_value = sent_together(
            (grad_query_group, pair_sums[..., :group_width], pair_sums[..., group_width:]),
            "head",
            1,
            2,
            0,
        )
        grad_joint_rows = jnp.concatenate([grad_query, grad_key, grad_value], axis=-1).reshape(
            row_count, 3 * width
        )
        grad_query_add = column_sums(grad_query)
        grad_value_add = column_sums(grad_value)
        grad_rows = grad_before + times_transposed(grad_joint_rows, joint_full)
        layer_grads[layer_index] = (
            hidden,
            mixed_rows,
            first_low,
            activated,
            grad_joint_rows,
            grad_branch,
            grad_up,
            grad_down,
        )
        vector_grads[layer_index] = (
            grad_query_add,
            grad_value_add,
            grad_out_add,
            grad_gain_first,
            grad_shift_first,
            grad_down_add,
            grad_gain_second,
            grad_shift_second,
            grad_up_add,
        )
    vectors = jnp.concatenate(
        [a.reshape(-1, 768) for layer in vector_grads for a in layer] + [jnp.zeros((8, 768), jnp.float32)]
    )
    joint_grad, out_grad, up_grad, down_grad, vectors = reduce_grads(layer_grads, vectors)
    vectors = vectors[:24].reshape(LAYERS, 12, 768)
    owner = lax.axis_index("batch") * blk_devices + lax.axis_index("blk")
    own_rows = lax.dynamic_slice_in_dim(vectors[:, :8], owner * 24, 24, axis=2)
    own_up = lax.dynamic_slice_in_dim(vectors[:, 8:].reshape(LAYERS, 3072), owner * 96, 96, axis=1)
    stacked = (
        joint_grad,
        own_rows[:, 0],
        own_rows[:, 1],
        out_grad,
        own_rows[:, 2],
        own_rows[:, 3],
        own_rows[:, 4],
        up_grad,
        own_up,
        down_grad,
        own_rows[:, 5],
        own_rows[:, 6],
        own_rows[:, 7],
    )
    activations = jnp.stack(outputs)
    input_grad = grad_rows.reshape(seq_count, tok_count, width)
    return (
        activations,
        input_grad,
        stacked[0],
        stacked[1],
        stacked[2],
        stacked[3],
        stacked[4],
        stacked[5],
        stacked[6],
        stacked[7],
        stacked[8],
        stacked[9],
        stacked[10],
        stacked[11],
        stacked[12],
    )


def solution(mesh):
    placed = (
        P("batch", ("head", "blk"), None),
        P("batch"),
        P(None, ("batch", "blk"), None),
        P(None, ("batch", "blk")),
        P(None, ("batch", "blk")),
        P(None, ("batch", "blk"), None),
        P(None, ("batch", "blk")),
        P(None, ("batch", "blk")),
        P(None, ("batch", "blk")),
        P(None, ("batch", "blk"), None),
        P(None, ("batch", "blk")),
        P(None, ("batch", "blk"), None),
        P(None, ("batch", "blk")),
        P(None, ("batch", "blk")),
        P(None, ("batch", "blk")),
        P("batch", ("head", "blk"), None),
    )
    return jax.shard_map(
        body,
        mesh=mesh,
        in_specs=placed,
        out_specs=(
            P(None, "batch", ("head", "blk"), None),
            P("batch", ("head", "blk"), None),
            P(None, ("batch", "blk"), None),
            P(None, ("batch", "blk")),
            P(None, ("batch", "blk")),
            P(None, ("batch", "blk"), None),
            P(None, ("batch", "blk")),
            P(None, ("batch", "blk")),
            P(None, ("batch", "blk")),
            P(None, ("batch", "blk"), None),
            P(None, ("batch", "blk")),
            P(None, ("batch", "blk"), None),
            P(None, ("batch", "blk")),
            P(None, ("batch", "blk")),
            P(None, ("batch", "blk")),
        ),
        check_vma=False,
    )
```

```python
import jax
import jax.numpy as jnp
from jax import lax
from jax.experimental import pallas as pl
from jax.experimental.pallas import tpu as pltpu
from jax.sharding import PartitionSpec as P

LAYERS = 2


EPSILON = 1e-12
MASKED = -1e30


MESH = pl.DeviceIdType.MESH
ALL = slice(None)


def my_place():
    b, x, k = lax.axis_index("batch"), lax.axis_index("head"), lax.axis_index("blk")
    return {"z": b // 2, "y": (k // 2) * 2 + b % 2, "x": x, "c": k % 2}


def device_of(place):
    return (
        place["z"] * 2 + place["y"] % 2,
        place["x"],
        (place["y"] // 2) * 2 + place["c"],
    )


def peer_of(place, axis, step):
    other = dict(place)
    other[axis] = (place[axis] + step) % (2 if axis == "c" else 4)
    return other


def greet_all(place):
    barrier = pltpu.get_barrier_semaphore()
    peers = [peer_of(place, a, s) for a in ("x", "y", "z") for s in (1, 2, 3)]
    peers.append(peer_of(place, "c", 1))
    for p in peers:
        pl.semaphore_signal(barrier, inc=1, device_id=device_of(p), device_id_type=MESH)
    pl.semaphore_wait(barrier, len(peers))


def remote(src, dst, send, recv, place):
    return pltpu.make_async_remote_copy(
        src_ref=src,
        dst_ref=dst,
        send_sem=send,
        recv_sem=recv,
        device_id=device_of(place),
        device_id_type=MESH,
    )


PIECES = (
    (0, ("z", "y", "x")),
    (1, ("z", "y")),
    (2, ("y", "z")),
    (3, ("z", "y", "x")),
    (4, ("z", "y")),
    (5, ("y", "z")),
    (6, ("y", "z")),
)


def gather_kernel(*refs):
    n = len(PIECES)
    ins, outs = refs[:n], refs[n : 2 * n]
    send, recv, fsend, frecv, local = refs[2 * n :]
    me = my_place()
    partner = peer_of(me, "c", 1)

    def region(i, phase, place):
        array, order = PIECES[i]
        done = order[:phase]
        z = ALL if "z" in done else place["z"]
        y = (ALL, ALL) if "y" in done else (place["y"] % 2, place["y"] // 2)
        cols = ALL
        if "x" in order and "x" not in done:
            cols = pl.ds(pl.multiple_of(place["x"] * 768, 128), 768)
        return outs[i].at[z, y[0], y[1], place["c"], ALL, cols]

    def own(i):
        if "x" in PIECES[i][1]:
            return ins[i].at[ALL, pl.ds(pl.multiple_of(me["x"] * 768, 128), 768)]
        return ins[i]

    def step(i, phase, s):
        axis = PIECES[i][1][phase]
        src = own(i) if phase == 0 else region(i, phase, me)
        return remote(
            src,
            region(i, phase, me),
            send.at[i, phase, s - 1],
            recv.at[i, phase, s - 1],
            peer_of(me, axis, s),
        )

    def landed(i, phase, s):
        axis = PIECES[i][1][phase]
        place = peer_of(me, axis, 4 - s)
        r = region(i, phase, place)
        return remote(r, r, send.at[i, phase, s - 1], recv.at[i, phase, s - 1], place)

    def forward(i, phase, s):
        axis = PIECES[i][1][phase]
        r = region(i, phase, peer_of(me, axis, 4 - s))
        return remote(r, r, fsend.at[i, phase, s - 1], frecv.at[i, phase, s - 1], partner)

    def forwarded(i, phase, s):
        axis = PIECES[i][1][phase]
        r = region(i, phase, peer_of(partner, axis, 4 - s))
        return remote(r, r, fsend.at[i, phase, s - 1], frecv.at[i, phase, s - 1], partner)

    greet_all(me)
    copies, sends, fwds = [], [], []
    for i in range(n):
        for s in (2, 1, 3):
            c = step(i, 0, s)
            c.start()
            sends.append(c)
        c = pltpu.make_async_copy(own(i), region(i, 0, me), local.at[i])
        c.start()
        copies.append(c)
        c = remote(own(i), region(i, 0, me), fsend.at[i, 3, 0], frecv.at[i, 3, 0], partner)
        c.start()
        fwds.append(c)
    for c in copies:
        c.wait()
    for phase in range(3):
        for i in range(n):
            order = PIECES[i][1]
            if phase >= len(order):
                continue
            for s in (1, 3, 2):
                landed(i, phase, s).wait_recv()
                c = forward(i, phase, s)
                c.start()
                fwds.append(c)
            if phase + 1 < len(order):
                for s in (2, 1, 3):
                    c = step(i, phase + 1, s)
                    c.start()
                    sends.append(c)
    for i in range(n):
        r = region(i, 0, partner)
        remote(r, r, fsend.at[i, 3, 0], frecv.at[i, 3, 0], partner).wait_recv()
        for phase in range(len(PIECES[i][1])):
            for s in (1, 2, 3):
                forwarded(i, phase, s).wait_recv()
    for c in sends + fwds:
        c.wait_send()


def gather_weights(pieces):
    n = len(pieces)
    anyspace = pl.BlockSpec(memory_space=pl.ANY)
    return pl.pallas_call(
        gather_kernel,
        out_shape=[jax.ShapeDtypeStruct((4, 2, 2, 2, *p.shape), p.dtype) for p in pieces],
        in_specs=[anyspace] * n,
        out_specs=[anyspace] * n,
        scratch_shapes=[
            pltpu.SemaphoreType.DMA((n, 3, 3)),
            pltpu.SemaphoreType.DMA((n, 3, 3)),
            pltpu.SemaphoreType.DMA((n, 4, 3)),
            pltpu.SemaphoreType.DMA((n, 4, 3)),
            pltpu.SemaphoreType.DMA((n,)),
        ],
        compiler_params=pltpu.CompilerParams(collective_id=0, has_side_effects=True),
        name="gather_weights",
    )(*pieces)


THIRDS = (("x", "y", "z"), ("y", "z", "x"), ("z", "x", "y"))


def reduce_kernel(*refs):
    ins = refs[:11]
    joint_out, out_out, up_out, down_out, vec_out = refs[11:16]
    lhs, rhs, g, r1, s1, r2, s2, r3, last, vc, va = refs[16:27]
    csend, crecv, lsem, ps, pr, vs, vr = refs[27:]
    vec_in = ins[10]
    me = my_place()
    partner = peer_of(me, "c", 1)
    c = me["c"]
    greet_all(me)
    half = pl.ds(pl.multiple_of(c * 128, 128), 128)
    other_half = pl.ds(pl.multiple_of((1 - c) * 128, 128), 128)
    starts = (0, 3072, 3840, 6144)
    widths = (3072, 768, 2304, 768)
    layers = (1, 0)

    def exchanges(l):
        lhs_in, rhs_in = ins[5 * l], ins[5 * l + 1 : 5 * l + 5]
        away = [
            remote(
                lhs_in.at[1 - c],
                lhs.at[l, ALL, half],
                csend.at[l, 0],
                crecv.at[l, 0],
                partner,
            )
        ]
        here = [pltpu.make_async_copy(lhs_in.at[c], lhs.at[l, ALL, half], lsem.at[l, 0])]
        for j in range(4):
            dst = rhs.at[l, half, pl.ds(starts[j], widths[j])]
            away.append(remote(rhs_in[j], dst, csend.at[l, j + 1], crecv.at[l, j + 1], partner))
            here.append(pltpu.make_async_copy(rhs_in[j], dst, lsem.at[l, j + 1]))
        return away, here

    exchanged = {}
    for l in layers:
        exchanged[l] = exchanges(l)
        for copy in exchanged[l][0] + exchanged[l][1]:
            copy.start()

    vec_axes = ("c", "x", "y", "z")
    vec_sends = []

    def vec_slot(phase, place):
        if phase == 0:
            return vc.at[place["c"]]
        return va.at[phase - 1, place[vec_axes[phase]]]

    def vec_start(phase, value):
        vec_slot(phase, me)[...] = value.astype(jnp.bfloat16)
        for s in range(1, 2 if phase == 0 else 4):
            copy = remote(
                vec_slot(phase, me),
                vec_slot(phase, me),
                vs.at[phase, s - 1],
                vr.at[phase, s - 1],
                peer_of(me, vec_axes[phase], s),
            )
            copy.start()
            vec_sends.append(copy)

    def vec_finish(phase):
        count = 2 if phase == 0 else 4
        for s in range(1, count):
            src = peer_of(me, vec_axes[phase], count - s)
            slot = vec_slot(phase, src)
            remote(slot, slot, vs.at[phase, s - 1], vr.at[phase, s - 1], src).wait_recv()
        total = None
        for j in range(count):
            part = (vc[j] if phase == 0 else va[phase - 1, j]).astype(jnp.float32)
            total = part if total is None else total + part
        return total

    vec_start(0, vec_in[...])

    sends = []

    def send_chunks(phase, t, l, source, target):
        axis = THIRDS[t][phase] if phase < 3 else "x"
        for s in (2, 1, 3):
            peer = peer_of(me, axis, s)
            copy = remote(
                source(peer[axis]),
                target(s),
                ps.at[phase, t, l, s - 1],
                pr.at[phase, t, l, s - 1],
                peer,
            )
            copy.start()
            sends.append(copy)

    def await_chunks(phase, t, l, target):
        axis = THIRDS[t][phase] if phase < 3 else "x"
        for s in (1, 3, 2):
            slot = target(s)
            remote(
                slot,
                slot,
                ps.at[phase, t, l, s - 1],
                pr.at[phase, t, l, s - 1],
                peer_of(me, axis, s),
            ).wait_recv()

    dims = (((0,), (0,)), ((), ()))
    for l in layers:
        away, here = exchanged[l]
        for copy in here:
            copy.wait()
        for copy in away:
            copy.wait_recv()
        for t in range(3):
            for q in range(4):
                unit = (0, 1 + q, 5 if q < 3 else 6)[t]
                col = (q * 768, 3072, 3840 + q * 768)[t]
                block = jnp.dot(
                    lhs[l, 384 * unit : 384 * unit + 384, :],
                    rhs[l, :, col : col + 768],
                    preferred_element_type=jnp.float32,
                )
                for i in range(16):
                    z, y = i // 4, (i % 2) * 2 + (i // 2) % 2
                    at = ((q, y, z), (y, z, q), (z, q, y))[t]
                    g[t, l, at[0], at[1], at[2]] = block[24 * i : 24 * i + 24].astype(jnp.bfloat16)
            send_chunks(
                0, t, l, lambda a, t=t, l=l: g.at[t, l, a], lambda s, t=t, l=l: r1.at[t, l, s - 1]
            )
    vec_start(1, vec_finish(0))
    f32 = jnp.float32
    for l in layers:
        for t in range(3):
            mine = me[THIRDS[t][0]]
            await_chunks(0, t, l, lambda s, t=t, l=l: r1.at[t, l, s - 1])

            def add1(i, carry, t=t, l=l, mine=mine):
                a, b = i // 4, i % 4
                total = g[t, l, mine, a, b].astype(f32)
                for s in range(3):
                    total = total + r1[t, l, s, a, b].astype(f32)
                s1[t, l, a, b] = total.astype(jnp.bfloat16)
                return carry

            lax.fori_loop(0, 16, add1, 0)
            send_chunks(
                1, t, l, lambda a, t=t, l=l: s1.at[t, l, a], lambda s, t=t, l=l: r2.at[t, l, s - 1]
            )
    vec_start(2, vec_finish(1))
    for l in layers:
        for t in range(3):
            mine = me[THIRDS[t][1]]
            await_chunks(1, t, l, lambda s, t=t, l=l: r2.at[t, l, s - 1])
            for a in range(4):
                total = s1[t, l, mine, a].astype(f32)
                for s in range(3):
                    total = total + r2[t, l, s, a].astype(f32)
                s2[t, l, a] = total.astype(jnp.bfloat16)
            send_chunks(
                2, t, l, lambda a, t=t, l=l: s2.at[t, l, a], lambda s, t=t, l=l: r3.at[t, l, s - 1]
            )
    vec_start(3, vec_finish(2))
    for l in layers:
        for t in range(3):
            mine = me[THIRDS[t][2]]
            await_chunks(2, t, l, lambda s, t=t, l=l: r3.at[t, l, s - 1])
            total = s2[t, l, mine].astype(f32)
            for s in range(3):
                total = total + r3[t, l, s].astype(f32)
            last[t, l, me["x"]] = total.astype(jnp.bfloat16)
            send_chunks(
                3,
                t,
                l,
                lambda a, t=t, l=l: last.at[t, l, me["x"]],
                lambda s, t=t, l=l: last.at[t, l, me["x"]],
            )
    vec_out[...] = vec_finish(3)
    for l in layers:
        for t in range(3):
            await_chunks(3, t, l, lambda s, t=t, l=l: last.at[t, l, (me["x"] + 4 - s) % 4])
            for q in range(4):
                part = last[t, l, q].astype(f32)
                if t == 0:
                    up_out[l, :, 768 * q : 768 * q + 768] = part
                elif t == 1:
                    down_out[l, 24 * q : 24 * q + 24, :] = part
                elif q < 3:
                    joint_out[l, :, 768 * q : 768 * q + 768] = part
                else:
                    out_out[l] = part
    for copy in sends + vec_sends + [a for l in layers for a in exchanged[l][0]]:
        copy.wait_send()


def for_owner_cores(array):
    tokens, width = array.shape
    n = width // 768
    t = array.T.reshape(16, 2, n, 24, tokens).transpose(1, 2, 0, 3, 4)
    return t.reshape(2, n * 384, tokens)


def reduce_grads(per_layer, vectors):
    operands = []
    for hidden, mixed, first, acts, d_joint, d_branch, d_up, d_down in per_layer:
        operands.append(
            jnp.concatenate([for_owner_cores(a) for a in (first, acts, hidden, mixed)], axis=1)
        )
        operands += [d_up, d_down, d_joint, d_branch]
    anyspace = pl.BlockSpec(memory_space=pl.ANY)
    vmem = pl.BlockSpec(memory_space=pltpu.VMEM)
    bf, dma = jnp.bfloat16, pltpu.SemaphoreType.DMA
    return pl.pallas_call(
        reduce_kernel,
        out_shape=[
            jax.ShapeDtypeStruct((2, 24, 2304), jnp.float32),
            jax.ShapeDtypeStruct((2, 24, 768), jnp.float32),
            jax.ShapeDtypeStruct((2, 24, 3072), jnp.float32),
            jax.ShapeDtypeStruct((2, 96, 768), jnp.float32),
            jax.ShapeDtypeStruct((32, 768), jnp.float32),
        ],
        in_specs=[anyspace] * 10 + [vmem],
        out_specs=[vmem] * 5,
        scratch_shapes=[
            pltpu.VMEM((2, 2688, 256), bf),
            pltpu.VMEM((2, 256, 6912), bf),
            pltpu.VMEM((3, 2, 4, 4, 4, 24, 768), bf),
            pltpu.VMEM((3, 2, 3, 4, 4, 24, 768), bf),
            pltpu.VMEM((3, 2, 4, 4, 24, 768), bf),
            pltpu.VMEM((3, 2, 3, 4, 24, 768), bf),
            pltpu.VMEM((3, 2, 4, 24, 768), bf),
            pltpu.VMEM((3, 2, 3, 24, 768), bf),
            pltpu.VMEM((3, 2, 4, 24, 768), bf),
            pltpu.VMEM((2, 32, 768), bf),
            pltpu.VMEM((3, 4, 32, 768), bf),
            dma((2, 5)),
            dma((2, 5)),
            dma((2, 5)),
            dma((4, 3, 2, 3)),
            dma((4, 3, 2, 3)),
            dma((4, 3)),
            dma((4, 3)),
        ],
        compiler_params=pltpu.CompilerParams(
            collective_id=1, has_side_effects=True, vmem_limit_bytes=62 * 1024 * 1024
        ),
        name="reduce_grads",
    )(*operands, vectors)


FAR = (((1,), (1,)), ((), ()))
NEAR = (((0,), (0,)), ((), ()))
F32 = jnp.float32
BF = jnp.bfloat16
KEYS = 128


def mxu(a, b, dims=None):
    if dims is None:
        return jnp.dot(a, b, preferred_element_type=F32)
    return lax.dot_general(a, b, dims, preferred_element_type=F32)


def normalized(values):
    average = jnp.mean(values, axis=-1, keepdims=True)
    centered = values - average
    variance = jnp.mean(centered * centered, axis=-1, keepdims=True)
    r = lax.rsqrt(variance + EPSILON)
    return centered * r, r


def norm_backward(values, gain, grad):
    xhat, r = normalized(values)
    g = grad * gain
    back = r * (
        g - jnp.mean(g, axis=-1, keepdims=True) - xhat * jnp.mean(g * xhat, axis=-1, keepdims=True)
    )
    gain_grad = jnp.sum(grad * xhat, axis=0, keepdims=True)
    return back, gain_grad, jnp.sum(grad, axis=0, keepdims=True)


def normal_cdf(u):
    return 0.5 * (1.0 + lax.erf(u * 0.7071067811865476))


def greet_sequence(me):
    barrier = pltpu.get_barrier_semaphore()
    peers = [peer_of(me, "x", s) for s in (1, 2, 3)]
    peers += [peer_of(me, "c", 1), peer_of(me, "y", 2)]
    for p in peers:
        pl.semaphore_signal(barrier, inc=1, device_id=device_of(p), device_id_type=MESH)
    pl.semaphore_wait(barrier, len(peers))


def key_bias(length, block, xs):
    limit = length - xs * 512 - block * 128
    rows = lax.broadcasted_iota(jnp.int32, (KEYS, 128), 0)
    return jnp.where(rows < limit, 0.0, MASKED)


def forward_kernel(*refs):
    hid, rows, up_add, lens, wj, wu, wd = refs[:7]
    res, q_out, kv_out, log_out, att_out, mixed_out = refs[7:13]
    before1_out, low_out, up_out, act_out, before2_out = refs[13:18]
    vj, vu, vd, qs, qb, kvb, sc, acc, back, ab = refs[18:28]
    wsem, osem, qsend, qrecv, xsend, xrecv, csend, crecv, ysend, yrecv, fsend, frecv = refs[28:40]
    bsend, brecv = refs[40:]
    me = my_place()
    x, c = me["x"], me["c"]
    yh = me["y"] // 2
    k = yh * 2 + c
    partner, across = peer_of(me, "c", 1), peer_of(me, "y", 2)
    k_partner = yh * 2 + 1 - c
    k_across = (1 - yh) * 2 + c
    k_diag = (1 - yh) * 2 + 1 - c
    loads = [
        pltpu.make_async_copy(a, b, wsem.at[i])
        for i, (a, b) in enumerate(((wj, vj), (wu, vu), (wd, vd)))
    ]
    for copy in loads:
        copy.start()
    greet_sequence(me)
    sends = []

    def send(src, dst, s, r, place):
        copy = remote(src, dst, s, r, place)
        copy.start()
        sends.append(copy)

    def arrived(slot, s, r, place):
        remote(slot, slot, s, r, place).wait_recv()

    loads[0].wait()
    for j in (1, 2, 0):
        p = mxu(hid[...], vj[:, 768 * j : 768 * j + 768])
        if j == 0:
            p = p + rows[0:1]
        if j == 2:
            p = p + rows[1:2]
        p = p.astype(BF).astype(F32)
        if j == 0:
            p = p * 0.125
        p = p.T.astype(BF)
        for g in range(4):
            qs[g, 192 * j : 192 * j + 192] = p[192 * g : 192 * g + 192]
        if j == 2:
            kvb[k, x] = qs[x, 192:576]
            for s in (2, 1, 3):
                peer = peer_of(me, "x", s)
                send(
                    qs.at[peer["x"], 192:576], kvb.at[k, x], xsend.at[s - 1], xrecv.at[s - 1], peer
                )
            send(kvb.at[k, x], kvb.at[k, x], ysend.at[0], yrecv.at[0], across)
            send(kvb.at[k, x], kvb.at[k, x], csend.at[0], crecv.at[0], partner)
    qb[x] = qs[x, 0:192]
    for s in (2, 1, 3):
        peer = peer_of(me, "x", s)
        send(qs.at[peer["x"], 0:192], qb.at[x], qsend.at[s - 1], qrecv.at[s - 1], peer)
    for s in (1, 3, 2):
        source = peer_of(me, "x", 4 - s)
        slot = kvb.at[k, source["x"]]
        arrived(slot, xsend.at[s - 1], xrecv.at[s - 1], source)
        send(slot, slot, ysend.at[s], yrecv.at[s], across)
        send(slot, slot, csend.at[s], crecv.at[s], partner)
    for s in (1, 3, 2):
        source = peer_of(me, "x", 4 - s)
        arrived(qb.at[source["x"]], qsend.at[s - 1], qrecv.at[s - 1], source)
    for s in (0, 1, 3, 2):
        arrived(kvb.at[k_partner, (x + 4 - s) % 4], csend.at[s], crecv.at[s], partner)

    length = lens[0]
    queries = [
        jnp.concatenate([qb[xs, 64 * n : 64 * n + 64] for xs in range(4)], axis=1)
        for n in range(3)
    ]

    def half(b0, b1, old):
        def scores(i, peaks):
            b = b0 + (b1 - b0) * (i // 4)
            xs = i % 4
            bias = key_bias(length, b, xs)
            bias = jnp.concatenate([bias] * 4, axis=1)
            new = []
            for n in range(3):
                keys = kvb[b, xs, 64 * n : 64 * n + 64, :]
                st = mxu(keys, queries[n], NEAR) + bias
                sc[n, pl.ds(pl.multiple_of(i * KEYS, KEYS), KEYS), :] = st
                new.append(jnp.maximum(peaks[n], jnp.max(st.reshape(16, 8, 512), axis=0)))
            return tuple(new)

        start = tuple(jnp.full((8, 512), MASKED, F32) for _ in range(3))
        peaks = lax.fori_loop(0, 8, scores, start)
        peaks = [jnp.max(p, axis=0, keepdims=True) for p in peaks]
        if old is not None:
            peaks = [jnp.maximum(p, o[0]) for p, o in zip(peaks, old)]
        totals = []
        for n in range(3):
            if old is None:
                acc[n] = jnp.zeros((64, 512), F32)
                totals.append(jnp.zeros((8, 512), F32))
            else:
                shrink = jnp.exp(old[n][0] - peaks[n])
                acc[n] = acc[n] * shrink
                totals.append(old[n][1] * shrink)

        def mix(i, sums):
            b = b0 + (b1 - b0) * (i // 2)
            xs = (i % 2) * 2
            new = []
            for n in range(3):
                at = pl.ds(pl.multiple_of(i * 256, 256), 256)
                p = jnp.exp(sc[n, at, :] - peaks[n])
                new.append(sums[n] + jnp.sum(p.reshape(32, 8, 512), axis=0))
                v = slice(192 + 64 * n, 256 + 64 * n)
                values = jnp.concatenate([kvb[b, xs, v, :], kvb[b, xs + 1, v, :]], axis=1)
                acc[n] += mxu(values, p.astype(BF))
            return tuple(new)

        totals = lax.fori_loop(0, 4, mix, tuple(totals))
        return list(zip(peaks, totals))

    state = half(k, k_partner, None)
    for s in (0, 1, 3, 2):
        slot = kvb.at[k_across, (x + 4 - s) % 4]
        arrived(slot, ysend.at[s], yrecv.at[s], across)
        send(slot, slot, fsend.at[s], frecv.at[s], partner)
    for s in (0, 1, 3, 2):
        arrived(kvb.at[k_diag, (x + 4 - s) % 4], fsend.at[s], frecv.at[s], partner)
    keep = pltpu.make_async_copy(kvb, kv_out, osem)
    keep.start()
    state = half(k_across, k_diag, state)
    log_out[...] = jnp.zeros_like(log_out)
    for n in range(3):
        total = jnp.sum(state[n][1], axis=0, keepdims=True)
        mixed = acc[n] / total
        att_out[64 * n : 64 * n + 64, :] = mixed
        log_out[n : n + 1, :] = state[n][0] + jnp.log(total)
        for xs in range(4):
            back[xs, 64 * n : 64 * n + 64, :] = mixed[:, 128 * xs : 128 * xs + 128].astype(BF)
    ab[x] = back[x]
    for s in (2, 1, 3):
        peer = peer_of(me, "x", s)
        send(back.at[peer["x"]], ab.at[x], bsend.at[s - 1], brecv.at[s - 1], peer)
    q_out[...] = qb[...]
    loads[1].wait()
    loads[2].wait()
    for s in (1, 3, 2):
        source = peer_of(me, "x", 4 - s)
        arrived(ab.at[source["x"]], bsend.at[s - 1], brecv.at[s - 1], source)
    mixed = ab[...].reshape(768, 128).astype(F32).T.astype(BF)
    mixed_out[...] = mixed
    before = hid[...].astype(F32) + (mxu(mixed, vj[:, 2304:3072]) + rows[2:3])
    before1_out[...] = before
    first = normalized(before)[0] * rows[3:4] + rows[4:5]
    low = first.astype(BF)
    low_out[...] = low
    second = first + rows[5:6]
    for q in range(4):
        at = slice(768 * q, 768 * q + 768)
        u = mxu(low, vu[:, at]) + up_add[:, at]
        up_out[:, at] = u
        a = (u * normal_cdf(u)).astype(BF)
        act_out[:, at] = a
        second = second + mxu(a, vd[at, :])
    before2_out[...] = second
    res[...] = (normalized(second)[0] * rows[6:7] + rows[7:8]).astype(BF)
    keep.wait()
    for copy in sends:
        copy.wait_send()


def forward_layer(hidden, rows, up_add, lengths, wj, wu, wd):
    vmem = pl.BlockSpec(memory_space=pltpu.VMEM)
    anyspace = pl.BlockSpec(memory_space=pl.ANY)
    dma = pltpu.SemaphoreType.DMA
    out = jax.ShapeDtypeStruct
    return pl.pallas_call(
        forward_kernel,
        out_shape=[
            out((128, 768), BF),
            out((4, 192, 128), BF),
            out((4, 4, 384, 128), BF),
            out((8, 512), F32),
            out((192, 512), F32),
            out((128, 768), BF),
            out((128, 768), F32),
            out((128, 768), BF),
            out((128, 3072), F32),
            out((128, 3072), BF),
            out((128, 768), F32),
        ],
        in_specs=[vmem, vmem, vmem, pl.BlockSpec(memory_space=pltpu.SMEM)] + [anyspace] * 3,
        out_specs=[vmem, vmem, anyspace] + [vmem] * 8,
        scratch_shapes=[
            pltpu.VMEM((768, 3072), BF),
            pltpu.VMEM((768, 3072), BF),
            pltpu.VMEM((3072, 768), BF),
            pltpu.VMEM((4, 576, 128), BF),
            pltpu.VMEM((4, 192, 128), BF),
            pltpu.VMEM((4, 4, 384, 128), BF),
            pltpu.VMEM((3, 1024, 512), F32),
            pltpu.VMEM((3, 64, 512), F32),
            pltpu.VMEM((4, 192, 128), BF),
            pltpu.VMEM((4, 192, 128), BF),
            dma((3,)),
            dma,
            dma((3,)),
            dma((3,)),
            dma((3,)),
            dma((3,)),
            dma((4,)),
            dma((4,)),
            dma((4,)),
            dma((4,)),
            dma((4,)),
            dma((4,)),
            dma((3,)),
            dma((3,)),
        ],
        compiler_params=pltpu.CompilerParams(
            collective_id=2, has_side_effects=True, vmem_limit_bytes=60 * 1024 * 1024
        ),
        name="forward_layer",
    )(hidden, rows, up_add, lengths, wj, wu, wd)


def backward_kernel(*refs):
    dy, rows, up, before2, before1, qb, kvb, logs, att, lens, wj, wu, wd = refs[:13]
    dh_out, dj_out, db_out, du_out, df_out, vec_out = refs[13:19]
    vj, vu, vd, das, dab, dkv, rx, ry, rl, py, dq, sb, dj = refs[19:32]
    wsem, asend, arecv, csend, crecv, jsend, jrecv = refs[32:]
    me = my_place()
    x, c = me["x"], me["c"]
    yh = me["y"] // 2
    partner, across = peer_of(me, "c", 1), peer_of(me, "y", 2)
    loads = [
        pltpu.make_async_copy(a, b, wsem.at[i])
        for i, (a, b) in enumerate(((wd, vd), (wu, vu), (wj, vj)))
    ]
    for copy in loads:
        copy.start()
    greet_sequence(me)
    sends = []

    def send(src, dst, s, r, place):
        copy = remote(src, dst, s, r, place)
        copy.start()
        sends.append(copy)

    def arrived(slot, s, r, place):
        remote(slot, slot, s, r, place).wait_recv()

    def column_sum(a):
        return jnp.sum(a.astype(F32), axis=0, keepdims=True)

    vec_out[...] = jnp.zeros_like(vec_out)
    d_second, gain_grad, shift_grad = norm_backward(before2[...], rows[6:7], dy[...])
    vec_out[6:7] = gain_grad
    vec_out[7:8] = shift_grad
    df = d_second.astype(BF)
    df_out[...] = df
    vec_out[5:6] = column_sum(df)
    loads[0].wait()
    loads[1].wait()
    d_first = d_second
    for q in range(4):
        at = slice(768 * q, 768 * q + 768)
        u = up[:, at]
        slope = normal_cdf(u) + u * (0.3989422804014327 * jnp.exp(-0.5 * u * u))
        du = (mxu(df, vd[at, :], FAR) * slope).astype(BF)
        du_out[:, at] = du
        vec_out[8 + q : 9 + q] = column_sum(du)
        d_first = d_first + mxu(du, vu[:, at], FAR)
    d_sum, gain_grad, shift_grad = norm_backward(before1[...], rows[3:4], d_first)
    vec_out[3:4] = gain_grad
    vec_out[4:5] = shift_grad
    db = d_sum.astype(BF)
    db_out[...] = db
    vec_out[2:3] = column_sum(db)
    dh_out[...] = d_sum
    loads[2].wait()
    da = mxu(db, vj[:, 2304:3072], FAR).T.astype(BF)
    for g in range(4):
        das[g] = da[192 * g : 192 * g + 192]
    dab[x] = das[x]
    for s in (2, 1, 3):
        peer = peer_of(me, "x", s)
        send(das.at[peer["x"]], dab.at[x], asend.at[s - 1], arecv.at[s - 1], peer)
    for s in (1, 3, 2):
        source = peer_of(me, "x", 4 - s)
        arrived(dab.at[source["x"]], asend.at[s - 1], arecv.at[s - 1], source)
    length = lens[0]

    def by_head(ref, n):
        return jnp.concatenate([ref[xs, 64 * n : 64 * n + 64] for xs in range(4)], axis=1)

    inner = []
    for n in range(3):
        dq[n] = jnp.zeros((64, 512), F32)
        inner.append(
            jnp.sum(
                by_head(dab, n).astype(F32) * att[64 * n : 64 * n + 64, :], axis=0, keepdims=True
            )
        )

    def half(which, base):
        def step(i, carry):
            core, xs = i // 4, i % 4
            b = base + core
            bias = key_bias(length, b, xs)
            bias = jnp.concatenate([bias] * 2, axis=1)
            for n in range(3):
                own = slice(64 * n, 64 * n + 64)
                keys = kvb[b, xs, own, :]
                values = kvb[b, xs, slice(192 + 64 * n, 256 + 64 * n), :]
                dk = dv = None
                for h in range(2):
                    at = slice(256 * h, 256 * h + 256)
                    q_n = jnp.concatenate([qb[2 * h, own], qb[2 * h + 1, own]], axis=1)
                    da_n = jnp.concatenate([dab[2 * h, own], dab[2 * h + 1, own]], axis=1)
                    p = jnp.exp(mxu(keys, q_n, NEAR) + bias - logs[n : n + 1, at])
                    dp = mxu(values, da_n, NEAR)
                    ds = (p * (dp - inner[n][:, at])).astype(BF)
                    dq[n, :, at] += mxu(keys, ds)
                    k_term = mxu(q_n, ds, FAR)
                    v_term = mxu(da_n, p.astype(BF), FAR)
                    dk = k_term if dk is None else dk + k_term
                    dv = v_term if dv is None else dv + v_term
                dkv[which, core, xs, 64 * n : 64 * n + 64, :] = dk.astype(BF)
                dkv[which, core, xs, 192 + 64 * n : 256 + 64 * n, :] = dv.astype(BF)
            return carry

        lax.fori_loop(0, 8, step, 0)

    half(0, (1 - yh) * 2)
    send(dkv.at[0, 1 - c], rx, csend.at[0], crecv.at[0], partner)
    arrived(rx, csend.at[0], crecv.at[0], partner)
    for xs in range(4):
        py[xs] = (dkv[0, c, xs].astype(F32) + rx[xs].astype(F32)).astype(BF)
    send(py, ry, csend.at[1], crecv.at[1], across)
    half(1, yh * 2)
    send(dkv.at[1, 1 - c], rl, csend.at[2], crecv.at[2], partner)
    for xs in range(4):
        for n in range(3):
            part = dq[n, :, 128 * xs : 128 * xs + 128] * 0.125
            sb[xs, 64 * n : 64 * n + 64, :] = part.astype(BF)
    arrived(rl, csend.at[2], crecv.at[2], partner)
    arrived(ry, csend.at[1], crecv.at[1], across)
    for xs in range(4):
        total = dkv[1, c, xs].astype(F32) + rl[xs].astype(F32) + ry[xs].astype(F32)
        sb[xs, 192:576, :] = total.astype(BF)
    dj[x] = sb[x]
    for s in (2, 1, 3):
        peer = peer_of(me, "x", s)
        send(sb.at[peer["x"]], dj.at[x], jsend.at[s - 1], jrecv.at[s - 1], peer)
    for s in (1, 3, 2):
        source = peer_of(me, "x", 4 - s)
        arrived(dj.at[source["x"]], jsend.at[s - 1], jrecv.at[s - 1], source)
    dh = dh_out[...]
    for j in range(3):
        at = slice(768 * j, 768 * j + 768)
        t = jnp.concatenate([dj[g, 192 * j : 192 * j + 192] for g in range(4)], axis=0)
        t = t.astype(F32).T.astype(BF)
        dj_out[:, at] = t
        if j != 1:
            row = 0 if j == 0 else 1
            vec_out[row : row + 1] = column_sum(t)
        dh = dh + mxu(t, vj[:, at], FAR)
    dh_out[...] = dh
    for copy in sends:
        copy.wait_send()


def backward_layer(dy, rows, up, before2, before1, q, kv, logs, att, lengths, wj, wu, wd):
    vmem = pl.BlockSpec(memory_space=pltpu.VMEM)
    anyspace = pl.BlockSpec(memory_space=pl.ANY)
    dma = pltpu.SemaphoreType.DMA
    out = jax.ShapeDtypeStruct
    return pl.pallas_call(
        backward_kernel,
        out_shape=[
            out((128, 768), F32),
            out((128, 2304), BF),
            out((128, 768), BF),
            out((128, 3072), BF),
            out((128, 768), BF),
            out((16, 768), F32),
        ],
        in_specs=[vmem] * 9 + [pl.BlockSpec(memory_space=pltpu.SMEM)] + [anyspace] * 3,
        out_specs=[vmem] * 6,
        scratch_shapes=[
            pltpu.VMEM((768, 3072), BF),
            pltpu.VMEM((768, 3072), BF),
            pltpu.VMEM((3072, 768), BF),
            pltpu.VMEM((4, 192, 128), BF),
            pltpu.VMEM((4, 192, 128), BF),
            pltpu.VMEM((2, 2, 4, 384, 128), BF),
            pltpu.VMEM((4, 384, 128), BF),
            pltpu.VMEM((4, 384, 128), BF),
            pltpu.VMEM((4, 384, 128), BF),
            pltpu.VMEM((4, 384, 128), BF),
            pltpu.VMEM((3, 64, 512), F32),
            pltpu.VMEM((4, 576, 128), BF),
            pltpu.VMEM((4, 576, 128), BF),
            dma((3,)),
            dma((3,)),
            dma((3,)),
            dma((3,)),
            dma((3,)),
            dma((3,)),
            dma((3,)),
        ],
        compiler_params=pltpu.CompilerParams(
            collective_id=3, has_side_effects=True, vmem_limit_bytes=60 * 1024 * 1024
        ),
        name="backward_layer",
    )(dy, rows, up, before2, before1, q, kv, logs, att, lengths, wj, wu, wd)


def body(
    inputs,
    lengths,
    joint_weight,
    query_bias,
    value_bias,
    output_weight,
    output_bias,
    first_gain,
    first_shift,
    up_weight,
    up_bias,
    down_weight,
    down_bias,
    second_gain,
    second_shift,
    cotangent,
):
    vectors = jnp.stack(
        (
            query_bias,
            value_bias,
            output_bias,
            first_gain,
            first_shift,
            down_bias,
            second_gain,
            second_shift,
        ),
        axis=1,
    )
    vectors = jnp.concatenate([vectors, up_bias.reshape(LAYERS, 4, 24)], axis=1)
    vectors = jnp.pad(vectors.reshape(24, 24), ((0, 8), (0, 104)))
    joint_and_out = jnp.concatenate([joint_weight, output_weight], axis=-1)
    pieces = []
    for layer_index in range(LAYERS):
        pieces += [up_weight[layer_index], down_weight[layer_index], joint_and_out[layer_index]]
    *gathered, vectors_all = gather_weights((*pieces, vectors))
    vectors_all = vectors_all.reshape(32, 32, 128)[:, :24, :24].reshape(32, LAYERS, 12, 24)
    rows_all = vectors_all[:, :, :8].transpose(1, 2, 0, 3).reshape(LAYERS, 8, 768)
    up_adds = vectors_all[:, :, 8:].transpose(1, 0, 2, 3).reshape(LAYERS, 3072)
    weights_of = []
    for layer_index in range(LAYERS):
        up_full, down_full, joint_out = gathered[3 * layer_index : 3 * layer_index + 3]
        weights_of.append(
            (joint_out.reshape(768, 3072), up_full.reshape(768, 3072), down_full.reshape(3072, 768))
        )
    rows_all = rows_all.astype(F32)
    up_adds = up_adds.astype(F32)
    hidden = inputs.reshape(128, 768)
    kept, outputs = [], []
    for l in range(LAYERS):
        result = forward_layer(
            hidden, rows_all[l], up_adds[l : l + 1], lengths, *weights_of[l]
        )
        kept.append((hidden, *result[1:]))
        hidden = result[0]
        outputs.append(hidden.reshape(1, 128, 768))
    grad_rows = cotangent.reshape(128, 768).astype(F32)
    layer_grads = [None] * LAYERS
    vector_grads = [None] * LAYERS
    for l in reversed(range(LAYERS)):
        hidden, q, kv, logs, att, mixed, before1, low, up, acts, before2 = kept[l]
        grad_rows, d_joint, d_branch, d_up, d_down, vector_grads[l] = backward_layer(
            grad_rows, rows_all[l], up, before2, before1, q, kv, logs, att, lengths, *weights_of[l]
        )
        layer_grads[l] = (hidden, mixed, low, acts, d_joint, d_branch, d_up, d_down)
    vectors = jnp.concatenate(vector_grads)
    joint_grad, out_grad, up_grad, down_grad, vectors = reduce_grads(layer_grads, vectors)
    vectors = vectors.reshape(LAYERS, 16, 768)
    owner = lax.axis_index("batch") * 4 + lax.axis_index("blk")
    own_rows = lax.dynamic_slice_in_dim(vectors[:, :8], owner * 24, 24, axis=2)
    own_up = lax.dynamic_slice_in_dim(vectors[:, 8:12].reshape(LAYERS, 3072), owner * 96, 96, axis=1)
    stacked = (
        joint_grad,
        own_rows[:, 0],
        own_rows[:, 1],
        out_grad,
        own_rows[:, 2],
        own_rows[:, 3],
        own_rows[:, 4],
        up_grad,
        own_up,
        down_grad,
        own_rows[:, 5],
        own_rows[:, 6],
        own_rows[:, 7],
    )
    activations = jnp.stack(outputs)
    input_grad = grad_rows.reshape(1, 128, 768)
    return (
        activations,
        input_grad,
        stacked[0],
        stacked[1],
        stacked[2],
        stacked[3],
        stacked[4],
        stacked[5],
        stacked[6],
        stacked[7],
        stacked[8],
        stacked[9],
        stacked[10],
        stacked[11],
        stacked[12],
    )


def solution(mesh):
    placed = (
        P("batch", ("head", "blk"), None),
        P("batch"),
        P(None, ("batch", "blk"), None),
        P(None, ("batch", "blk")),
        P(None, ("batch", "blk")),
        P(None, ("batch", "blk"), None),
        P(None, ("batch", "blk")),
        P(None, ("batch", "blk")),
        P(None, ("batch", "blk")),
        P(None, ("batch", "blk"), None),
        P(None, ("batch", "blk")),
        P(None, ("batch", "blk"), None),
        P(None, ("batch", "blk")),
        P(None, ("batch", "blk")),
        P(None, ("batch", "blk")),
        P("batch", ("head", "blk"), None),
    )
    return jax.shard_map(
        body,
        mesh=mesh,
        in_specs=placed,
        out_specs=(
            P(None, "batch", ("head", "blk"), None),
            P("batch", ("head", "blk"), None),
            P(None, ("batch", "blk"), None),
            P(None, ("batch", "blk")),
            P(None, ("batch", "blk")),
            P(None, ("batch", "blk"), None),
            P(None, ("batch", "blk")),
            P(None, ("batch", "blk")),
            P(None, ("batch", "blk")),
            P(None, ("batch", "blk"), None),
            P(None, ("batch", "blk")),
            P(None, ("batch", "blk"), None),
            P(None, ("batch", "blk")),
            P(None, ("batch", "blk")),
            P(None, ("batch", "blk")),
        ),
        check_vma=False,
    )
```

```python
import functools

import jax
import jax.numpy as jnp
from jax import lax
from jax.experimental import pallas as pl
from jax.experimental.pallas import tpu as pltpu
from jax.sharding import PartitionSpec as P

LAYERS = 2


EPSILON = 1e-12
MASKED = -1e30


MESH = pl.DeviceIdType.MESH
ALL = slice(None)


def my_place():
    b, x, k = lax.axis_index("batch"), lax.axis_index("head"), lax.axis_index("blk")
    return {"z": b // 2, "y": (k // 2) * 2 + b % 2, "x": x, "c": k % 2}


def device_of(place):
    return (
        place["z"] * 2 + place["y"] % 2,
        place["x"],
        (place["y"] // 2) * 2 + place["c"],
    )


def peer_of(place, axis, step):
    other = dict(place)
    other[axis] = (place[axis] + step) % (2 if axis == "c" else 4)
    return other


def greet_all(place):
    barrier = pltpu.get_barrier_semaphore()
    peers = [peer_of(place, a, s) for a in ("x", "y", "z") for s in (1, 2, 3)]
    peers.append(peer_of(place, "c", 1))
    for p in peers:
        pl.semaphore_signal(barrier, inc=1, device_id=device_of(p), device_id_type=MESH)
    pl.semaphore_wait(barrier, len(peers))


def remote(src, dst, send, recv, place):
    return pltpu.make_async_remote_copy(
        src_ref=src,
        dst_ref=dst,
        send_sem=send,
        recv_sem=recv,
        device_id=device_of(place),
        device_id_type=MESH,
    )


class Gather:
    def __init__(self, me, pieces, ins, outs, sems):
        self.me, self.pieces, self.ins, self.outs = me, pieces, ins, outs
        self.send, self.recv, self.fsend, self.frecv, self.local = sems
        self.partner = peer_of(me, "c", 1)
        self.started, self.locals = [], {}

    def order(self, i):
        return self.pieces[i][3]

    def direct(self, i, phase):
        return phase in self.pieces[i][5]

    def region(self, i, phase, place, half=None):
        array, start, width, order, by_rows, _ = self.pieces[i]
        done = order[:phase]
        z = ALL if "z" in done else place["z"]
        y = (ALL, ALL) if "y" in done else (place["y"] % 2, place["y"] // 2)
        lines = ALL
        if "x" in order and "x" not in done:
            width = width // 4
            start = start + place["x"] * width
        if half is not None:
            if by_rows:
                count = self.outs[array].shape[-2] // 2
                lines = pl.ds(count * half, count)
            else:
                width = width // 2
                start = start + half * width
        columns = self.columns(array, start, width)
        return self.outs[array].at[z, y[0], y[1], place["c"], lines, columns]

    def columns(self, array, start, width):
        if width == self.outs[array].shape[-1]:
            return ALL
        return pl.ds(start if isinstance(start, int) else pl.multiple_of(start, 128), width)

    def own(self, i):
        array, start, width, order, _, _ = self.pieces[i]
        if "x" in order:
            width = width // 4
            start = start + self.me["x"] * width
        columns = self.columns(array, start, width)
        return self.ins[array].at[ALL, columns]

    def copy(self, src, dst, s, r, place):
        copy = remote(src, dst, s, r, place)
        copy.start()
        self.started.append(copy)

    def near(self, i, phase):
        axis = self.order(i)[phase]
        return peer_of(self.me, axis, 1), peer_of(self.me, axis, 3), peer_of(self.me, axis, 2)

    def start(self, i, phase):
        right, left, opposite = self.near(i, phase)
        dst = self.region(i, phase, self.me)
        if phase == 0:
            copy = pltpu.make_async_copy(self.own(i), dst, self.local.at[i])
            copy.start()
            self.locals[i] = copy
        src = self.own(i) if phase == 0 else dst
        places = [(0, right), (1, left)]
        if self.direct(i, phase):
            places = [(2, opposite)] + places
        for j, place in places:
            self.copy(src, dst, self.send.at[i, phase, j], self.recv.at[i, phase, j], place)
        if phase == 0:
            self.copy(src, dst, self.fsend.at[i, 3, 0], self.frecv.at[i, 3, 0], self.partner)

    def arrived(self, slot, i, phase, j, place):
        remote(
            slot, slot, self.send.at[i, phase, j], self.recv.at[i, phase, j], place
        ).wait_recv()

    def pass_on(self, i, phase, j, place):
        slot = self.region(i, phase, place)
        self.copy(
            slot, slot, self.fsend.at[i, phase, j], self.frecv.at[i, phase, j], self.partner
        )

    def relay(self, i, phase):
        right, left, _ = self.near(i, phase)
        for j, source, target in ((0, left, right), (1, right, left)):
            self.arrived(self.region(i, phase, source), i, phase, j, source)
            if not self.direct(i, phase):
                part = self.region(i, phase, source, j)
                self.copy(
                    part, part, self.send.at[i, phase, 2 + j], self.recv.at[i, phase, 2 + j], target
                )
            self.pass_on(i, phase, j, source)

    def close(self, i, phase):
        right, left, opposite = self.near(i, phase)
        if self.direct(i, phase):
            self.arrived(self.region(i, phase, opposite), i, phase, 2, opposite)
        else:
            for j, source in ((0, left), (1, right)):
                self.arrived(self.region(i, phase, opposite, j), i, phase, 2 + j, source)
        self.pass_on(i, phase, 2, opposite)
        if phase == 0:
            self.locals[i].wait()

    def complete(self, i):
        slots = [((3, 0), self.region(i, 0, self.partner))]
        for phase, axis in enumerate(self.order(i)):
            for j, s in ((0, 3), (1, 1), (2, 2)):
                slots.append(((phase, j), self.region(i, phase, peer_of(self.partner, axis, s))))
        for at, slot in slots:
            remote(
                slot, slot, self.fsend.at[i, *at], self.frecv.at[i, *at], self.partner
            ).wait_recv()

    def end(self):
        for copy in self.started:
            copy.wait_send()


    def relay_all(self, phase, *group):
        for i in group:
            self.relay(i, phase)

    def close_all(self, phase, *group):
        for i in group:
            self.close(i, phase)
            if phase + 1 < len(self.order(i)):
                self.start(i, phase + 1)


def joint_pieces(array, direct):
    return (
        (array, 0, 1536, ("y", "z"), False, direct),
        (array, 1536, 1536, ("z", "y"), False, direct),
    )


def feed_pieces(array, order, direct):
    return (
        (array, 0, 3072, order, False, direct),
        (array + 1, 0, 384, ("y", "z"), True, direct),
        (array + 1, 384, 384, ("y", "z"), True, direct),
    )


NEVER = ()
FIRST_PIECES = (
    feed_pieces(0, ("y", "z", "x"), NEVER)
    + joint_pieces(2, NEVER)
    + joint_pieces(3, NEVER)
    + ((4, 0, 256, ("y", "z"), True, NEVER),)
)
SECOND_PIECES = feed_pieces(0, ("y", "z", "x"), NEVER)


THIRDS = (("x", "y", "z"), ("y", "z", "x"), ("z", "x", "y"))


def reduce_kernel(*refs):
    ins = refs[:11]
    joint_out, out_out, up_out, down_out, vec_out = refs[11:16]
    lhs, rhs, g, o1, r1, s1, o2, r2, s2, r3, last, vc, va = refs[16:29]
    csend, crecv, lsem, ps, pr, qs, qr, vs, vr = refs[29:]
    vec_in = ins[10]
    me = my_place()
    partner = peer_of(me, "c", 1)
    c = me["c"]
    greet_all(me)
    half = pl.ds(pl.multiple_of(c * 128, 128), 128)
    other_half = pl.ds(pl.multiple_of((1 - c) * 128, 128), 128)
    starts = (0, 3072, 3840, 6144)
    widths = (3072, 768, 2304, 768)
    layers = (1, 0)

    def exchanges(l):
        lhs_in, rhs_in = ins[5 * l], ins[5 * l + 1 : 5 * l + 5]
        away = [
            remote(
                lhs_in.at[1 - c],
                lhs.at[l, ALL, half],
                csend.at[l, 0],
                crecv.at[l, 0],
                partner,
            )
        ]
        here = [pltpu.make_async_copy(lhs_in.at[c], lhs.at[l, ALL, half], lsem.at[l, 0])]
        for j in range(4):
            dst = rhs.at[l, half, pl.ds(starts[j], widths[j])]
            away.append(remote(rhs_in[j], dst, csend.at[l, j + 1], crecv.at[l, j + 1], partner))
            here.append(pltpu.make_async_copy(rhs_in[j], dst, lsem.at[l, j + 1]))
        return away, here

    exchanged = {}
    for l in layers:
        exchanged[l] = exchanges(l)
        for copy in exchanged[l][0] + exchanged[l][1]:
            copy.start()

    vec_axes = ("c", "x", "y", "z")
    vec_sends = []

    def vec_slot(phase, place):
        if phase == 0:
            return vc.at[place["c"]]
        return va.at[phase - 1, place[vec_axes[phase]]]

    def vec_start(phase, value):
        vec_slot(phase, me)[...] = value.astype(jnp.bfloat16)
        for s in range(1, 2 if phase == 0 else 4):
            copy = remote(
                vec_slot(phase, me),
                vec_slot(phase, me),
                vs.at[phase, s - 1],
                vr.at[phase, s - 1],
                peer_of(me, vec_axes[phase], s),
            )
            copy.start()
            vec_sends.append(copy)

    def vec_finish(phase):
        count = 2 if phase == 0 else 4
        for s in range(1, count):
            src = peer_of(me, vec_axes[phase], count - s)
            slot = vec_slot(phase, src)
            remote(slot, slot, vs.at[phase, s - 1], vr.at[phase, s - 1], src).wait_recv()
        total = None
        for j in range(count):
            part = (vc[j] if phase == 0 else va[phase - 1, j]).astype(jnp.float32)
            total = part if total is None else total + part
        return total

    vec_start(0, vec_in[...])

    sends = []

    def send_chunks(phase, t, l, source, target):
        axis = THIRDS[t][phase] if phase < 3 else "x"
        for s in (2, 1, 3):
            peer = peer_of(me, axis, s)
            copy = remote(
                source(peer[axis]),
                target(s),
                ps.at[phase, t, l, s - 1],
                pr.at[phase, t, l, s - 1],
                peer,
            )
            copy.start()
            sends.append(copy)

    def await_chunks(phase, t, l, target):
        axis = THIRDS[t][phase] if phase < 3 else "x"
        for s in (1, 3, 2):
            slot = target(s)
            remote(
                slot,
                slot,
                ps.at[phase, t, l, s - 1],
                pr.at[phase, t, l, s - 1],
                peer_of(me, axis, s),
            ).wait_recv()

    def ring_copy(phase, t, l, j, src, dst, peer):
        copy = remote(src, dst, qs.at[phase, t, l, j], qr.at[phase, t, l, j], peer)
        copy.start()
        sends.append(copy)

    def ring_wait(phase, t, l, j, slot, peer):
        remote(slot, slot, qs.at[phase, t, l, j], qr.at[phase, t, l, j], peer).wait_recv()

    def ring_refs(phase, t, l):
        axis = THIRDS[t][phase]
        places = [peer_of(me, axis, s) for s in (1, 3, 2)]
        held, over, got = ((g, o1, r1), (s1, o2, r2))[phase]
        return axis, places, held.at[t, l], over.at[t, l], got.at[t, l]

    low_half, high_half = pl.ds(0, 2), pl.ds(2, 2)

    def ring_start(phase, t, l):
        axis, (right, left, far), held, over, got = ring_refs(phase, t, l)
        ring_copy(phase, t, l, 0, held.at[far[axis], low_half], over.at[0], right)
        ring_copy(phase, t, l, 1, held.at[far[axis], high_half], over.at[1], left)
        ring_copy(
            phase, t, l, 2, held.at[right[axis], high_half], got.at[0, high_half], right
        )
        ring_copy(phase, t, l, 3, held.at[left[axis], low_half], got.at[1, low_half], left)

    def ring_middle(phase, t, l):
        axis, (right, left, far), held, over, got = ring_refs(phase, t, l)
        for j, source, target in ((0, left, right), (1, right, left)):
            ring_wait(phase, t, l, j, over.at[j], source)
            for a in range(2):
                at = target[axis]
                if phase == 0:

                    def merge(b, carry, a=a, j=j, at=at):
                        total = held[at, 2 * j + a, b].astype(f32) + over[j, a, b].astype(f32)
                        held[at, 2 * j + a, b] = total.astype(jnp.bfloat16)
                        return carry

                    lax.fori_loop(0, 4, merge, 0)
                else:
                    total = held[at, 2 * j + a].astype(f32) + over[j, a].astype(f32)
                    held[at, 2 * j + a] = total.astype(jnp.bfloat16)
            part = (low_half, high_half)[j]
            ring_copy(
                phase, t, l, 4 + j, held.at[target[axis], part], got.at[j, part], target
            )

    def ring_finish(phase, t, l):
        axis, (right, left, far), held, over, got = ring_refs(phase, t, l)
        ring_wait(phase, t, l, 2, got.at[0, high_half], left)
        ring_wait(phase, t, l, 3, got.at[1, low_half], right)
        ring_wait(phase, t, l, 4, got.at[0, low_half], left)
        ring_wait(phase, t, l, 5, got.at[1, high_half], right)

    f32 = jnp.float32
    for l in layers:
        away, here = exchanged[l]
        for copy in here:
            copy.wait()
        for copy in away:
            copy.wait_recv()
        for t in range(3):
            for q in range(4):
                unit = (0, 1 + q, 5 if q < 3 else 6)[t]
                col = (q * 768, 3072, 3840 + q * 768)[t]
                block = jnp.dot(
                    lhs[l, 384 * unit : 384 * unit + 384, :],
                    rhs[l, :, col : col + 768],
                    preferred_element_type=jnp.float32,
                )
                for i in range(16):
                    z, y = i // 4, (i % 2) * 2 + (i // 2) % 2
                    at = ((q, y, z), (y, z, q), (z, q, y))[t]
                    g[t, l, at[0], at[1], at[2]] = block[24 * i : 24 * i + 24].astype(jnp.bfloat16)
            ring_start(0, t, l)
    vec_start(1, vec_finish(0))
    for l in layers:
        for t in range(3):
            ring_middle(0, t, l)
    for l in layers:
        for t in range(3):
            mine = me[THIRDS[t][0]]
            ring_finish(0, t, l)

            def add1(i, carry, t=t, l=l, mine=mine):
                a, b = i // 4, i % 4
                total = g[t, l, mine, a, b].astype(f32)
                for s in range(2):
                    total = total + r1[t, l, s, a, b].astype(f32)
                s1[t, l, a, b] = total.astype(jnp.bfloat16)
                return carry

            lax.fori_loop(0, 16, add1, 0)
            ring_start(1, t, l)
    vec_start(2, vec_finish(1))
    for l in layers:
        for t in range(3):
            ring_middle(1, t, l)
    for l in layers:
        for t in range(3):
            mine = me[THIRDS[t][1]]
            ring_finish(1, t, l)
            for a in range(4):
                total = s1[t, l, mine, a].astype(f32)
                for s in range(2):
                    total = total + r2[t, l, s, a].astype(f32)
                s2[t, l, a] = total.astype(jnp.bfloat16)
            send_chunks(
                2, t, l, lambda a, t=t, l=l: s2.at[t, l, a], lambda s, t=t, l=l: r3.at[t, l, s - 1]
            )
    vec_start(3, vec_finish(2))
    for l in layers:
        for t in range(3):
            mine = me[THIRDS[t][2]]
            await_chunks(2, t, l, lambda s, t=t, l=l: r3.at[t, l, s - 1])
            total = s2[t, l, mine].astype(f32)
            for s in range(3):
                total = total + r3[t, l, s].astype(f32)
            last[t, l, me["x"]] = total.astype(jnp.bfloat16)
            send_chunks(
                3,
                t,
                l,
                lambda a, t=t, l=l: last.at[t, l, me["x"]],
                lambda s, t=t, l=l: last.at[t, l, me["x"]],
            )
    vec_out[...] = vec_finish(3)
    for l in layers:
        for t in range(3):
            await_chunks(3, t, l, lambda s, t=t, l=l: last.at[t, l, (me["x"] + 4 - s) % 4])
            for q in range(4):
                part = last[t, l, q].astype(f32)
                if t == 0:
                    up_out[l, :, 768 * q : 768 * q + 768] = part
                elif t == 1:
                    down_out[l, 24 * q : 24 * q + 24, :] = part
                elif q < 3:
                    joint_out[l, :, 768 * q : 768 * q + 768] = part
                else:
                    out_out[l] = part
    for copy in sends + vec_sends + [a for l in layers for a in exchanged[l][0]]:
        copy.wait_send()


def for_owner_cores(array):
    tokens, width = array.shape
    n = width // 768
    t = array.T.reshape(16, 2, n, 24, tokens).transpose(1, 2, 0, 3, 4)
    return t.reshape(2, n * 384, tokens)


def reduce_grads(per_layer, vectors):
    operands = []
    for hidden, mixed, first, acts, d_joint, d_branch, d_up, d_down in per_layer:
        operands.append(
            jnp.concatenate([for_owner_cores(a) for a in (first, acts, hidden, mixed)], axis=1)
        )
        operands += [d_up, d_down, d_joint, d_branch]
    anyspace = pl.BlockSpec(memory_space=pl.ANY)
    vmem = pl.BlockSpec(memory_space=pltpu.VMEM)
    bf, dma = jnp.bfloat16, pltpu.SemaphoreType.DMA
    return pl.pallas_call(
        reduce_kernel,
        out_shape=[
            jax.ShapeDtypeStruct((2, 24, 2304), jnp.float32),
            jax.ShapeDtypeStruct((2, 24, 768), jnp.float32),
            jax.ShapeDtypeStruct((2, 24, 3072), jnp.float32),
            jax.ShapeDtypeStruct((2, 96, 768), jnp.float32),
            jax.ShapeDtypeStruct((32, 768), jnp.float32),
        ],
        in_specs=[anyspace] * 10 + [vmem],
        out_specs=[vmem] * 5,
        scratch_shapes=[
            pltpu.VMEM((2, 2688, 256), bf),
            pltpu.VMEM((2, 256, 6912), bf),
            pltpu.VMEM((3, 2, 4, 4, 4, 24, 768), bf),
            pltpu.VMEM((3, 2, 2, 2, 4, 24, 768), bf),
            pltpu.VMEM((3, 2, 2, 4, 4, 24, 768), bf),
            pltpu.VMEM((3, 2, 4, 4, 24, 768), bf),
            pltpu.VMEM((3, 2, 2, 2, 24, 768), bf),
            pltpu.VMEM((3, 2, 2, 4, 24, 768), bf),
            pltpu.VMEM((3, 2, 4, 24, 768), bf),
            pltpu.VMEM((3, 2, 3, 24, 768), bf),
            pltpu.VMEM((3, 2, 4, 24, 768), bf),
            pltpu.VMEM((2, 32, 768), bf),
            pltpu.VMEM((3, 4, 32, 768), bf),
            dma((2, 5)),
            dma((2, 5)),
            dma((2, 5)),
            dma((4, 3, 2, 3)),
            dma((4, 3, 2, 3)),
            dma((2, 3, 2, 6)),
            dma((2, 3, 2, 6)),
            dma((4, 3)),
            dma((4, 3)),
        ],
        compiler_params=pltpu.CompilerParams(
            collective_id=1, has_side_effects=True, vmem_limit_bytes=62 * 1024 * 1024
        ),
        name="reduce_grads",
    )(*operands, vectors)


FAR = (((1,), (1,)), ((), ()))
NEAR = (((0,), (0,)), ((), ()))
F32 = jnp.float32
BF = jnp.bfloat16
KEYS = 128


def mxu(a, b, dims=None):
    if dims is None:
        return jnp.dot(a, b, preferred_element_type=F32)
    return lax.dot_general(a, b, dims, preferred_element_type=F32)


def normalized(values):
    average = jnp.mean(values, axis=-1, keepdims=True)
    centered = values - average
    variance = jnp.mean(centered * centered, axis=-1, keepdims=True)
    r = lax.rsqrt(variance + EPSILON)
    return centered * r, r


def norm_backward(values, gain, grad):
    xhat, r = normalized(values)
    g = grad * gain
    back = r * (
        g - jnp.mean(g, axis=-1, keepdims=True) - xhat * jnp.mean(g * xhat, axis=-1, keepdims=True)
    )
    gain_grad = jnp.sum(grad * xhat, axis=0, keepdims=True)
    return back, gain_grad, jnp.sum(grad, axis=0, keepdims=True)


def normal_cdf(u):
    return 0.5 * (1.0 + lax.erf(u * 0.7071067811865476))


def greet_sequence(me):
    barrier = pltpu.get_barrier_semaphore()
    peers = [peer_of(me, "x", s) for s in (1, 2, 3)]
    peers += [peer_of(me, "c", 1), peer_of(me, "y", 2)]
    for p in peers:
        pl.semaphore_signal(barrier, inc=1, device_id=device_of(p), device_id_type=MESH)
    pl.semaphore_wait(barrier, len(peers))


def key_bias(length, block, xs):
    limit = length - xs * 512 - block * 128
    rows = lax.broadcasted_iota(jnp.int32, (KEYS, 128), 0)
    return jnp.where(rows < limit, 0.0, MASKED)


def forward_kernel(first, *refs):
    refs = list(refs)

    def take(count):
        out = refs[:count]
        del refs[:count]
        return out

    hid, lens = take(2)
    if first:
        small_in = take(9)
        up, down, joint_in = take(3)
        shards = [up.at[0], down.at[0], joint_in.at[0], joint_in.at[1]]
    else:
        rows, up_add, wj = take(3)
        up, down = take(2)
        shards = [up.at[1], down.at[1]]
    res, q_out, kv_out, log_out, att_out, mixed_out = take(6)
    before1_out, low_out, up_out, act_out, before2_out = take(5)
    if first:
        rows_out, add_out = take(2)
    gathered = take(4 if first else 2)
    vj, vu, vd, qs, qb, kvb, sc, acc, back, ab, vv, rsum, usum = take(13)
    wsem, osem, qsend, qrecv, xsend, xrecv, csend, crecv, ysend, yrecv, fsend, frecv = take(12)
    bsend, brecv = take(2)
    flat, own_small = take(2)
    me = my_place()
    if first:
        shards.append(own_small)
    lands = [vu, vd, vj, gathered[3], vv] if first else [vu, vd]
    plan = Gather(me, FIRST_PIECES if first else SECOND_PIECES, shards, lands, refs)
    feed, joint, later, small = (0, 1, 2), (3, 4), (5, 6), (7,)
    x, c = me["x"], me["c"]
    yh = me["y"] // 2
    k = yh * 2 + c
    partner, across = peer_of(me, "c", 1), peer_of(me, "y", 2)
    k_partner = yh * 2 + 1 - c
    k_across = (1 - yh) * 2 + c
    k_diag = (1 - yh) * 2 + 1 - c
    greet_all(me)
    loads = []

    def load(src, dst):
        copy = pltpu.make_async_copy(src, dst, wsem.at[len(loads)])
        copy.start()
        loads.append(copy)

    if first:
        flat[...] = jnp.zeros_like(flat)
        for j in range(9):
            for l in range(2):
                flat[16 * l + j : 16 * l + j + 1, 0 : small_in[j].shape[1]] = small_in[j][
                    l : l + 1, :
                ].astype(F32)
        owner = lax.axis_index("batch") * 4 + lax.axis_index("blk")
        lines = lax.broadcasted_iota(jnp.int32, (32, 256), 0) % 16
        moved = pltpu.roll(flat[...], (owner * 24) % 128, axis=1)
        moved_up = pltpu.roll(flat[...], (owner * 96) % 128, axis=1)
        own_small[...] = jnp.where(lines == 8, moved_up, moved).astype(BF)
        for i in small + joint + feed:
            plan.start(i, 0)
        plan.relay_all(0, *small, *joint)
        plan.close_all(0, *small, *joint)
        plan.relay_all(0, *feed)
        plan.relay_all(1, *small, *joint)
        plan.close_all(0, *feed)
        plan.close_all(1, *small, *joint)
        for i in small + joint:
            plan.complete(i)
        load(vj, gathered[2])
        rsum[...] = jnp.zeros_like(rsum)
        usum[...] = jnp.zeros_like(usum)
        for o in range(32):
            z, yl, yh, core = o // 8, (o // 4) % 2, (o // 2) % 2, o % 2
            at, up_at = (24 * o) // 128 * 128, (96 * o) // 128 * 128
            for l in range(2):
                part = vv[z, yl, yh, core, 16 * l : 16 * l + 16, :].astype(F32)
                rsum[l, :, at : at + 256] += part[0:8]
                usum[l, 0:1, up_at : up_at + 256] += part[8:9]
        for l in range(2):
            rows_out[l] = rsum[l, :, 0:768]
            add_out[l] = usum[l, :, 0:3072]
        rows, up_add = rows_out.at[0], add_out.at[0]
    else:
        load(wj, vj)
        for i in feed:
            plan.start(i, 0)
        plan.relay_all(0, 0)
        plan.close_all(0, 0)
        rows, up_add = rows.at[1], up_add.at[1]

    def joint_columns(start):
        return vj[:, :, :, :, :, start : start + 768].reshape(768, 768)

    sends = []

    def send(src, dst, s, r, place):
        copy = remote(src, dst, s, r, place)
        copy.start()
        sends.append(copy)

    def arrived(slot, s, r, place):
        remote(slot, slot, s, r, place).wait_recv()

    if not first:
        loads[0].wait()
    for j in (1, 2, 0):
        p = mxu(hid[...], joint_columns(768 * j))
        if j == 0:
            p = p + rows[0:1]
        if j == 2:
            p = p + rows[1:2]
        p = p.astype(BF).astype(F32)
        if j == 0:
            p = p * 0.125
        p = p.T.astype(BF)
        for g in range(4):
            qs[g, 192 * j : 192 * j + 192] = p[192 * g : 192 * g + 192]
        if j == 2:
            kvb[k, x] = qs[x, 192:576]
            for s in (2, 1, 3):
                peer = peer_of(me, "x", s)
                send(
                    qs.at[peer["x"], 192:576], kvb.at[k, x], xsend.at[s - 1], xrecv.at[s - 1], peer
                )
            send(kvb.at[k, x], kvb.at[k, x], ysend.at[0], yrecv.at[0], across)
            send(kvb.at[k, x], kvb.at[k, x], csend.at[0], crecv.at[0], partner)
    qb[x] = qs[x, 0:192]
    for s in (2, 1, 3):
        peer = peer_of(me, "x", s)
        send(qs.at[peer["x"], 0:192], qb.at[x], qsend.at[s - 1], qrecv.at[s - 1], peer)
    if first:
        plan.relay_all(1, 0)
        plan.close_all(1, 0)
        for i in later:
            plan.start(i, 0)
    else:
        plan.relay_all(1, 0)
        plan.relay_all(0, 1, 2)
        plan.close_all(1, 0)
        plan.close_all(0, 1, 2)
    for s in (1, 3, 2):
        source = peer_of(me, "x", 4 - s)
        slot = kvb.at[k, source["x"]]
        arrived(slot, xsend.at[s - 1], xrecv.at[s - 1], source)
        send(slot, slot, ysend.at[s], yrecv.at[s], across)
        send(slot, slot, csend.at[s], crecv.at[s], partner)
    if first:
        plan.relay_all(1, 1, 2)
        plan.relay_all(0, *later)
    for s in (1, 3, 2):
        source = peer_of(me, "x", 4 - s)
        arrived(qb.at[source["x"]], qsend.at[s - 1], qrecv.at[s - 1], source)
    for s in (0, 1, 3, 2):
        arrived(kvb.at[k_partner, (x + 4 - s) % 4], csend.at[s], crecv.at[s], partner)

    length = lens[0]
    queries = [
        jnp.concatenate([qb[xs, 64 * n : 64 * n + 64] for xs in range(4)], axis=1)
        for n in range(3)
    ]

    def half(b0, b1, old):
        def scores(i, peaks):
            b = b0 + (b1 - b0) * (i // 4)
            xs = i % 4
            bias = key_bias(length, b, xs)
            bias = jnp.concatenate([bias] * 4, axis=1)
            new = []
            for n in range(3):
                keys = kvb[b, xs, 64 * n : 64 * n + 64, :]
                st = mxu(keys, queries[n], NEAR) + bias
                sc[n, pl.ds(pl.multiple_of(i * KEYS, KEYS), KEYS), :] = st
                new.append(jnp.maximum(peaks[n], jnp.max(st.reshape(16, 8, 512), axis=0)))
            return tuple(new)

        start = tuple(jnp.full((8, 512), MASKED, F32) for _ in range(3))
        peaks = lax.fori_loop(0, 8, scores, start)
        peaks = [jnp.max(p, axis=0, keepdims=True) for p in peaks]
        if old is not None:
            peaks = [jnp.maximum(p, o[0]) for p, o in zip(peaks, old)]
        totals = []
        for n in range(3):
            if old is None:
                acc[n] = jnp.zeros((64, 512), F32)
                totals.append(jnp.zeros((8, 512), F32))
            else:
                shrink = jnp.exp(old[n][0] - peaks[n])
                acc[n] = acc[n] * shrink
                totals.append(old[n][1] * shrink)

        def mix(i, sums):
            b = b0 + (b1 - b0) * (i // 2)
            xs = (i % 2) * 2
            new = []
            for n in range(3):
                at = pl.ds(pl.multiple_of(i * 256, 256), 256)
                p = jnp.exp(sc[n, at, :] - peaks[n])
                new.append(sums[n] + jnp.sum(p.reshape(32, 8, 512), axis=0))
                v = slice(192 + 64 * n, 256 + 64 * n)
                values = jnp.concatenate([kvb[b, xs, v, :], kvb[b, xs + 1, v, :]], axis=1)
                acc[n] += mxu(values, p.astype(BF))
            return tuple(new)

        totals = lax.fori_loop(0, 4, mix, tuple(totals))
        return list(zip(peaks, totals))

    state = half(k, k_partner, None)
    if first:
        plan.close_all(0, *later)
        plan.close_all(1, 1, 2)
        plan.relay_all(2, 0)
    else:
        plan.relay_all(1, 1, 2)
        plan.relay_all(2, 0)
    for s in (0, 1, 3, 2):
        slot = kvb.at[k_across, (x + 4 - s) % 4]
        arrived(slot, ysend.at[s], yrecv.at[s], across)
        send(slot, slot, fsend.at[s], frecv.at[s], partner)
    for s in (0, 1, 3, 2):
        arrived(kvb.at[k_diag, (x + 4 - s) % 4], fsend.at[s], frecv.at[s], partner)
    keep = pltpu.make_async_copy(kvb, kv_out, osem)
    keep.start()
    state = half(k_across, k_diag, state)
    log_out[...] = jnp.zeros_like(log_out)
    for n in range(3):
        total = jnp.sum(state[n][1], axis=0, keepdims=True)
        mixed = acc[n] / total
        att_out[64 * n : 64 * n + 64, :] = mixed
        log_out[n : n + 1, :] = state[n][0] + jnp.log(total)
        for xs in range(4):
            back[xs, 64 * n : 64 * n + 64, :] = mixed[:, 128 * xs : 128 * xs + 128].astype(BF)
    ab[x] = back[x]
    for s in (2, 1, 3):
        peer = peer_of(me, "x", s)
        send(back.at[peer["x"]], ab.at[x], bsend.at[s - 1], brecv.at[s - 1], peer)
    q_out[...] = qb[...]
    if first:
        plan.relay_all(1, *later)
    else:
        plan.close_all(1, 1, 2)
    plan.close_all(2, 0)
    for i in feed:
        plan.complete(i)
    load(vu, gathered[0])
    load(vd, gathered[1])
    for s in (1, 3, 2):
        source = peer_of(me, "x", 4 - s)
        arrived(ab.at[source["x"]], bsend.at[s - 1], brecv.at[s - 1], source)
    mixed = ab[...].reshape(768, 128).astype(F32).T.astype(BF)
    mixed_out[...] = mixed
    before = hid[...].astype(F32) + (mxu(mixed, joint_columns(2304)) + rows[2:3])
    before1_out[...] = before
    first_norm = normalized(before)[0] * rows[3:4] + rows[4:5]
    low = first_norm.astype(BF)
    low_out[...] = low
    second = first_norm + rows[5:6]
    for q in range(4):
        at = slice(768 * q, 768 * q + 768)
        u = mxu(low, vu[:, :, :, :, :, at].reshape(768, 768)) + up_add[0:1, at]
        up_out[:, at] = u
        a = (u * normal_cdf(u)).astype(BF)
        act_out[:, at] = a
        second = second + mxu(a, vd[q].reshape(768, 768))
    before2_out[...] = second
    res[...] = (normalized(second)[0] * rows[6:7] + rows[7:8]).astype(BF)
    keep.wait()
    if first:
        plan.close_all(1, *later)
        for i in later:
            plan.complete(i)
    plan.end()
    for copy in loads[0 if first else 1 :]:
        copy.wait()
    for copy in sends:
        copy.wait_send()


def forward_layer(first, hidden, lengths, known, shards):
    vmem = pl.BlockSpec(memory_space=pltpu.VMEM)
    anyspace = pl.BlockSpec(memory_space=pl.ANY)
    dma = pltpu.SemaphoreType.DMA
    out = jax.ShapeDtypeStruct
    n = len(FIRST_PIECES if first else SECOND_PIECES)
    got = [(24, 3072), (96, 768)]
    if first:
        got += [(24, 3072), (24, 3072)]
    return pl.pallas_call(
        functools.partial(forward_kernel, first),
        out_shape=[
            out((128, 768), BF),
            out((4, 192, 128), BF),
            out((4, 4, 384, 128), BF),
            out((8, 512), F32),
            out((192, 512), F32),
            out((128, 768), BF),
            out((128, 768), F32),
            out((128, 768), BF),
            out((128, 3072), F32),
            out((128, 3072), BF),
            out((128, 768), F32),
        ]
        + ([out((2, 8, 768), F32), out((2, 8, 3072), F32)] if first else [])
        + [out((4, 2, 2, 2, *s), BF) for s in got],
        in_specs=[vmem, pl.BlockSpec(memory_space=pltpu.SMEM)]
        + ([vmem] * 9 if first else [vmem, vmem, anyspace])
        + [anyspace] * len(shards),
        out_specs=[vmem, vmem, anyspace]
        + [vmem] * (10 if first else 8)
        + [anyspace] * len(got),
        scratch_shapes=[
            pltpu.VMEM((4, 2, 2, 2, 24, 3072), BF),
            pltpu.VMEM((4, 2, 2, 2, 24, 3072), BF),
            pltpu.VMEM((4, 2, 2, 2, 96, 768), BF),
            pltpu.VMEM((4, 576, 128), BF),
            pltpu.VMEM((4, 192, 128), BF),
            pltpu.VMEM((4, 4, 384, 128), BF),
            pltpu.VMEM((3, 1024, 512), F32),
            pltpu.VMEM((3, 64, 512), F32),
            pltpu.VMEM((4, 192, 128), BF),
            pltpu.VMEM((4, 192, 128), BF),
            pltpu.VMEM((4, 2, 2, 2, 32, 256), BF),
            pltpu.VMEM((2, 8, 896), F32),
            pltpu.VMEM((2, 8, 3200), F32),
            dma((4,)),
            dma,
            dma((3,)),
            dma((3,)),
            dma((3,)),
            dma((3,)),
            dma((4,)),
            dma((4,)),
            dma((4,)),
            dma((4,)),
            dma((4,)),
            dma((4,)),
            dma((3,)),
            dma((3,)),
            pltpu.VMEM((32, 256), F32),
            pltpu.VMEM((32, 256), BF),
            dma((n, 3, 4)),
            dma((n, 3, 4)),
            dma((n, 4, 3)),
            dma((n, 4, 3)),
            dma((n,)),
        ],
        compiler_params=pltpu.CompilerParams(
            collective_id=2 if first else 0,
            has_side_effects=True,
            vmem_limit_bytes=60 * 1024 * 1024,
        ),
        name="forward_first" if first else "forward_second",
    )(hidden, lengths, *known, *shards)


def backward_kernel(layer, *refs):
    dy, rows, up, before2, before1, qb, kvb, logs, att, lens, wj, wu, wd = refs[:13]
    dh_out, dj_out, db_out, du_out, df_out, vec_out = refs[13:19]
    vj, vu, vd, das, dab, dkv, rx, ry, rl, py, dq, sb, dj = refs[19:32]
    wsem, asend, arecv, csend, crecv, jsend, jrecv = refs[32:]
    rows = rows.at[layer]
    me = my_place()
    x, c = me["x"], me["c"]
    yh = me["y"] // 2
    partner, across = peer_of(me, "c", 1), peer_of(me, "y", 2)
    loads = []
    for q in range(4):
        at = slice(768 * q, 768 * q + 768)
        for a, b in ((wd.at[at], vd.at[at]), (wu.at[:, at], vu.at[:, at])):
            loads.append(pltpu.make_async_copy(a, b, wsem.at[len(loads)]))
    loads.append(pltpu.make_async_copy(wj, vj, wsem.at[8]))
    for copy in loads:
        copy.start()
    greet_sequence(me)
    sends = []

    def send(src, dst, s, r, place):
        copy = remote(src, dst, s, r, place)
        copy.start()
        sends.append(copy)

    def arrived(slot, s, r, place):
        remote(slot, slot, s, r, place).wait_recv()

    def column_sum(a):
        return jnp.sum(a.astype(F32), axis=0, keepdims=True)

    vec_out[...] = jnp.zeros_like(vec_out)
    d_second, gain_grad, shift_grad = norm_backward(before2[...], rows[6:7], dy[...])
    vec_out[6:7] = gain_grad
    vec_out[7:8] = shift_grad
    df = d_second.astype(BF)
    df_out[...] = df
    vec_out[5:6] = column_sum(df)
    d_first = d_second
    for q in range(4):
        loads[2 * q].wait()
        loads[2 * q + 1].wait()
        at = slice(768 * q, 768 * q + 768)
        u = up[:, at]
        slope = normal_cdf(u) + u * (0.3989422804014327 * jnp.exp(-0.5 * u * u))
        du = (mxu(df, vd[at, :], FAR) * slope).astype(BF)
        du_out[:, at] = du
        vec_out[8 + q : 9 + q] = column_sum(du)
        d_first = d_first + mxu(du, vu[:, at], FAR)
    d_sum, gain_grad, shift_grad = norm_backward(before1[...], rows[3:4], d_first)
    vec_out[3:4] = gain_grad
    vec_out[4:5] = shift_grad
    db = d_sum.astype(BF)
    db_out[...] = db
    vec_out[2:3] = column_sum(db)
    dh_out[...] = d_sum
    loads[8].wait()
    da = mxu(db, vj[:, 2304:3072], FAR).T.astype(BF)
    for g in range(4):
        das[g] = da[192 * g : 192 * g + 192]
    dab[x] = das[x]
    for s in (2, 1, 3):
        peer = peer_of(me, "x", s)
        send(das.at[peer["x"]], dab.at[x], asend.at[s - 1], arecv.at[s - 1], peer)
    for s in (1, 3, 2):
        source = peer_of(me, "x", 4 - s)
        arrived(dab.at[source["x"]], asend.at[s - 1], arecv.at[s - 1], source)
    length = lens[0]

    def by_head(ref, n):
        return jnp.concatenate([ref[xs, 64 * n : 64 * n + 64] for xs in range(4)], axis=1)

    inner = []
    for n in range(3):
        dq[n] = jnp.zeros((64, 512), F32)
        inner.append(
            jnp.sum(
                by_head(dab, n).astype(F32) * att[64 * n : 64 * n + 64, :], axis=0, keepdims=True
            )
        )

    def half(which, base):
        def step(i, carry):
            core, xs = i // 4, i % 4
            b = base + core
            bias = key_bias(length, b, xs)
            bias = jnp.concatenate([bias] * 2, axis=1)
            for n in range(3):
                own = slice(64 * n, 64 * n + 64)
                keys = kvb[b, xs, own, :]
                values = kvb[b, xs, slice(192 + 64 * n, 256 + 64 * n), :]
                dk = dv = None
                for h in range(2):
                    at = slice(256 * h, 256 * h + 256)
                    q_n = jnp.concatenate([qb[2 * h, own], qb[2 * h + 1, own]], axis=1)
                    da_n = jnp.concatenate([dab[2 * h, own], dab[2 * h + 1, own]], axis=1)
                    p = jnp.exp(mxu(keys, q_n, NEAR) + bias - logs[n : n + 1, at])
                    dp = mxu(values, da_n, NEAR)
                    ds = (p * (dp - inner[n][:, at])).astype(BF)
                    dq[n, :, at] += mxu(keys, ds)
                    k_term = mxu(q_n, ds, FAR)
                    v_term = mxu(da_n, p.astype(BF), FAR)
                    dk = k_term if dk is None else dk + k_term
                    dv = v_term if dv is None else dv + v_term
                dkv[which, core, xs, 64 * n : 64 * n + 64, :] = dk.astype(BF)
                dkv[which, core, xs, 192 + 64 * n : 256 + 64 * n, :] = dv.astype(BF)
            return carry

        lax.fori_loop(0, 8, step, 0)

    half(0, (1 - yh) * 2)
    send(dkv.at[0, 1 - c], rx, csend.at[0], crecv.at[0], partner)
    arrived(rx, csend.at[0], crecv.at[0], partner)
    for xs in range(4):
        py[xs] = (dkv[0, c, xs].astype(F32) + rx[xs].astype(F32)).astype(BF)
    send(py, ry, csend.at[1], crecv.at[1], across)
    half(1, yh * 2)
    send(dkv.at[1, 1 - c], rl, csend.at[2], crecv.at[2], partner)
    for xs in range(4):
        for n in range(3):
            part = dq[n, :, 128 * xs : 128 * xs + 128] * 0.125
            sb[xs, 64 * n : 64 * n + 64, :] = part.astype(BF)
    arrived(rl, csend.at[2], crecv.at[2], partner)
    arrived(ry, csend.at[1], crecv.at[1], across)
    for xs in range(4):
        total = dkv[1, c, xs].astype(F32) + rl[xs].astype(F32) + ry[xs].astype(F32)
        sb[xs, 192:576, :] = total.astype(BF)
    dj[x] = sb[x]
    for s in (2, 1, 3):
        peer = peer_of(me, "x", s)
        send(sb.at[peer["x"]], dj.at[x], jsend.at[s - 1], jrecv.at[s - 1], peer)
    for s in (1, 3, 2):
        source = peer_of(me, "x", 4 - s)
        arrived(dj.at[source["x"]], jsend.at[s - 1], jrecv.at[s - 1], source)
    dh = dh_out[...]
    for j in range(3):
        at = slice(768 * j, 768 * j + 768)
        t = jnp.concatenate([dj[g, 192 * j : 192 * j + 192] for g in range(4)], axis=0)
        t = t.astype(F32).T.astype(BF)
        dj_out[:, at] = t
        if j != 1:
            row = 0 if j == 0 else 1
            vec_out[row : row + 1] = column_sum(t)
        dh = dh + mxu(t, vj[:, at], FAR)
    dh_out[...] = dh
    for copy in sends:
        copy.wait_send()


def backward_layer(layer, dy, rows, up, before2, before1, q, kv, logs, att, lengths, wj, wu, wd):
    vmem = pl.BlockSpec(memory_space=pltpu.VMEM)
    anyspace = pl.BlockSpec(memory_space=pl.ANY)
    dma = pltpu.SemaphoreType.DMA
    out = jax.ShapeDtypeStruct
    return pl.pallas_call(
        functools.partial(backward_kernel, layer),
        out_shape=[
            out((128, 768), F32),
            out((128, 2304), BF),
            out((128, 768), BF),
            out((128, 3072), BF),
            out((128, 768), BF),
            out((16, 768), F32),
        ],
        in_specs=[vmem] * 9 + [pl.BlockSpec(memory_space=pltpu.SMEM)] + [anyspace] * 3,
        out_specs=[vmem] * 6,
        scratch_shapes=[
            pltpu.VMEM((768, 3072), BF),
            pltpu.VMEM((768, 3072), BF),
            pltpu.VMEM((3072, 768), BF),
            pltpu.VMEM((4, 192, 128), BF),
            pltpu.VMEM((4, 192, 128), BF),
            pltpu.VMEM((2, 2, 4, 384, 128), BF),
            pltpu.VMEM((4, 384, 128), BF),
            pltpu.VMEM((4, 384, 128), BF),
            pltpu.VMEM((4, 384, 128), BF),
            pltpu.VMEM((4, 384, 128), BF),
            pltpu.VMEM((3, 64, 512), F32),
            pltpu.VMEM((4, 576, 128), BF),
            pltpu.VMEM((4, 576, 128), BF),
            dma((9,)),
            dma((3,)),
            dma((3,)),
            dma((3,)),
            dma((3,)),
            dma((3,)),
            dma((3,)),
        ],
        compiler_params=pltpu.CompilerParams(
            collective_id=3 + layer, has_side_effects=True, vmem_limit_bytes=60 * 1024 * 1024
        ),
        name="backward_layer",
    )(dy, rows, up, before2, before1, q, kv, logs, att, lengths, wj, wu, wd)


def body(
    inputs,
    lengths,
    joint_weight,
    query_bias,
    value_bias,
    output_weight,
    output_bias,
    first_gain,
    first_shift,
    up_weight,
    up_bias,
    down_weight,
    down_bias,
    second_gain,
    second_shift,
    cotangent,
):
    small = (
        query_bias,
        value_bias,
        output_bias,
        first_gain,
        first_shift,
        down_bias,
        second_gain,
        second_shift,
        up_bias,
    )
    joint_and_out = jnp.concatenate([joint_weight, output_weight], axis=-1)
    hidden0 = inputs.reshape(128, 768)
    got = forward_layer(
        True,
        hidden0,
        lengths,
        small,
        (up_weight, down_weight, joint_and_out),
    )
    rows_all, up_adds, up0, down0, joint0, joint1 = got[11:]
    more = forward_layer(
        False, got[0], lengths, (rows_all, up_adds, joint1), (up_weight, down_weight)
    )
    up1, down1 = more[11:]
    weights_of = [
        (j.reshape(768, 3072), u.reshape(768, 3072), d.reshape(3072, 768))
        for j, u, d in ((joint0, up0, down0), (joint1, up1, down1))
    ]
    kept = [(hidden0, *got[1:11]), (got[0], *more[1:11])]
    outputs = [got[0].reshape(1, 128, 768), more[0].reshape(1, 128, 768)]
    grad_rows = cotangent.reshape(128, 768).astype(F32)
    layer_grads = [None] * LAYERS
    vector_grads = [None] * LAYERS
    for l in reversed(range(LAYERS)):
        hidden, q, kv, logs, att, mixed, before1, low, up, acts, before2 = kept[l]
        grad_rows, d_joint, d_branch, d_up, d_down, vector_grads[l] = backward_layer(
            l, grad_rows, rows_all, up, before2, before1, q, kv, logs, att, lengths, *weights_of[l]
        )
        layer_grads[l] = (hidden, mixed, low, acts, d_joint, d_branch, d_up, d_down)
    vectors = jnp.concatenate(vector_grads)
    joint_grad, out_grad, up_grad, down_grad, vectors = reduce_grads(layer_grads, vectors)
    vectors = vectors.reshape(LAYERS, 16, 768)
    owner = lax.axis_index("batch") * 4 + lax.axis_index("blk")
    own_rows = lax.dynamic_slice_in_dim(vectors[:, :8], owner * 24, 24, axis=2)
    own_up = lax.dynamic_slice_in_dim(vectors[:, 8:12].reshape(LAYERS, 3072), owner * 96, 96, axis=1)
    stacked = (
        joint_grad,
        own_rows[:, 0],
        own_rows[:, 1],
        out_grad,
        own_rows[:, 2],
        own_rows[:, 3],
        own_rows[:, 4],
        up_grad,
        own_up,
        down_grad,
        own_rows[:, 5],
        own_rows[:, 6],
        own_rows[:, 7],
    )
    activations = jnp.stack(outputs)
    input_grad = grad_rows.reshape(1, 128, 768)
    return (
        activations,
        input_grad,
        stacked[0],
        stacked[1],
        stacked[2],
        stacked[3],
        stacked[4],
        stacked[5],
        stacked[6],
        stacked[7],
        stacked[8],
        stacked[9],
        stacked[10],
        stacked[11],
        stacked[12],
    )


def solution(mesh):
    placed = (
        P("batch", ("head", "blk"), None),
        P("batch"),
        P(None, ("batch", "blk"), None),
        P(None, ("batch", "blk")),
        P(None, ("batch", "blk")),
        P(None, ("batch", "blk"), None),
        P(None, ("batch", "blk")),
        P(None, ("batch", "blk")),
        P(None, ("batch", "blk")),
        P(None, ("batch", "blk"), None),
        P(None, ("batch", "blk")),
        P(None, ("batch", "blk"), None),
        P(None, ("batch", "blk")),
        P(None, ("batch", "blk")),
        P(None, ("batch", "blk")),
        P("batch", ("head", "blk"), None),
    )
    return jax.shard_map(
        body,
        mesh=mesh,
        in_specs=placed,
        out_specs=(
            P(None, "batch", ("head", "blk"), None),
            P("batch", ("head", "blk"), None),
            P(None, ("batch", "blk"), None),
            P(None, ("batch", "blk")),
            P(None, ("batch", "blk")),
            P(None, ("batch", "blk"), None),
            P(None, ("batch", "blk")),
            P(None, ("batch", "blk")),
            P(None, ("batch", "blk")),
            P(None, ("batch", "blk"), None),
            P(None, ("batch", "blk")),
            P(None, ("batch", "blk"), None),
            P(None, ("batch", "blk")),
            P(None, ("batch", "blk")),
            P(None, ("batch", "blk")),
        ),
        check_vma=False,
    )
```

```python
import functools

import jax
import jax.numpy as jnp
from jax import lax
from jax.experimental import pallas as pl
from jax.experimental.pallas import tpu as pltpu
from jax.sharding import PartitionSpec as P

LAYERS = 2


EPSILON = 1e-12
MASKED = -1e30


MESH = pl.DeviceIdType.MESH
ALL = slice(None)


def my_place():
    b, x, k = lax.axis_index("batch"), lax.axis_index("head"), lax.axis_index("blk")
    return {"z": b // 2, "y": (k // 2) * 2 + b % 2, "x": x, "c": k % 2}


def device_of(place):
    return (
        place["z"] * 2 + place["y"] % 2,
        place["x"],
        (place["y"] // 2) * 2 + place["c"],
    )


def peer_of(place, axis, step):
    other = dict(place)
    other[axis] = (place[axis] + step) % (2 if axis == "c" else 4)
    return other


def greet_all(place):
    barrier = pltpu.get_barrier_semaphore()
    peers = [peer_of(place, a, s) for a in ("x", "y", "z") for s in (1, 2, 3)]
    peers.append(peer_of(place, "c", 1))
    for p in peers:
        pl.semaphore_signal(barrier, inc=1, device_id=device_of(p), device_id_type=MESH)
    pl.semaphore_wait(barrier, len(peers))


def remote(src, dst, send, recv, place):
    return pltpu.make_async_remote_copy(
        src_ref=src,
        dst_ref=dst,
        send_sem=send,
        recv_sem=recv,
        device_id=device_of(place),
        device_id_type=MESH,
    )


class Gather:
    def __init__(self, me, pieces, ins, outs, sems):
        self.me, self.pieces, self.ins, self.outs = me, pieces, ins, outs
        self.send, self.recv, self.fsend, self.frecv, self.local = sems
        self.partner = peer_of(me, "c", 1)
        self.started, self.locals = [], {}

    def order(self, i):
        return self.pieces[i][3]

    def direct(self, i, phase):
        return phase in self.pieces[i][5]

    def region(self, i, phase, place, half=None):
        array, start, width, order, by_rows, _ = self.pieces[i]
        done = order[:phase]
        z = ALL if "z" in done else place["z"]
        y = (ALL, ALL) if "y" in done else (place["y"] % 2, place["y"] // 2)
        lines = ALL
        if "x" in order and "x" not in done:
            width = width // 4
            start = start + place["x"] * width
        if half is not None:
            if by_rows:
                count = self.outs[array].shape[-2] // 2
                lines = pl.ds(count * half, count)
            else:
                width = width // 2
                start = start + half * width
        columns = self.columns(array, start, width)
        return self.outs[array].at[z, y[0], y[1], place["c"], lines, columns]

    def columns(self, array, start, width):
        if width == self.outs[array].shape[-1]:
            return ALL
        return pl.ds(start if isinstance(start, int) else pl.multiple_of(start, 128), width)

    def own(self, i):
        array, start, width, order, _, _ = self.pieces[i]
        if "x" in order:
            width = width // 4
            start = start + self.me["x"] * width
        columns = self.columns(array, start, width)
        return self.ins[array].at[ALL, columns]

    def copy(self, src, dst, s, r, place):
        copy = remote(src, dst, s, r, place)
        copy.start()
        self.started.append(copy)

    def near(self, i, phase):
        axis = self.order(i)[phase]
        return peer_of(self.me, axis, 1), peer_of(self.me, axis, 3), peer_of(self.me, axis, 2)

    def start(self, i, phase):
        right, left, opposite = self.near(i, phase)
        dst = self.region(i, phase, self.me)
        if phase == 0:
            copy = pltpu.make_async_copy(self.own(i), dst, self.local.at[i])
            copy.start()
            self.locals[i] = copy
        src = self.own(i) if phase == 0 else dst
        places = [(0, right), (1, left)]
        if self.direct(i, phase):
            places = [(2, opposite)] + places
        for j, place in places:
            self.copy(src, dst, self.send.at[i, phase, j], self.recv.at[i, phase, j], place)
        if phase == 0:
            self.copy(src, dst, self.fsend.at[i, 3, 0], self.frecv.at[i, 3, 0], self.partner)

    def arrived(self, slot, i, phase, j, place):
        remote(
            slot, slot, self.send.at[i, phase, j], self.recv.at[i, phase, j], place
        ).wait_recv()

    def pass_on(self, i, phase, j, place):
        slot = self.region(i, phase, place)
        self.copy(
            slot, slot, self.fsend.at[i, phase, j], self.frecv.at[i, phase, j], self.partner
        )

    def relay(self, i, phase):
        right, left, _ = self.near(i, phase)
        for j, source, target in ((0, left, right), (1, right, left)):
            self.arrived(self.region(i, phase, source), i, phase, j, source)
            if not self.direct(i, phase):
                part = self.region(i, phase, source, j)
                self.copy(
                    part, part, self.send.at[i, phase, 2 + j], self.recv.at[i, phase, 2 + j], target
                )
            self.pass_on(i, phase, j, source)

    def close(self, i, phase):
        right, left, opposite = self.near(i, phase)
        if self.direct(i, phase):
            self.arrived(self.region(i, phase, opposite), i, phase, 2, opposite)
        else:
            for j, source in ((0, left), (1, right)):
                self.arrived(self.region(i, phase, opposite, j), i, phase, 2 + j, source)
        self.pass_on(i, phase, 2, opposite)
        if phase == 0:
            self.locals[i].wait()

    def complete(self, i):
        slots = [((3, 0), self.region(i, 0, self.partner))]
        for phase, axis in enumerate(self.order(i)):
            for j, s in ((0, 3), (1, 1), (2, 2)):
                slots.append(((phase, j), self.region(i, phase, peer_of(self.partner, axis, s))))
        for at, slot in slots:
            remote(
                slot, slot, self.fsend.at[i, *at], self.frecv.at[i, *at], self.partner
            ).wait_recv()

    def end(self):
        for copy in self.started:
            copy.wait_send()


    def relay_all(self, phase, *group):
        for i in group:
            self.relay(i, phase)

    def close_all(self, phase, *group):
        for i in group:
            self.close(i, phase)
            if phase + 1 < len(self.order(i)):
                self.start(i, phase + 1)


def joint_pieces(array, direct):
    return (
        (array, 0, 1536, ("y", "z"), False, direct),
        (array, 1536, 1536, ("z", "y"), False, direct),
    )


def feed_pieces(array, order, direct):
    return (
        (array, 0, 3072, order, False, direct),
        (array + 1, 0, 384, ("y", "z"), True, direct),
        (array + 1, 384, 384, ("y", "z"), True, direct),
    )


NEVER = ()
FIRST_PIECES = (
    feed_pieces(0, ("y", "z", "x"), NEVER)
    + joint_pieces(2, NEVER)
    + joint_pieces(3, NEVER)
    + ((4, 0, 256, ("y", "z"), True, NEVER),)
)
SECOND_PIECES = feed_pieces(0, ("y", "z", "x"), NEVER)


THIRDS = (("x", "y", "z"), ("y", "z", "x"), ("z", "x", "y"))


class Reducer:
    low_half, high_half = pl.ds(0, 2), pl.ds(2, 2)

    def __init__(self, me, ins, bufs, s2, sems):
        self.me, self.ins, self.s2 = me, ins, s2
        self.lhs, self.rhs, self.g, self.o1, self.r1, self.s1, self.o2, self.r2 = bufs
        self.csend, self.crecv, self.lsem, self.qs, self.qr = sems
        self.sends = []

    def exchange(self):
        me, c = self.me, self.me["c"]
        partner = peer_of(me, "c", 1)
        half = pl.ds(pl.multiple_of(c * 128, 128), 128)
        lhs_in, rhs_in = self.ins[0], self.ins[1:]
        dst = self.lhs.at[ALL, half]
        self.away = [remote(lhs_in.at[1 - c], dst, self.csend.at[0], self.crecv.at[0], partner)]
        self.here = [pltpu.make_async_copy(lhs_in.at[c], dst, self.lsem.at[0])]
        starts, widths = (0, 3072, 3840, 6144), (3072, 768, 2304, 768)
        for j in range(4):
            dst = self.rhs.at[half, pl.ds(starts[j], widths[j])]
            self.away.append(
                remote(rhs_in[j], dst, self.csend.at[j + 1], self.crecv.at[j + 1], partner)
            )
            self.here.append(pltpu.make_async_copy(rhs_in[j], dst, self.lsem.at[j + 1]))
        for copy in self.away + self.here:
            copy.start()

    def exchanged(self):
        for copy in self.here:
            copy.wait()
        for copy in self.away:
            copy.wait_recv()

    def products(self, t):
        for q in range(4):
            unit = (0, 1 + q, 5 if q < 3 else 6)[t]
            col = (q * 768, 3072, 3840 + q * 768)[t]
            block = jnp.dot(
                self.lhs[384 * unit : 384 * unit + 384, :],
                self.rhs[:, col : col + 768],
                preferred_element_type=jnp.float32,
            )
            for i in range(16):
                z, y = i // 4, (i % 2) * 2 + (i // 2) % 2
                at = ((q, y, z), (y, z, q), (z, q, y))[t]
                part = block[24 * i : 24 * i + 24]
                self.g[t, at[0], at[1], at[2]] = part.astype(jnp.bfloat16)
        self.start(0, t)

    def copy(self, phase, t, j, src, dst, peer):
        copy = remote(src, dst, self.qs.at[phase, t, j], self.qr.at[phase, t, j], peer)
        copy.start()
        self.sends.append(copy)

    def wait(self, phase, t, j, slot, peer):
        remote(slot, slot, self.qs.at[phase, t, j], self.qr.at[phase, t, j], peer).wait_recv()

    def refs(self, phase, t):
        axis = THIRDS[t][phase]
        places = [peer_of(self.me, axis, s) for s in (1, 3, 2)]
        held, over, got = (
            (self.g, self.o1, self.r1),
            (self.s1, self.o2, self.r2),
        )[phase]
        return axis, places, held.at[t], over.at[t], got.at[t]

    def start(self, phase, t):
        axis, (right, left, far), held, over, got = self.refs(phase, t)
        low, high = self.low_half, self.high_half
        self.copy(phase, t, 0, held.at[far[axis], low], over.at[0], right)
        self.copy(phase, t, 1, held.at[far[axis], high], over.at[1], left)
        self.copy(phase, t, 2, held.at[right[axis], high], got.at[0, high], right)
        self.copy(phase, t, 3, held.at[left[axis], low], got.at[1, low], left)

    def middle(self, phase, t):
        axis, (right, left, far), held, over, got = self.refs(phase, t)
        f32 = jnp.float32
        for j, source, target in ((0, left, right), (1, right, left)):
            self.wait(phase, t, j, over.at[j], source)
            at = target[axis]
            for a in range(2):
                if phase == 0:

                    def merge(b, carry, a=a, j=j, at=at):
                        total = held[at, 2 * j + a, b].astype(f32) + over[j, a, b].astype(f32)
                        held[at, 2 * j + a, b] = total.astype(jnp.bfloat16)
                        return carry

                    lax.fori_loop(0, 4, merge, 0)
                else:
                    total = held[at, 2 * j + a].astype(f32) + over[j, a].astype(f32)
                    held[at, 2 * j + a] = total.astype(jnp.bfloat16)
            part = (self.low_half, self.high_half)[j]
            self.copy(phase, t, 4 + j, held.at[at, part], got.at[j, part], target)

    def finish(self, phase, t):
        axis, (right, left, far), held, over, got = self.refs(phase, t)
        low, high = self.low_half, self.high_half
        self.wait(phase, t, 2, got.at[0, high], left)
        self.wait(phase, t, 3, got.at[1, low], right)
        self.wait(phase, t, 4, got.at[0, low], left)
        self.wait(phase, t, 5, got.at[1, high], right)
        mine = self.me[axis]
        f32 = jnp.float32
        if phase == 0:

            def add(i, carry):
                a, b = i // 4, i % 4
                total = held[mine, a, b].astype(f32)
                for s in range(2):
                    total = total + got[s, a, b].astype(f32)
                self.s1[t, a, b] = total.astype(jnp.bfloat16)
                return carry

            lax.fori_loop(0, 16, add, 0)
            self.start(1, t)
        else:
            for a in range(4):
                total = held[mine, a].astype(f32)
                for s in range(2):
                    total = total + got[s, a].astype(f32)
                self.s2[t, a] = total.astype(jnp.bfloat16)

    def end(self):
        for copy in self.sends + self.away:
            copy.wait_send()


def reducer_buffers():
    bf = jnp.bfloat16
    return [
        pltpu.VMEM((2688, 256), bf),
        pltpu.VMEM((256, 6912), bf),
        pltpu.VMEM((3, 4, 4, 4, 24, 768), bf),
        pltpu.VMEM((3, 2, 2, 4, 24, 768), bf),
        pltpu.VMEM((3, 2, 4, 4, 24, 768), bf),
        pltpu.VMEM((3, 4, 4, 24, 768), bf),
        pltpu.VMEM((3, 2, 2, 24, 768), bf),
        pltpu.VMEM((3, 2, 4, 24, 768), bf),
    ]


def reducer_semaphores():
    dma = pltpu.SemaphoreType.DMA
    return [dma((5,)), dma((5,)), dma((5,)), dma((2, 3, 6)), dma((2, 3, 6))]


def reduce_kernel(*refs):
    s2_in, vec_in = refs[5:7]
    joint_out, out_out, up_out, down_out, vec_out = refs[7:12]
    s2, r3, last, vc, va = refs[20:25]
    ps, pr, vs, vr = refs[30:]
    me = my_place()
    layers = (1, 0)
    f32 = jnp.float32
    reducer = Reducer(me, refs[:5], refs[12:20], s2.at[0], refs[25:30])
    greet_all(me)
    reducer.exchange()

    vec_axes = ("c", "x", "y", "z")
    vec_sends = []

    def vec_slot(phase, place):
        if phase == 0:
            return vc.at[place["c"]]
        return va.at[phase - 1, place[vec_axes[phase]]]

    def vec_start(phase, value):
        vec_slot(phase, me)[...] = value.astype(jnp.bfloat16)
        for s in range(1, 2 if phase == 0 else 4):
            copy = remote(
                vec_slot(phase, me),
                vec_slot(phase, me),
                vs.at[phase, s - 1],
                vr.at[phase, s - 1],
                peer_of(me, vec_axes[phase], s),
            )
            copy.start()
            vec_sends.append(copy)

    def vec_finish(phase):
        count = 2 if phase == 0 else 4
        for s in range(1, count):
            src = peer_of(me, vec_axes[phase], count - s)
            slot = vec_slot(phase, src)
            remote(slot, slot, vs.at[phase, s - 1], vr.at[phase, s - 1], src).wait_recv()
        total = None
        for j in range(count):
            part = (vc[j] if phase == 0 else va[phase - 1, j]).astype(jnp.float32)
            total = part if total is None else total + part
        return total

    vec_start(0, vec_in[...])

    sends = []

    def send_chunks(phase, t, l, source, target):
        axis = THIRDS[t][phase] if phase < 3 else "x"
        for s in (2, 1, 3):
            peer = peer_of(me, axis, s)
            copy = remote(
                source(peer[axis]),
                target(s),
                ps.at[phase, t, l, s - 1],
                pr.at[phase, t, l, s - 1],
                peer,
            )
            copy.start()
            sends.append(copy)

    def await_chunks(phase, t, l, target):
        axis = THIRDS[t][phase] if phase < 3 else "x"
        for s in (1, 3, 2):
            slot = target(s)
            remote(
                slot,
                slot,
                ps.at[phase, t, l, s - 1],
                pr.at[phase, t, l, s - 1],
                peer_of(me, axis, s),
            ).wait_recv()

    def third_phase(l, t):
        send_chunks(2, t, l, lambda a: s2.at[l, t, a], lambda s: r3.at[t, l, s - 1])

    s2[1] = s2_in[...]
    for t in range(3):
        third_phase(1, t)
    reducer.exchanged()
    for t in range(3):
        reducer.products(t)
    vec_start(1, vec_finish(0))
    for t in range(3):
        reducer.middle(0, t)
    for t in range(3):
        reducer.finish(0, t)
    vec_start(2, vec_finish(1))
    for t in range(3):
        reducer.middle(1, t)
    for t in range(3):
        reducer.finish(1, t)
        third_phase(0, t)
    vec_start(3, vec_finish(2))
    for l in layers:
        for t in range(3):
            mine = me[THIRDS[t][2]]
            await_chunks(2, t, l, lambda s, t=t, l=l: r3.at[t, l, s - 1])
            total = s2[l, t, mine].astype(f32)
            for s in range(3):
                total = total + r3[t, l, s].astype(f32)
            last[t, l, me["x"]] = total.astype(jnp.bfloat16)
            send_chunks(
                3,
                t,
                l,
                lambda a, t=t, l=l: last.at[t, l, me["x"]],
                lambda s, t=t, l=l: last.at[t, l, me["x"]],
            )
    vec_out[...] = vec_finish(3)
    for l in layers:
        for t in range(3):
            await_chunks(3, t, l, lambda s, t=t, l=l: last.at[t, l, (me["x"] + 4 - s) % 4])
            for q in range(4):
                part = last[t, l, q].astype(f32)
                if t == 0:
                    up_out[l, :, 768 * q : 768 * q + 768] = part
                elif t == 1:
                    down_out[l, 24 * q : 24 * q + 24, :] = part
                elif q < 3:
                    joint_out[l, :, 768 * q : 768 * q + 768] = part
                else:
                    out_out[l] = part
    reducer.end()
    for copy in sends + vec_sends:
        copy.wait_send()


def for_owner_cores(array):
    tokens, width = array.shape
    n = width // 768
    t = array.T.reshape(16, 2, n, 24, tokens).transpose(1, 2, 0, 3, 4)
    return t.reshape(2, n * 384, tokens)


def reducer_operands(hidden, mixed, first, acts, d_joint, d_branch, d_up, d_down):
    lhs = jnp.concatenate([for_owner_cores(a) for a in (first, acts, hidden, mixed)], axis=1)
    return lhs, d_up, d_down, d_joint, d_branch


def reduce_grads(operands, later, vectors):
    anyspace = pl.BlockSpec(memory_space=pl.ANY)
    vmem = pl.BlockSpec(memory_space=pltpu.VMEM)
    bf, dma = jnp.bfloat16, pltpu.SemaphoreType.DMA
    return pl.pallas_call(
        reduce_kernel,
        out_shape=[
            jax.ShapeDtypeStruct((2, 24, 2304), jnp.float32),
            jax.ShapeDtypeStruct((2, 24, 768), jnp.float32),
            jax.ShapeDtypeStruct((2, 24, 3072), jnp.float32),
            jax.ShapeDtypeStruct((2, 96, 768), jnp.float32),
            jax.ShapeDtypeStruct((32, 768), jnp.float32),
        ],
        in_specs=[anyspace] * 5 + [vmem] * 2,
        out_specs=[vmem] * 5,
        scratch_shapes=reducer_buffers()
        + [
            pltpu.VMEM((2, 3, 4, 24, 768), bf),
            pltpu.VMEM((3, 2, 3, 24, 768), bf),
            pltpu.VMEM((3, 2, 4, 24, 768), bf),
            pltpu.VMEM((2, 32, 768), bf),
            pltpu.VMEM((3, 4, 32, 768), bf),
        ]
        + reducer_semaphores()
        + [dma((4, 3, 2, 3)), dma((4, 3, 2, 3)), dma((4, 3)), dma((4, 3))],
        compiler_params=pltpu.CompilerParams(
            collective_id=1, has_side_effects=True, vmem_limit_bytes=60 * 1024 * 1024
        ),
        name="reduce_grads",
    )(*operands, later, vectors)


FAR = (((1,), (1,)), ((), ()))
NEAR = (((0,), (0,)), ((), ()))
F32 = jnp.float32
BF = jnp.bfloat16
KEYS = 128


def mxu(a, b, dims=None):
    if dims is None:
        return jnp.dot(a, b, preferred_element_type=F32)
    return lax.dot_general(a, b, dims, preferred_element_type=F32)


def normalized(values):
    average = jnp.mean(values, axis=-1, keepdims=True)
    centered = values - average
    variance = jnp.mean(centered * centered, axis=-1, keepdims=True)
    r = lax.rsqrt(variance + EPSILON)
    return centered * r, r


def norm_backward(values, gain, grad):
    xhat, r = normalized(values)
    g = grad * gain
    back = r * (
        g - jnp.mean(g, axis=-1, keepdims=True) - xhat * jnp.mean(g * xhat, axis=-1, keepdims=True)
    )
    gain_grad = jnp.sum(grad * xhat, axis=0, keepdims=True)
    return back, gain_grad, jnp.sum(grad, axis=0, keepdims=True)


def normal_cdf(u):
    return 0.5 * (1.0 + lax.erf(u * 0.7071067811865476))


def greet_sequence(me):
    barrier = pltpu.get_barrier_semaphore()
    peers = [peer_of(me, "x", s) for s in (1, 2, 3)]
    peers += [peer_of(me, "c", 1), peer_of(me, "y", 2)]
    for p in peers:
        pl.semaphore_signal(barrier, inc=1, device_id=device_of(p), device_id_type=MESH)
    pl.semaphore_wait(barrier, len(peers))


def key_bias(length, block, xs):
    limit = length - xs * 512 - block * 128
    rows = lax.broadcasted_iota(jnp.int32, (KEYS, 128), 0)
    return jnp.where(rows < limit, 0.0, MASKED)


def forward_kernel(first, *refs):
    refs = list(refs)

    def take(count):
        out = refs[:count]
        del refs[:count]
        return out

    hid, lens = take(2)
    if first:
        small_in = take(9)
        up, down, joint_in = take(3)
        shards = [up.at[0], down.at[0], joint_in.at[0], joint_in.at[1]]
    else:
        rows, up_add, wj = take(3)
        up, down = take(2)
        shards = [up.at[1], down.at[1]]
    res, q_out, kv_out, log_out, att_out, mixed_out = take(6)
    before1_out, low_out, up_out, act_out, before2_out = take(5)
    if first:
        rows_out, add_out = take(2)
    gathered = take(4 if first else 2)
    vj, vu, vd, qs, qb, kvb, sc, acc, back, ab, vv, rsum, usum = take(13)
    wsem, osem, qsend, qrecv, xsend, xrecv, csend, crecv, ysend, yrecv, fsend, frecv = take(12)
    bsend, brecv = take(2)
    flat, own_small = take(2)
    me = my_place()
    if first:
        shards.append(own_small)
    lands = [vu, vd, vj, gathered[3], vv] if first else [vu, vd]
    plan = Gather(me, FIRST_PIECES if first else SECOND_PIECES, shards, lands, refs)
    feed, joint, later, small = (0, 1, 2), (3, 4), (5, 6), (7,)
    x, c = me["x"], me["c"]
    yh = me["y"] // 2
    k = yh * 2 + c
    partner, across = peer_of(me, "c", 1), peer_of(me, "y", 2)
    k_partner = yh * 2 + 1 - c
    k_across = (1 - yh) * 2 + c
    k_diag = (1 - yh) * 2 + 1 - c
    greet_all(me)
    loads = []

    def load(src, dst):
        copy = pltpu.make_async_copy(src, dst, wsem.at[len(loads)])
        copy.start()
        loads.append(copy)

    if first:
        flat[...] = jnp.zeros_like(flat)
        for j in range(9):
            for l in range(2):
                flat[16 * l + j : 16 * l + j + 1, 0 : small_in[j].shape[1]] = small_in[j][
                    l : l + 1, :
                ].astype(F32)
        owner = lax.axis_index("batch") * 4 + lax.axis_index("blk")
        lines = lax.broadcasted_iota(jnp.int32, (32, 256), 0) % 16
        moved = pltpu.roll(flat[...], (owner * 24) % 128, axis=1)
        moved_up = pltpu.roll(flat[...], (owner * 96) % 128, axis=1)
        own_small[...] = jnp.where(lines == 8, moved_up, moved).astype(BF)
        for i in small + joint + feed:
            plan.start(i, 0)
        plan.relay_all(0, *small, *joint)
        plan.close_all(0, *small, *joint)
        plan.relay_all(0, *feed)
        plan.relay_all(1, *small, *joint)
        plan.close_all(0, *feed)
        plan.close_all(1, *small, *joint)
        for i in small + joint:
            plan.complete(i)
        load(vj, gathered[2])
        rsum[...] = jnp.zeros_like(rsum)
        usum[...] = jnp.zeros_like(usum)
        for o in range(32):
            z, yl, yh, core = o // 8, (o // 4) % 2, (o // 2) % 2, o % 2
            at, up_at = (24 * o) // 128 * 128, (96 * o) // 128 * 128
            for l in range(2):
                part = vv[z, yl, yh, core, 16 * l : 16 * l + 16, :].astype(F32)
                rsum[l, :, at : at + 256] += part[0:8]
                usum[l, 0:1, up_at : up_at + 256] += part[8:9]
        for l in range(2):
            rows_out[l] = rsum[l, :, 0:768]
            add_out[l] = usum[l, :, 0:3072]
        rows, up_add = rows_out.at[0], add_out.at[0]
    else:
        load(wj, vj)
        for i in feed:
            plan.start(i, 0)
        plan.relay_all(0, 0)
        plan.close_all(0, 0)
        rows, up_add = rows.at[1], up_add.at[1]

    def joint_columns(start):
        return vj[:, :, :, :, :, start : start + 768].reshape(768, 768)

    sends = []

    def send(src, dst, s, r, place):
        copy = remote(src, dst, s, r, place)
        copy.start()
        sends.append(copy)

    def arrived(slot, s, r, place):
        remote(slot, slot, s, r, place).wait_recv()

    if not first:
        loads[0].wait()
    for j in (1, 2, 0):
        p = mxu(hid[...], joint_columns(768 * j))
        if j == 0:
            p = p + rows[0:1]
        if j == 2:
            p = p + rows[1:2]
        p = p.astype(BF).astype(F32)
        if j == 0:
            p = p * 0.125
        p = p.T.astype(BF)
        for g in range(4):
            qs[g, 192 * j : 192 * j + 192] = p[192 * g : 192 * g + 192]
        if j == 2:
            kvb[k, x] = qs[x, 192:576]
            for s in (2, 1, 3):
                peer = peer_of(me, "x", s)
                send(
                    qs.at[peer["x"], 192:576], kvb.at[k, x], xsend.at[s - 1], xrecv.at[s - 1], peer
                )
            send(kvb.at[k, x], kvb.at[k, x], ysend.at[0], yrecv.at[0], across)
            send(kvb.at[k, x], kvb.at[k, x], csend.at[0], crecv.at[0], partner)
    qb[x] = qs[x, 0:192]
    for s in (2, 1, 3):
        peer = peer_of(me, "x", s)
        send(qs.at[peer["x"], 0:192], qb.at[x], qsend.at[s - 1], qrecv.at[s - 1], peer)
    if first:
        plan.relay_all(1, 0)
        plan.close_all(1, 0)
        for i in later:
            plan.start(i, 0)
    else:
        plan.relay_all(1, 0)
        plan.relay_all(0, 1, 2)
        plan.close_all(1, 0)
        plan.close_all(0, 1, 2)
    for s in (1, 3, 2):
        source = peer_of(me, "x", 4 - s)
        slot = kvb.at[k, source["x"]]
        arrived(slot, xsend.at[s - 1], xrecv.at[s - 1], source)
        send(slot, slot, ysend.at[s], yrecv.at[s], across)
        send(slot, slot, csend.at[s], crecv.at[s], partner)
    if first:
        plan.relay_all(1, 1, 2)
        plan.relay_all(0, *later)
    for s in (1, 3, 2):
        source = peer_of(me, "x", 4 - s)
        arrived(qb.at[source["x"]], qsend.at[s - 1], qrecv.at[s - 1], source)
    for s in (0, 1, 3, 2):
        arrived(kvb.at[k_partner, (x + 4 - s) % 4], csend.at[s], crecv.at[s], partner)

    length = lens[0]
    queries = [
        jnp.concatenate([qb[xs, 64 * n : 64 * n + 64] for xs in range(4)], axis=1)
        for n in range(3)
    ]

    def half(b0, b1, old):
        def scores(i, peaks):
            b = b0 + (b1 - b0) * (i // 4)
            xs = i % 4
            bias = key_bias(length, b, xs)
            bias = jnp.concatenate([bias] * 4, axis=1)
            new = []
            for n in range(3):
                keys = kvb[b, xs, 64 * n : 64 * n + 64, :]
                st = mxu(keys, queries[n], NEAR) + bias
                sc[n, pl.ds(pl.multiple_of(i * KEYS, KEYS), KEYS), :] = st
                new.append(jnp.maximum(peaks[n], jnp.max(st.reshape(16, 8, 512), axis=0)))
            return tuple(new)

        start = tuple(jnp.full((8, 512), MASKED, F32) for _ in range(3))
        peaks = lax.fori_loop(0, 8, scores, start)
        peaks = [jnp.max(p, axis=0, keepdims=True) for p in peaks]
        if old is not None:
            peaks = [jnp.maximum(p, o[0]) for p, o in zip(peaks, old)]
        totals = []
        for n in range(3):
            if old is None:
                acc[n] = jnp.zeros((64, 512), F32)
                totals.append(jnp.zeros((8, 512), F32))
            else:
                shrink = jnp.exp(old[n][0] - peaks[n])
                acc[n] = acc[n] * shrink
                totals.append(old[n][1] * shrink)

        def mix(i, sums):
            b = b0 + (b1 - b0) * (i // 2)
            xs = (i % 2) * 2
            new = []
            for n in range(3):
                at = pl.ds(pl.multiple_of(i * 256, 256), 256)
                p = jnp.exp(sc[n, at, :] - peaks[n])
                new.append(sums[n] + jnp.sum(p.reshape(32, 8, 512), axis=0))
                v = slice(192 + 64 * n, 256 + 64 * n)
                values = jnp.concatenate([kvb[b, xs, v, :], kvb[b, xs + 1, v, :]], axis=1)
                acc[n] += mxu(values, p.astype(BF))
            return tuple(new)

        totals = lax.fori_loop(0, 4, mix, tuple(totals))
        return list(zip(peaks, totals))

    state = half(k, k_partner, None)
    if first:
        plan.close_all(0, *later)
        plan.close_all(1, 1, 2)
        plan.relay_all(2, 0)
    else:
        plan.relay_all(1, 1, 2)
        plan.relay_all(2, 0)
    for s in (0, 1, 3, 2):
        slot = kvb.at[k_across, (x + 4 - s) % 4]
        arrived(slot, ysend.at[s], yrecv.at[s], across)
        send(slot, slot, fsend.at[s], frecv.at[s], partner)
    for s in (0, 1, 3, 2):
        arrived(kvb.at[k_diag, (x + 4 - s) % 4], fsend.at[s], frecv.at[s], partner)
    keep = pltpu.make_async_copy(kvb, kv_out, osem)
    keep.start()
    state = half(k_across, k_diag, state)
    log_out[...] = jnp.zeros_like(log_out)
    for n in range(3):
        total = jnp.sum(state[n][1], axis=0, keepdims=True)
        mixed = acc[n] / total
        att_out[64 * n : 64 * n + 64, :] = mixed
        log_out[n : n + 1, :] = state[n][0] + jnp.log(total)
        for xs in range(4):
            back[xs, 64 * n : 64 * n + 64, :] = mixed[:, 128 * xs : 128 * xs + 128].astype(BF)
    ab[x] = back[x]
    for s in (2, 1, 3):
        peer = peer_of(me, "x", s)
        send(back.at[peer["x"]], ab.at[x], bsend.at[s - 1], brecv.at[s - 1], peer)
    q_out[...] = qb[...]
    if first:
        plan.relay_all(1, *later)
    else:
        plan.close_all(1, 1, 2)
    plan.close_all(2, 0)
    for i in feed:
        plan.complete(i)
    load(vu, gathered[0])
    load(vd, gathered[1])
    for s in (1, 3, 2):
        source = peer_of(me, "x", 4 - s)
        arrived(ab.at[source["x"]], bsend.at[s - 1], brecv.at[s - 1], source)
    mixed = ab[...].reshape(768, 128).astype(F32).T.astype(BF)
    mixed_out[...] = mixed
    before = hid[...].astype(F32) + (mxu(mixed, joint_columns(2304)) + rows[2:3])
    before1_out[...] = before
    first_norm = normalized(before)[0] * rows[3:4] + rows[4:5]
    low = first_norm.astype(BF)
    low_out[...] = low
    second = first_norm + rows[5:6]
    for q in range(4):
        at = slice(768 * q, 768 * q + 768)
        u = mxu(low, vu[:, :, :, :, :, at].reshape(768, 768)) + up_add[0:1, at]
        up_out[:, at] = u
        a = (u * normal_cdf(u)).astype(BF)
        act_out[:, at] = a
        second = second + mxu(a, vd[q].reshape(768, 768))
    before2_out[...] = second
    res[...] = (normalized(second)[0] * rows[6:7] + rows[7:8]).astype(BF)
    keep.wait()
    if first:
        plan.close_all(1, *later)
        for i in later:
            plan.complete(i)
    plan.end()
    for copy in loads[0 if first else 1 :]:
        copy.wait()
    for copy in sends:
        copy.wait_send()


def forward_layer(first, hidden, lengths, known, shards):
    vmem = pl.BlockSpec(memory_space=pltpu.VMEM)
    anyspace = pl.BlockSpec(memory_space=pl.ANY)
    dma = pltpu.SemaphoreType.DMA
    out = jax.ShapeDtypeStruct
    n = len(FIRST_PIECES if first else SECOND_PIECES)
    got = [(24, 3072), (96, 768)]
    if first:
        got += [(24, 3072), (24, 3072)]
    return pl.pallas_call(
        functools.partial(forward_kernel, first),
        out_shape=[
            out((128, 768), BF),
            out((4, 192, 128), BF),
            out((4, 4, 384, 128), BF),
            out((8, 512), F32),
            out((192, 512), F32),
            out((128, 768), BF),
            out((128, 768), F32),
            out((128, 768), BF),
            out((128, 3072), F32),
            out((128, 3072), BF),
            out((128, 768), F32),
        ]
        + ([out((2, 8, 768), F32), out((2, 8, 3072), F32)] if first else [])
        + [out((4, 2, 2, 2, *s), BF) for s in got],
        in_specs=[vmem, pl.BlockSpec(memory_space=pltpu.SMEM)]
        + ([vmem] * 9 if first else [vmem, vmem, anyspace])
        + [anyspace] * len(shards),
        out_specs=[vmem, vmem, anyspace]
        + [vmem] * (10 if first else 8)
        + [anyspace] * len(got),
        scratch_shapes=[
            pltpu.VMEM((4, 2, 2, 2, 24, 3072), BF),
            pltpu.VMEM((4, 2, 2, 2, 24, 3072), BF),
            pltpu.VMEM((4, 2, 2, 2, 96, 768), BF),
            pltpu.VMEM((4, 576, 128), BF),
            pltpu.VMEM((4, 192, 128), BF),
            pltpu.VMEM((4, 4, 384, 128), BF),
            pltpu.VMEM((3, 1024, 512), F32),
            pltpu.VMEM((3, 64, 512), F32),
            pltpu.VMEM((4, 192, 128), BF),
            pltpu.VMEM((4, 192, 128), BF),
            pltpu.VMEM((4, 2, 2, 2, 32, 256), BF),
            pltpu.VMEM((2, 8, 896), F32),
            pltpu.VMEM((2, 8, 3200), F32),
            dma((4,)),
            dma,
            dma((3,)),
            dma((3,)),
            dma((3,)),
            dma((3,)),
            dma((4,)),
            dma((4,)),
            dma((4,)),
            dma((4,)),
            dma((4,)),
            dma((4,)),
            dma((3,)),
            dma((3,)),
            pltpu.VMEM((32, 256), F32),
            pltpu.VMEM((32, 256), BF),
            dma((n, 3, 4)),
            dma((n, 3, 4)),
            dma((n, 4, 3)),
            dma((n, 4, 3)),
            dma((n,)),
        ],
        compiler_params=pltpu.CompilerParams(
            collective_id=2 if first else 0,
            has_side_effects=True,
            vmem_limit_bytes=60 * 1024 * 1024,
        ),
        name="forward_first" if first else "forward_second",
    )(hidden, lengths, *known, *shards)


def backward_kernel(layer, *refs):
    refs = list(refs)

    def take(count):
        out = refs[:count]
        del refs[:count]
        return out

    beside = layer == 0
    dy, rows, up, before2, before1, qb, kvb, logs, att, lens, wj, wu, wd = take(13)
    operands = take(5) if beside else None
    dh_out, dj_out, db_out, du_out, df_out, vec_out = take(6)
    sums_out = take(1)[0] if beside else None
    vj, vu, vd, das, dab, dkv, rx, ry, rl, py, dq, sb, dj = take(13)
    wsem, asend, arecv, csend, crecv, jsend, jrecv = take(7)
    rows = rows.at[layer]
    me = my_place()
    x, c = me["x"], me["c"]
    yh = me["y"] // 2
    partner, across = peer_of(me, "c", 1), peer_of(me, "y", 2)
    loads = []
    for q in range(4):
        at = slice(768 * q, 768 * q + 768)
        for a, b in ((wd.at[at], vd.at[at]), (wu.at[:, at], vu.at[:, at])):
            loads.append(pltpu.make_async_copy(a, b, wsem.at[len(loads)]))
    loads.append(pltpu.make_async_copy(wj, vj, wsem.at[8]))
    for copy in loads:
        copy.start()
    if beside:
        reducer = Reducer(me, operands, refs[:8], sums_out, refs[8:])
        greet_all(me)
        reducer.exchange()
    else:
        greet_sequence(me)
    sends = []

    def send(src, dst, s, r, place):
        copy = remote(src, dst, s, r, place)
        copy.start()
        sends.append(copy)

    def arrived(slot, s, r, place):
        remote(slot, slot, s, r, place).wait_recv()

    def column_sum(a):
        return jnp.sum(a.astype(F32), axis=0, keepdims=True)

    vec_out[...] = jnp.zeros_like(vec_out)
    d_second, gain_grad, shift_grad = norm_backward(before2[...], rows[6:7], dy[...])
    vec_out[6:7] = gain_grad
    vec_out[7:8] = shift_grad
    df = d_second.astype(BF)
    df_out[...] = df
    vec_out[5:6] = column_sum(df)
    d_first = d_second
    for q in range(4):
        loads[2 * q].wait()
        loads[2 * q + 1].wait()
        at = slice(768 * q, 768 * q + 768)
        u = up[:, at]
        slope = normal_cdf(u) + u * (0.3989422804014327 * jnp.exp(-0.5 * u * u))
        du = (mxu(df, vd[at, :], FAR) * slope).astype(BF)
        du_out[:, at] = du
        vec_out[8 + q : 9 + q] = column_sum(du)
        d_first = d_first + mxu(du, vu[:, at], FAR)
    d_sum, gain_grad, shift_grad = norm_backward(before1[...], rows[3:4], d_first)
    vec_out[3:4] = gain_grad
    vec_out[4:5] = shift_grad
    db = d_sum.astype(BF)
    db_out[...] = db
    vec_out[2:3] = column_sum(db)
    dh_out[...] = d_sum
    loads[8].wait()
    da = mxu(db, vj[:, 2304:3072], FAR).T.astype(BF)
    for g in range(4):
        das[g] = da[192 * g : 192 * g + 192]
    dab[x] = das[x]
    for s in (2, 1, 3):
        peer = peer_of(me, "x", s)
        send(das.at[peer["x"]], dab.at[x], asend.at[s - 1], arecv.at[s - 1], peer)
    if beside:
        reducer.exchanged()
        for third in range(3):
            reducer.products(third)
    for s in (1, 3, 2):
        source = peer_of(me, "x", 4 - s)
        arrived(dab.at[source["x"]], asend.at[s - 1], arecv.at[s - 1], source)
    length = lens[0]

    def by_head(ref, n):
        return jnp.concatenate([ref[xs, 64 * n : 64 * n + 64] for xs in range(4)], axis=1)

    inner = []
    for n in range(3):
        dq[n] = jnp.zeros((64, 512), F32)
        inner.append(
            jnp.sum(
                by_head(dab, n).astype(F32) * att[64 * n : 64 * n + 64, :], axis=0, keepdims=True
            )
        )

    def half(which, base):
        def step(i, carry):
            core, xs = i // 4, i % 4
            b = base + core
            bias = key_bias(length, b, xs)
            bias = jnp.concatenate([bias] * 2, axis=1)
            for n in range(3):
                own = slice(64 * n, 64 * n + 64)
                keys = kvb[b, xs, own, :]
                values = kvb[b, xs, slice(192 + 64 * n, 256 + 64 * n), :]
                dk = dv = None
                for h in range(2):
                    at = slice(256 * h, 256 * h + 256)
                    q_n = jnp.concatenate([qb[2 * h, own], qb[2 * h + 1, own]], axis=1)
                    da_n = jnp.concatenate([dab[2 * h, own], dab[2 * h + 1, own]], axis=1)
                    p = jnp.exp(mxu(keys, q_n, NEAR) + bias - logs[n : n + 1, at])
                    dp = mxu(values, da_n, NEAR)
                    ds = (p * (dp - inner[n][:, at])).astype(BF)
                    dq[n, :, at] += mxu(keys, ds)
                    k_term = mxu(q_n, ds, FAR)
                    v_term = mxu(da_n, p.astype(BF), FAR)
                    dk = k_term if dk is None else dk + k_term
                    dv = v_term if dv is None else dv + v_term
                dkv[which, core, xs, 64 * n : 64 * n + 64, :] = dk.astype(BF)
                dkv[which, core, xs, 192 + 64 * n : 256 + 64 * n, :] = dv.astype(BF)
            return carry

        lax.fori_loop(0, 8, step, 0)

    half(0, (1 - yh) * 2)
    send(dkv.at[0, 1 - c], rx, csend.at[0], crecv.at[0], partner)
    arrived(rx, csend.at[0], crecv.at[0], partner)
    for xs in range(4):
        py[xs] = (dkv[0, c, xs].astype(F32) + rx[xs].astype(F32)).astype(BF)
    send(py, ry, csend.at[1], crecv.at[1], across)
    if beside:
        for third in range(3):
            reducer.middle(0, third)
    half(1, yh * 2)
    send(dkv.at[1, 1 - c], rl, csend.at[2], crecv.at[2], partner)
    if beside:
        for third in range(3):
            reducer.finish(0, third)
    for xs in range(4):
        for n in range(3):
            part = dq[n, :, 128 * xs : 128 * xs + 128] * 0.125
            sb[xs, 64 * n : 64 * n + 64, :] = part.astype(BF)
    arrived(rl, csend.at[2], crecv.at[2], partner)
    arrived(ry, csend.at[1], crecv.at[1], across)
    for xs in range(4):
        total = dkv[1, c, xs].astype(F32) + rl[xs].astype(F32) + ry[xs].astype(F32)
        sb[xs, 192:576, :] = total.astype(BF)
    dj[x] = sb[x]
    for s in (2, 1, 3):
        peer = peer_of(me, "x", s)
        send(sb.at[peer["x"]], dj.at[x], jsend.at[s - 1], jrecv.at[s - 1], peer)
    if beside:
        for third in range(3):
            reducer.middle(1, third)
    for s in (1, 3, 2):
        source = peer_of(me, "x", 4 - s)
        arrived(dj.at[source["x"]], jsend.at[s - 1], jrecv.at[s - 1], source)
    dh = dh_out[...]
    for j in range(3):
        at = slice(768 * j, 768 * j + 768)
        t = jnp.concatenate([dj[g, 192 * j : 192 * j + 192] for g in range(4)], axis=0)
        t = t.astype(F32).T.astype(BF)
        dj_out[:, at] = t
        if j != 1:
            row = 0 if j == 0 else 1
            vec_out[row : row + 1] = column_sum(t)
        dh = dh + mxu(t, vj[:, at], FAR)
    dh_out[...] = dh
    if beside:
        for third in range(3):
            reducer.finish(1, third)
        reducer.end()
    for copy in sends:
        copy.wait_send()


def backward_layer(layer, dy, rows, up, before2, before1, q, kv, logs, att, lengths, wj, wu, wd, later):
    vmem = pl.BlockSpec(memory_space=pltpu.VMEM)
    anyspace = pl.BlockSpec(memory_space=pl.ANY)
    dma = pltpu.SemaphoreType.DMA
    out = jax.ShapeDtypeStruct
    return pl.pallas_call(
        functools.partial(backward_kernel, layer),
        out_shape=[
            out((128, 768), F32),
            out((128, 2304), BF),
            out((128, 768), BF),
            out((128, 3072), BF),
            out((128, 768), BF),
            out((16, 768), F32),
        ]
        + ([out((3, 4, 24, 768), BF)] if layer == 0 else []),
        in_specs=[vmem] * 9
        + [pl.BlockSpec(memory_space=pltpu.SMEM)]
        + [anyspace] * (3 + len(later)),
        out_specs=[vmem] * (7 if layer == 0 else 6),
        scratch_shapes=[
            pltpu.VMEM((768, 3072), BF),
            pltpu.VMEM((768, 3072), BF),
            pltpu.VMEM((3072, 768), BF),
            pltpu.VMEM((4, 192, 128), BF),
            pltpu.VMEM((4, 192, 128), BF),
            pltpu.VMEM((2, 2, 4, 384, 128), BF),
            pltpu.VMEM((4, 384, 128), BF),
            pltpu.VMEM((4, 384, 128), BF),
            pltpu.VMEM((4, 384, 128), BF),
            pltpu.VMEM((4, 384, 128), BF),
            pltpu.VMEM((3, 64, 512), F32),
            pltpu.VMEM((4, 576, 128), BF),
            pltpu.VMEM((4, 576, 128), BF),
            dma((9,)),
            dma((3,)),
            dma((3,)),
            dma((3,)),
            dma((3,)),
            dma((3,)),
            dma((3,)),
        ]
        + (reducer_buffers() + reducer_semaphores() if layer == 0 else []),
        compiler_params=pltpu.CompilerParams(
            collective_id=3 + layer, has_side_effects=True, vmem_limit_bytes=60 * 1024 * 1024
        ),
        name="backward_layer",
    )(dy, rows, up, before2, before1, q, kv, logs, att, lengths, wj, wu, wd, *later)


def body(
    inputs,
    lengths,
    joint_weight,
    query_bias,
    value_bias,
    output_weight,
    output_bias,
    first_gain,
    first_shift,
    up_weight,
    up_bias,
    down_weight,
    down_bias,
    second_gain,
    second_shift,
    cotangent,
):
    small = (
        query_bias,
        value_bias,
        output_bias,
        first_gain,
        first_shift,
        down_bias,
        second_gain,
        second_shift,
        up_bias,
    )
    joint_and_out = jnp.concatenate([joint_weight, output_weight], axis=-1)
    hidden0 = inputs.reshape(128, 768)
    got = forward_layer(
        True,
        hidden0,
        lengths,
        small,
        (up_weight, down_weight, joint_and_out),
    )
    rows_all, up_adds, up0, down0, joint0, joint1 = got[11:]
    more = forward_layer(
        False, got[0], lengths, (rows_all, up_adds, joint1), (up_weight, down_weight)
    )
    up1, down1 = more[11:]
    weights_of = [
        (j.reshape(768, 3072), u.reshape(768, 3072), d.reshape(3072, 768))
        for j, u, d in ((joint0, up0, down0), (joint1, up1, down1))
    ]
    kept = [(hidden0, *got[1:11]), (got[0], *more[1:11])]
    outputs = [got[0].reshape(1, 128, 768), more[0].reshape(1, 128, 768)]
    grad_rows = cotangent.reshape(128, 768).astype(F32)
    vector_grads = [None] * LAYERS
    later = ()
    for l in reversed(range(LAYERS)):
        hidden, q, kv, logs, att, mixed, before1, low, up, acts, before2 = kept[l]
        grad_rows, d_joint, d_branch, d_up, d_down, vector_grads[l], *sums = backward_layer(
            l,
            grad_rows,
            rows_all,
            up,
            before2,
            before1,
            q,
            kv,
            logs,
            att,
            lengths,
            *weights_of[l],
            later,
        )
        later = reducer_operands(hidden, mixed, low, acts, d_joint, d_branch, d_up, d_down)
    vectors = jnp.concatenate(vector_grads)
    joint_grad, out_grad, up_grad, down_grad, vectors = reduce_grads(later, sums[0], vectors)
    vectors = vectors.reshape(LAYERS, 16, 768)
    owner = lax.axis_index("batch") * 4 + lax.axis_index("blk")
    own_rows = lax.dynamic_slice_in_dim(vectors[:, :8], owner * 24, 24, axis=2)
    own_up = lax.dynamic_slice_in_dim(vectors[:, 8:12].reshape(LAYERS, 3072), owner * 96, 96, axis=1)
    stacked = (
        joint_grad,
        own_rows[:, 0],
        own_rows[:, 1],
        out_grad,
        own_rows[:, 2],
        own_rows[:, 3],
        own_rows[:, 4],
        up_grad,
        own_up,
        down_grad,
        own_rows[:, 5],
        own_rows[:, 6],
        own_rows[:, 7],
    )
    activations = jnp.stack(outputs)
    input_grad = grad_rows.reshape(1, 128, 768)
    return (
        activations,
        input_grad,
        stacked[0],
        stacked[1],
        stacked[2],
        stacked[3],
        stacked[4],
        stacked[5],
        stacked[6],
        stacked[7],
        stacked[8],
        stacked[9],
        stacked[10],
        stacked[11],
        stacked[12],
    )


def solution(mesh):
    placed = (
        P("batch", ("head", "blk"), None),
        P("batch"),
        P(None, ("batch", "blk"), None),
        P(None, ("batch", "blk")),
        P(None, ("batch", "blk")),
        P(None, ("batch", "blk"), None),
        P(None, ("batch", "blk")),
        P(None, ("batch", "blk")),
        P(None, ("batch", "blk")),
        P(None, ("batch", "blk"), None),
        P(None, ("batch", "blk")),
        P(None, ("batch", "blk"), None),
        P(None, ("batch", "blk")),
        P(None, ("batch", "blk")),
        P(None, ("batch", "blk")),
        P("batch", ("head", "blk"), None),
    )
    return jax.shard_map(
        body,
        mesh=mesh,
        in_specs=placed,
        out_specs=(
            P(None, "batch", ("head", "blk"), None),
            P("batch", ("head", "blk"), None),
            P(None, ("batch", "blk"), None),
            P(None, ("batch", "blk")),
            P(None, ("batch", "blk")),
            P(None, ("batch", "blk"), None),
            P(None, ("batch", "blk")),
            P(None, ("batch", "blk")),
            P(None, ("batch", "blk")),
            P(None, ("batch", "blk"), None),
            P(None, ("batch", "blk")),
            P(None, ("batch", "blk"), None),
            P(None, ("batch", "blk")),
            P(None, ("batch", "blk")),
            P(None, ("batch", "blk")),
        ),
        check_vma=False,
    )
```

```python
import functools

import jax
import jax.numpy as jnp
from jax import lax
from jax.experimental import pallas as pl
from jax.experimental.pallas import tpu as pltpu
from jax.sharding import PartitionSpec as P

LAYERS = 2


EPSILON = 1e-12
MASKED = -1e30


MESH = pl.DeviceIdType.MESH
ALL = slice(None)


def my_place():
    b, x, k = lax.axis_index("batch"), lax.axis_index("head"), lax.axis_index("blk")
    return {"z": b // 2, "y": (k // 2) * 2 + b % 2, "x": x, "c": k % 2}


def device_of(place):
    return (
        place["z"] * 2 + place["y"] % 2,
        place["x"],
        (place["y"] // 2) * 2 + place["c"],
    )


def peer_of(place, axis, step):
    other = dict(place)
    other[axis] = (place[axis] + step) % (2 if axis == "c" else 4)
    return other


def greet_all(place):
    barrier = pltpu.get_barrier_semaphore()
    peers = [peer_of(place, a, s) for a in ("x", "y", "z") for s in (1, 2, 3)]
    peers.append(peer_of(place, "c", 1))
    for p in peers:
        pl.semaphore_signal(barrier, inc=1, device_id=device_of(p), device_id_type=MESH)
    pl.semaphore_wait(barrier, len(peers))


def remote(src, dst, send, recv, place):
    return pltpu.make_async_remote_copy(
        src_ref=src,
        dst_ref=dst,
        send_sem=send,
        recv_sem=recv,
        device_id=device_of(place),
        device_id_type=MESH,
    )


class Gather:
    def __init__(self, me, pieces, ins, outs, sems):
        self.me, self.pieces, self.ins, self.outs = me, pieces, ins, outs
        self.send, self.recv, self.fsend, self.frecv, self.local = sems
        self.partner = peer_of(me, "c", 1)
        self.started, self.locals = [], {}

    def order(self, i):
        return self.pieces[i][3]

    def direct(self, i, phase):
        return phase in self.pieces[i][5]

    def region(self, i, phase, place, half=None):
        array, start, width, order, by_rows, _ = self.pieces[i]
        done = order[:phase]
        z = ALL if "z" in done else place["z"]
        y = (ALL, ALL) if "y" in done else (place["y"] % 2, place["y"] // 2)
        lines = ALL
        if "x" in order and "x" not in done:
            width = width // 4
            start = start + place["x"] * width
        if half is not None:
            if by_rows:
                count = self.outs[array].shape[-2] // 2
                lines = pl.ds(count * half, count)
            else:
                width = width // 2
                start = start + half * width
        columns = self.columns(array, start, width)
        return self.outs[array].at[z, y[0], y[1], place["c"], lines, columns]

    def columns(self, array, start, width):
        if width == self.outs[array].shape[-1]:
            return ALL
        return pl.ds(start if isinstance(start, int) else pl.multiple_of(start, 128), width)

    def own(self, i):
        array, start, width, order, _, _ = self.pieces[i]
        if "x" in order:
            width = width // 4
            start = start + self.me["x"] * width
        columns = self.columns(array, start, width)
        return self.ins[array].at[ALL, columns]

    def copy(self, src, dst, s, r, place):
        copy = remote(src, dst, s, r, place)
        copy.start()
        self.started.append(copy)

    def near(self, i, phase):
        axis = self.order(i)[phase]
        return peer_of(self.me, axis, 1), peer_of(self.me, axis, 3), peer_of(self.me, axis, 2)

    def start(self, i, phase):
        right, left, opposite = self.near(i, phase)
        dst = self.region(i, phase, self.me)
        if phase == 0:
            copy = pltpu.make_async_copy(self.own(i), dst, self.local.at[i])
            copy.start()
            self.locals[i] = copy
        src = self.own(i) if phase == 0 else dst
        places = [(0, right), (1, left)]
        if self.direct(i, phase):
            places = [(2, opposite)] + places
        for j, place in places:
            self.copy(src, dst, self.send.at[i, phase, j], self.recv.at[i, phase, j], place)
        if phase == 0:
            self.copy(src, dst, self.fsend.at[i, 3, 0], self.frecv.at[i, 3, 0], self.partner)

    def arrived(self, slot, i, phase, j, place):
        remote(
            slot, slot, self.send.at[i, phase, j], self.recv.at[i, phase, j], place
        ).wait_recv()

    def pass_on(self, i, phase, j, place):
        slot = self.region(i, phase, place)
        self.copy(
            slot, slot, self.fsend.at[i, phase, j], self.frecv.at[i, phase, j], self.partner
        )

    def relay(self, i, phase):
        right, left, _ = self.near(i, phase)
        for j, source, target in ((0, left, right), (1, right, left)):
            self.arrived(self.region(i, phase, source), i, phase, j, source)
            if not self.direct(i, phase):
                part = self.region(i, phase, source, j)
                self.copy(
                    part, part, self.send.at[i, phase, 2 + j], self.recv.at[i, phase, 2 + j], target
                )
            self.pass_on(i, phase, j, source)

    def close(self, i, phase):
        right, left, opposite = self.near(i, phase)
        if self.direct(i, phase):
            self.arrived(self.region(i, phase, opposite), i, phase, 2, opposite)
        else:
            for j, source in ((0, left), (1, right)):
                self.arrived(self.region(i, phase, opposite, j), i, phase, 2 + j, source)
        self.pass_on(i, phase, 2, opposite)
        if phase == 0:
            self.locals[i].wait()

    def complete(self, i):
        slots = [((3, 0), self.region(i, 0, self.partner))]
        for phase, axis in enumerate(self.order(i)):
            for j, s in ((0, 3), (1, 1), (2, 2)):
                slots.append(((phase, j), self.region(i, phase, peer_of(self.partner, axis, s))))
        for at, slot in slots:
            remote(
                slot, slot, self.fsend.at[i, *at], self.frecv.at[i, *at], self.partner
            ).wait_recv()

    def end(self):
        for copy in self.started:
            copy.wait_send()


    def relay_all(self, phase, *group):
        for i in group:
            self.relay(i, phase)

    def close_all(self, phase, *group):
        for i in group:
            self.close(i, phase)
            if phase + 1 < len(self.order(i)):
                self.start(i, phase + 1)


def joint_pieces(array, direct):
    return (
        (array, 0, 1536, ("y", "z"), False, direct),
        (array, 1536, 1536, ("z", "y"), False, direct),
    )


def feed_pieces(array, order, direct):
    return (
        (array, 0, 3072, order, False, direct),
        (array + 1, 0, 384, ("y", "z"), True, direct),
        (array + 1, 384, 384, ("y", "z"), True, direct),
    )


NEVER = ()
FIRST_PIECES = (
    feed_pieces(0, ("y", "z", "x"), NEVER)
    + (
        (2, 0, 1280, ("y", "z"), False, NEVER),
        (2, 1280, 1024, ("z", "y"), False, NEVER),
        (2, 2304, 768, ("z", "y"), False, NEVER),
    )
    + joint_pieces(3, NEVER)
    + ((4, 0, 256, ("y", "z"), True, NEVER),)
)
SECOND_PIECES = feed_pieces(0, ("y", "z", "x"), NEVER)


THIRDS = (("x", "y", "z"), ("y", "z", "x"), ("z", "x", "y"))


class Reducer:
    low_half, high_half = pl.ds(0, 2), pl.ds(2, 2)

    def __init__(self, me, ins, bufs, s2, sems):
        self.me, self.ins, self.s2 = me, ins, s2
        self.lhs, self.rhs, self.g, self.o1, self.r1, self.s1, self.o2, self.r2 = bufs
        self.csend, self.crecv, self.lsem, self.qs, self.qr = sems
        self.sends = []

    def exchange(self):
        me, c = self.me, self.me["c"]
        partner = peer_of(me, "c", 1)
        half = pl.ds(pl.multiple_of(c * 128, 128), 128)
        lhs_in, rhs_in = self.ins[0], self.ins[1:]
        dst = self.lhs.at[ALL, half]
        self.away = [remote(lhs_in.at[1 - c], dst, self.csend.at[0], self.crecv.at[0], partner)]
        self.here = [pltpu.make_async_copy(lhs_in.at[c], dst, self.lsem.at[0])]
        starts, widths = (0, 3072, 3840, 6144), (3072, 768, 2304, 768)
        for j in range(4):
            dst = self.rhs.at[half, pl.ds(starts[j], widths[j])]
            self.away.append(
                remote(rhs_in[j], dst, self.csend.at[j + 1], self.crecv.at[j + 1], partner)
            )
            self.here.append(pltpu.make_async_copy(rhs_in[j], dst, self.lsem.at[j + 1]))
        for copy in self.away + self.here:
            copy.start()

    def products(self, t):
        for j in ((0, 1), (2,), (3, 4))[t]:
            self.here[j].wait()
            self.away[j].wait_recv()
        for q in range(4):
            unit = (0, 1 + q, 5 if q < 3 else 6)[t]
            col = (q * 768, 3072, 3840 + q * 768)[t]
            block = jnp.dot(
                self.lhs[384 * unit : 384 * unit + 384, :],
                self.rhs[:, col : col + 768],
                preferred_element_type=jnp.float32,
            )
            for i in range(16):
                z, y = i // 4, (i % 2) * 2 + (i // 2) % 2
                at = ((q, y, z), (y, z, q), (z, q, y))[t]
                part = block[24 * i : 24 * i + 24]
                self.g[t, at[0], at[1], at[2]] = part.astype(jnp.bfloat16)
        self.start(0, t)

    def copy(self, phase, t, j, src, dst, peer):
        copy = remote(src, dst, self.qs.at[phase, t, j], self.qr.at[phase, t, j], peer)
        copy.start()
        self.sends.append(copy)

    def wait(self, phase, t, j, slot, peer):
        remote(slot, slot, self.qs.at[phase, t, j], self.qr.at[phase, t, j], peer).wait_recv()

    def refs(self, phase, t):
        axis = THIRDS[t][phase]
        places = [peer_of(self.me, axis, s) for s in (1, 3, 2)]
        held, over, got = (
            (self.g, self.o1, self.r1),
            (self.s1, self.o2, self.r2),
        )[phase]
        return axis, places, held.at[t], over.at[t], got.at[t]

    def start(self, phase, t):
        axis, (right, left, far), held, over, got = self.refs(phase, t)
        low, high = self.low_half, self.high_half
        self.copy(phase, t, 0, held.at[far[axis], low], over.at[0], right)
        self.copy(phase, t, 1, held.at[far[axis], high], over.at[1], left)
        self.copy(phase, t, 2, held.at[right[axis], high], got.at[0, high], right)
        self.copy(phase, t, 3, held.at[left[axis], low], got.at[1, low], left)

    def middle(self, phase, t):
        axis, (right, left, far), held, over, got = self.refs(phase, t)
        f32 = jnp.float32
        for j, source, target in ((0, left, right), (1, right, left)):
            self.wait(phase, t, j, over.at[j], source)
            at = target[axis]
            for a in range(2):
                if phase == 0:

                    def merge(b, carry, a=a, j=j, at=at):
                        total = held[at, 2 * j + a, b].astype(f32) + over[j, a, b].astype(f32)
                        held[at, 2 * j + a, b] = total.astype(jnp.bfloat16)
                        return carry

                    lax.fori_loop(0, 4, merge, 0)
                else:
                    total = held[at, 2 * j + a].astype(f32) + over[j, a].astype(f32)
                    held[at, 2 * j + a] = total.astype(jnp.bfloat16)
            part = (self.low_half, self.high_half)[j]
            self.copy(phase, t, 4 + j, held.at[at, part], got.at[j, part], target)

    def finish(self, phase, t):
        axis, (right, left, far), held, over, got = self.refs(phase, t)
        low, high = self.low_half, self.high_half
        self.wait(phase, t, 2, got.at[0, high], left)
        self.wait(phase, t, 3, got.at[1, low], right)
        self.wait(phase, t, 4, got.at[0, low], left)
        self.wait(phase, t, 5, got.at[1, high], right)
        mine = self.me[axis]
        f32 = jnp.float32
        if phase == 0:

            def add(i, carry):
                a, b = i // 4, i % 4
                total = held[mine, a, b].astype(f32)
                for s in range(2):
                    total = total + got[s, a, b].astype(f32)
                self.s1[t, a, b] = total.astype(jnp.bfloat16)
                return carry

            lax.fori_loop(0, 16, add, 0)
            self.start(1, t)
        else:
            for a in range(4):
                total = held[mine, a].astype(f32)
                for s in range(2):
                    total = total + got[s, a].astype(f32)
                self.s2[t, a] = total.astype(jnp.bfloat16)

    def end(self):
        for copy in self.sends + self.away:
            copy.wait_send()


def reducer_buffers():
    bf = jnp.bfloat16
    return [
        pltpu.VMEM((2688, 256), bf),
        pltpu.VMEM((256, 6912), bf),
        pltpu.VMEM((3, 4, 4, 4, 24, 768), bf),
        pltpu.VMEM((3, 2, 2, 4, 24, 768), bf),
        pltpu.VMEM((3, 2, 4, 4, 24, 768), bf),
        pltpu.VMEM((3, 4, 4, 24, 768), bf),
        pltpu.VMEM((3, 2, 2, 24, 768), bf),
        pltpu.VMEM((3, 2, 4, 24, 768), bf),
    ]


def reducer_semaphores():
    dma = pltpu.SemaphoreType.DMA
    return [dma((5,)), dma((5,)), dma((5,)), dma((2, 3, 6)), dma((2, 3, 6))]


def reduce_kernel(*refs):
    operands = refs[:5]
    s2_in, vec_first, vec_last = refs[5:8]
    refs = refs[1:]
    joint_out, out_out, up_out, down_out, vec_out = refs[7:12]
    s2, r3, last, vc, va = refs[20:25]
    ps, pr, vs, vr = refs[30:]
    me = my_place()
    layers = (1, 0)
    f32 = jnp.float32
    reducer = Reducer(me, operands, refs[12:20], s2.at[0], refs[25:30])
    greet_all(me)
    reducer.exchange()

    vec_axes = ("c", "x", "y", "z")
    vec_sends = []

    def vec_slot(phase, place):
        if phase == 0:
            return vc.at[place["c"]]
        return va.at[phase - 1, place[vec_axes[phase]]]

    def vec_start(phase, value):
        vec_slot(phase, me)[...] = value.astype(jnp.bfloat16)
        for s in range(1, 2 if phase == 0 else 4):
            copy = remote(
                vec_slot(phase, me),
                vec_slot(phase, me),
                vs.at[phase, s - 1],
                vr.at[phase, s - 1],
                peer_of(me, vec_axes[phase], s),
            )
            copy.start()
            vec_sends.append(copy)

    def vec_finish(phase):
        count = 2 if phase == 0 else 4
        for s in range(1, count):
            src = peer_of(me, vec_axes[phase], count - s)
            slot = vec_slot(phase, src)
            remote(slot, slot, vs.at[phase, s - 1], vr.at[phase, s - 1], src).wait_recv()
        total = None
        for j in range(count):
            part = (vc[j] if phase == 0 else va[phase - 1, j]).astype(jnp.float32)
            total = part if total is None else total + part
        return total

    vec_start(0, jnp.concatenate([vec_first[...], vec_last[...]], axis=0))

    sends = []

    def send_chunks(phase, t, l, source, target):
        axis = THIRDS[t][phase] if phase < 3 else "x"
        for s in (2, 1, 3):
            peer = peer_of(me, axis, s)
            copy = remote(
                source(peer[axis]),
                target(s),
                ps.at[phase, t, l, s - 1],
                pr.at[phase, t, l, s - 1],
                peer,
            )
            copy.start()
            sends.append(copy)

    def await_chunks(phase, t, l, target):
        axis = THIRDS[t][phase] if phase < 3 else "x"
        for s in (1, 3, 2):
            slot = target(s)
            remote(
                slot,
                slot,
                ps.at[phase, t, l, s - 1],
                pr.at[phase, t, l, s - 1],
                peer_of(me, axis, s),
            ).wait_recv()

    def third_phase(l, t):
        send_chunks(2, t, l, lambda a: s2.at[l, t, a], lambda s: r3.at[t, l, s - 1])

    s2[1] = s2_in[...]
    for t in range(3):
        third_phase(1, t)
    for t in range(3):
        reducer.products(t)
    vec_start(1, vec_finish(0))
    for t in range(3):
        reducer.middle(0, t)
    for t in range(3):
        reducer.finish(0, t)
    vec_start(2, vec_finish(1))
    for t in range(3):
        reducer.middle(1, t)
    for t in range(3):
        reducer.finish(1, t)
        third_phase(0, t)
    vec_start(3, vec_finish(2))
    for l in layers:
        for t in range(3):
            mine = me[THIRDS[t][2]]
            await_chunks(2, t, l, lambda s, t=t, l=l: r3.at[t, l, s - 1])
            total = s2[l, t, mine].astype(f32)
            for s in range(3):
                total = total + r3[t, l, s].astype(f32)
            last[t, l, me["x"]] = total.astype(jnp.bfloat16)
            send_chunks(
                3,
                t,
                l,
                lambda a, t=t, l=l: last.at[t, l, me["x"]],
                lambda s, t=t, l=l: last.at[t, l, me["x"]],
            )
    vec_out[...] = vec_finish(3)
    for l in layers:
        for t in range(3):
            await_chunks(3, t, l, lambda s, t=t, l=l: last.at[t, l, (me["x"] + 4 - s) % 4])
            for q in range(4):
                part = last[t, l, q].astype(f32)
                if t == 0:
                    up_out[l, :, 768 * q : 768 * q + 768] = part
                elif t == 1:
                    down_out[l, 24 * q : 24 * q + 24, :] = part
                elif q < 3:
                    joint_out[l, :, 768 * q : 768 * q + 768] = part
                else:
                    out_out[l] = part
    reducer.end()
    for copy in sends + vec_sends:
        copy.wait_send()


def for_owner_cores(array):
    tokens, width = array.shape
    n = width // 768
    t = array.T.reshape(16, 2, n, 24, tokens).transpose(1, 2, 0, 3, 4)
    return t.reshape(2, n * 384, tokens)


def reducer_operands(hidden, mixed, first, acts, d_joint, d_branch, d_up, d_down):
    lhs = jnp.concatenate([for_owner_cores(a) for a in (first, acts, hidden, mixed)], axis=1)
    return lhs, d_up, d_down, d_joint, d_branch


def reduce_grads(operands, later, vectors):
    anyspace = pl.BlockSpec(memory_space=pl.ANY)
    vmem = pl.BlockSpec(memory_space=pltpu.VMEM)
    bf, dma = jnp.bfloat16, pltpu.SemaphoreType.DMA
    return pl.pallas_call(
        reduce_kernel,
        out_shape=[
            jax.ShapeDtypeStruct((2, 24, 2304), jnp.float32),
            jax.ShapeDtypeStruct((2, 24, 768), jnp.float32),
            jax.ShapeDtypeStruct((2, 24, 3072), jnp.float32),
            jax.ShapeDtypeStruct((2, 96, 768), jnp.float32),
            jax.ShapeDtypeStruct((32, 768), jnp.float32),
        ],
        in_specs=[anyspace] * 5 + [vmem] * 3,
        out_specs=[vmem] * 5,
        scratch_shapes=reducer_buffers()
        + [
            pltpu.VMEM((2, 3, 4, 24, 768), bf),
            pltpu.VMEM((3, 2, 3, 24, 768), bf),
            pltpu.VMEM((3, 2, 4, 24, 768), bf),
            pltpu.VMEM((2, 32, 768), bf),
            pltpu.VMEM((3, 4, 32, 768), bf),
        ]
        + reducer_semaphores()
        + [dma((4, 3, 2, 3)), dma((4, 3, 2, 3)), dma((4, 3)), dma((4, 3))],
        compiler_params=pltpu.CompilerParams(
            collective_id=1, has_side_effects=True, vmem_limit_bytes=60 * 1024 * 1024
        ),
        name="reduce_grads",
    )(*operands, later, *vectors)


FAR = (((1,), (1,)), ((), ()))
NEAR = (((0,), (0,)), ((), ()))
F32 = jnp.float32
BF = jnp.bfloat16
KEYS = 128


def mxu(a, b, dims=None):
    if dims is None:
        return jnp.dot(a, b, preferred_element_type=F32)
    return lax.dot_general(a, b, dims, preferred_element_type=F32)


def normalized(values):
    average = jnp.mean(values, axis=-1, keepdims=True)
    centered = values - average
    variance = jnp.mean(centered * centered, axis=-1, keepdims=True)
    r = lax.rsqrt(variance + EPSILON)
    return centered * r, r


def norm_backward(values, gain, grad):
    xhat, r = normalized(values)
    g = grad * gain
    back = r * (
        g - jnp.mean(g, axis=-1, keepdims=True) - xhat * jnp.mean(g * xhat, axis=-1, keepdims=True)
    )
    gain_grad = jnp.sum(grad * xhat, axis=0, keepdims=True)
    return back, gain_grad, jnp.sum(grad, axis=0, keepdims=True)


def normal_cdf(u):
    return 0.5 * (1.0 + lax.erf(u * 0.7071067811865476))


def greet_sequence(me):
    barrier = pltpu.get_barrier_semaphore()
    peers = [peer_of(me, "x", s) for s in (1, 2, 3)]
    peers += [peer_of(me, "c", 1), peer_of(me, "y", 2)]
    for p in peers:
        pl.semaphore_signal(barrier, inc=1, device_id=device_of(p), device_id_type=MESH)
    pl.semaphore_wait(barrier, len(peers))


def key_bias(length, block, xs):
    limit = length - xs * 512 - block * 128
    rows = lax.broadcasted_iota(jnp.int32, (KEYS, 128), 0)
    return jnp.where(rows < limit, 0.0, MASKED)


def forward_kernel(first, *refs):
    refs = list(refs)

    def take(count):
        out = refs[:count]
        del refs[:count]
        return out

    hid, lens = take(2)
    if first:
        small_in = take(9)
        up, down, joint_in = take(3)
        shards = [up.at[0], down.at[0], joint_in.at[0], joint_in.at[1]]
    else:
        rows, up_add, wj = take(3)
        up, down = take(2)
        shards = [up.at[1], down.at[1]]
    res, q_out, kv_out, log_out, att_out, mixed_out = take(6)
    before1_out, low_out, up_out, act_out, before2_out = take(5)
    if first:
        rows_out, add_out = take(2)
    gathered = take(4 if first else 2)
    vj, vu, vd, qs, qb, kvb, sc, acc, back, ab, vv, rsum, usum = take(13)
    wsem, osem, qsend, qrecv, xsend, xrecv, csend, crecv, ysend, yrecv, fsend, frecv = take(12)
    bsend, brecv = take(2)
    flat, own_small = take(2)
    me = my_place()
    if first:
        shards.append(own_small)
    lands = [vu, vd, vj, gathered[3], vv] if first else [vu, vd]
    plan = Gather(me, FIRST_PIECES if first else SECOND_PIECES, shards, lands, refs)
    joint, later, small = (3, 4), (6, 7), (8,)
    feed = (0, 1, 2, 5) if first else (0, 1, 2)
    x, c = me["x"], me["c"]
    yh = me["y"] // 2
    k = yh * 2 + c
    partner, across = peer_of(me, "c", 1), peer_of(me, "y", 2)
    k_partner = yh * 2 + 1 - c
    k_across = (1 - yh) * 2 + c
    k_diag = (1 - yh) * 2 + 1 - c
    greet_all(me)
    loads = []

    def load(src, dst):
        copy = pltpu.make_async_copy(src, dst, wsem.at[len(loads)])
        copy.start()
        loads.append(copy)

    if first:
        flat[...] = jnp.zeros_like(flat)
        for j in range(9):
            for l in range(2):
                flat[16 * l + j : 16 * l + j + 1, 0 : small_in[j].shape[1]] = small_in[j][
                    l : l + 1, :
                ].astype(F32)
        owner = lax.axis_index("batch") * 4 + lax.axis_index("blk")
        lines = lax.broadcasted_iota(jnp.int32, (32, 256), 0) % 16
        moved = pltpu.roll(flat[...], (owner * 24) % 128, axis=1)
        moved_up = pltpu.roll(flat[...], (owner * 96) % 128, axis=1)
        own_small[...] = jnp.where(lines == 8, moved_up, moved).astype(BF)
        for i in small + joint + feed:
            plan.start(i, 0)
        plan.relay_all(0, *small, *joint)
        plan.close_all(0, *small, *joint)
        plan.relay_all(0, *feed)
        plan.relay_all(1, *small, *joint)
        plan.close_all(0, *feed)
        plan.close_all(1, *small, *joint)
        for i in small + joint:
            plan.complete(i)
        rsum[...] = jnp.zeros_like(rsum)
        usum[...] = jnp.zeros_like(usum)

        def small_rows(l):
            for o in range(32):
                z, yl, yh, core = o // 8, (o // 4) % 2, (o // 2) % 2, o % 2
                at = (24 * o) // 128 * 128
                part = vv[z, yl, yh, core, 16 * l : 16 * l + 16, :].astype(F32)
                rsum[l, :, at : at + 256] += part[0:8]
            rows_out[l] = rsum[l, :, 0:768]

        def small_adds(l):
            for o in range(32):
                z, yl, yh, core = o // 8, (o // 4) % 2, (o // 2) % 2, o % 2
                at = (96 * o) // 128 * 128
                part = vv[z, yl, yh, core, 16 * l : 16 * l + 16, :].astype(F32)
                usum[l, 0:1, at : at + 256] += part[8:9]
            add_out[l] = usum[l, :, 0:3072]

        small_rows(0)
        rows, up_add = rows_out.at[0], add_out.at[0]
    else:
        load(wj, vj)
        for i in feed:
            plan.start(i, 0)
        plan.relay_all(0, 0)
        plan.close_all(0, 0)
        rows, up_add = rows.at[1], up_add.at[1]

    def joint_columns(start):
        return vj[:, :, :, :, :, start : start + 768].reshape(768, 768)

    sends = []

    def send(src, dst, s, r, place):
        copy = remote(src, dst, s, r, place)
        copy.start()
        sends.append(copy)

    def arrived(slot, s, r, place):
        remote(slot, slot, s, r, place).wait_recv()

    if not first:
        loads[0].wait()
    for j in (1, 2, 0):
        p = mxu(hid[...], joint_columns(768 * j))
        if j == 0:
            p = p + rows[0:1]
        if j == 2:
            p = p + rows[1:2]
        p = p.astype(BF).astype(F32)
        if j == 0:
            p = p * 0.125
        p = p.T.astype(BF)
        for g in range(4):
            qs[g, 192 * j : 192 * j + 192] = p[192 * g : 192 * g + 192]
        if j == 2:
            kvb[k, x] = qs[x, 192:576]
            for s in (2, 1, 3):
                peer = peer_of(me, "x", s)
                send(
                    qs.at[peer["x"], 192:576], kvb.at[k, x], xsend.at[s - 1], xrecv.at[s - 1], peer
                )
            send(kvb.at[k, x], kvb.at[k, x], ysend.at[0], yrecv.at[0], across)
            send(kvb.at[k, x], kvb.at[k, x], csend.at[0], crecv.at[0], partner)
    qb[x] = qs[x, 0:192]
    for s in (2, 1, 3):
        peer = peer_of(me, "x", s)
        send(qs.at[peer["x"], 0:192], qb.at[x], qsend.at[s - 1], qrecv.at[s - 1], peer)
    if first:
        small_rows(1)
        small_adds(0)
        small_adds(1)
        plan.relay_all(1, 0)
        plan.close_all(1, 0)
        for i in later:
            plan.start(i, 0)
    else:
        plan.relay_all(1, 0)
        plan.relay_all(0, 1, 2)
        plan.close_all(1, 0)
        plan.close_all(0, 1, 2)
    for s in (1, 3, 2):
        source = peer_of(me, "x", 4 - s)
        slot = kvb.at[k, source["x"]]
        arrived(slot, xsend.at[s - 1], xrecv.at[s - 1], source)
        send(slot, slot, ysend.at[s], yrecv.at[s], across)
        send(slot, slot, csend.at[s], crecv.at[s], partner)
    if first:
        plan.relay_all(1, 1, 2, 5)
        plan.relay_all(0, *later)
    for s in (1, 3, 2):
        source = peer_of(me, "x", 4 - s)
        arrived(qb.at[source["x"]], qsend.at[s - 1], qrecv.at[s - 1], source)
    for s in (0, 1, 3, 2):
        arrived(kvb.at[k_partner, (x + 4 - s) % 4], csend.at[s], crecv.at[s], partner)

    length = lens[0]
    queries = [
        jnp.concatenate([qb[xs, 64 * n : 64 * n + 64] for xs in range(4)], axis=1)
        for n in range(3)
    ]

    def half(b0, b1, old):
        def scores(i, peaks):
            b = b0 + (b1 - b0) * (i // 4)
            xs = i % 4
            bias = key_bias(length, b, xs)
            bias = jnp.concatenate([bias] * 4, axis=1)
            new = []
            for n in range(3):
                keys = kvb[b, xs, 64 * n : 64 * n + 64, :]
                st = mxu(keys, queries[n], NEAR) + bias
                sc[n, pl.ds(pl.multiple_of(i * KEYS, KEYS), KEYS), :] = st
                new.append(jnp.maximum(peaks[n], jnp.max(st.reshape(16, 8, 512), axis=0)))
            return tuple(new)

        start = tuple(jnp.full((8, 512), MASKED, F32) for _ in range(3))
        peaks = lax.fori_loop(0, 8, scores, start)
        peaks = [jnp.max(p, axis=0, keepdims=True) for p in peaks]
        if old is not None:
            peaks = [jnp.maximum(p, o[0]) for p, o in zip(peaks, old)]
        totals = []
        for n in range(3):
            if old is None:
                acc[n] = jnp.zeros((64, 512), F32)
                totals.append(jnp.zeros((8, 512), F32))
            else:
                shrink = jnp.exp(old[n][0] - peaks[n])
                acc[n] = acc[n] * shrink
                totals.append(old[n][1] * shrink)

        def mix(i, sums):
            b = b0 + (b1 - b0) * (i // 2)
            xs = (i % 2) * 2
            new = []
            for n in range(3):
                at = pl.ds(pl.multiple_of(i * 256, 256), 256)
                p = jnp.exp(sc[n, at, :] - peaks[n])
                new.append(sums[n] + jnp.sum(p.reshape(32, 8, 512), axis=0))
                v = slice(192 + 64 * n, 256 + 64 * n)
                values = jnp.concatenate([kvb[b, xs, v, :], kvb[b, xs + 1, v, :]], axis=1)
                acc[n] += mxu(values, p.astype(BF))
            return tuple(new)

        totals = lax.fori_loop(0, 4, mix, tuple(totals))
        return list(zip(peaks, totals))

    state = half(k, k_partner, None)
    if first:
        plan.close_all(0, *later)
        plan.close_all(1, 1, 2, 5)
        plan.relay_all(2, 0)
    else:
        plan.relay_all(1, 1, 2)
        plan.relay_all(2, 0)
    for s in (0, 1, 3, 2):
        slot = kvb.at[k_across, (x + 4 - s) % 4]
        arrived(slot, ysend.at[s], yrecv.at[s], across)
        send(slot, slot, fsend.at[s], frecv.at[s], partner)
    for s in (0, 1, 3, 2):
        arrived(kvb.at[k_diag, (x + 4 - s) % 4], fsend.at[s], frecv.at[s], partner)
    keep = pltpu.make_async_copy(kvb, kv_out, osem)
    keep.start()
    state = half(k_across, k_diag, state)
    log_out[...] = jnp.zeros_like(log_out)
    for n in range(3):
        total = jnp.sum(state[n][1], axis=0, keepdims=True)
        mixed = acc[n] / total
        att_out[64 * n : 64 * n + 64, :] = mixed
        log_out[n : n + 1, :] = state[n][0] + jnp.log(total)
        for xs in range(4):
            back[xs, 64 * n : 64 * n + 64, :] = mixed[:, 128 * xs : 128 * xs + 128].astype(BF)
    ab[x] = back[x]
    for s in (2, 1, 3):
        peer = peer_of(me, "x", s)
        send(back.at[peer["x"]], ab.at[x], bsend.at[s - 1], brecv.at[s - 1], peer)
    q_out[...] = qb[...]
    if first:
        plan.relay_all(1, *later)
    else:
        plan.close_all(1, 1, 2)
    plan.close_all(2, 0)
    for i in feed:
        plan.complete(i)
    if first:
        load(vj, gathered[2])
    load(vu, gathered[0])
    load(vd, gathered[1])
    for s in (1, 3, 2):
        source = peer_of(me, "x", 4 - s)
        arrived(ab.at[source["x"]], bsend.at[s - 1], brecv.at[s - 1], source)
    mixed = ab[...].reshape(768, 128).astype(F32).T.astype(BF)
    mixed_out[...] = mixed
    before = hid[...].astype(F32) + (mxu(mixed, joint_columns(2304)) + rows[2:3])
    before1_out[...] = before
    first_norm = normalized(before)[0] * rows[3:4] + rows[4:5]
    low = first_norm.astype(BF)
    low_out[...] = low
    second = first_norm + rows[5:6]
    for q in range(4):
        at = slice(768 * q, 768 * q + 768)
        u = mxu(low, vu[:, :, :, :, :, at].reshape(768, 768)) + up_add[0:1, at]
        up_out[:, at] = u
        a = (u * normal_cdf(u)).astype(BF)
        act_out[:, at] = a
        second = second + mxu(a, vd[q].reshape(768, 768))
    before2_out[...] = second
    res[...] = (normalized(second)[0] * rows[6:7] + rows[7:8]).astype(BF)
    keep.wait()
    if first:
        plan.close_all(1, *later)
        for i in later:
            plan.complete(i)
    plan.end()
    for copy in loads[0 if first else 1 :]:
        copy.wait()
    for copy in sends:
        copy.wait_send()


def forward_layer(first, hidden, lengths, known, shards):
    vmem = pl.BlockSpec(memory_space=pltpu.VMEM)
    anyspace = pl.BlockSpec(memory_space=pl.ANY)
    dma = pltpu.SemaphoreType.DMA
    out = jax.ShapeDtypeStruct
    n = len(FIRST_PIECES if first else SECOND_PIECES)
    got = [(24, 3072), (96, 768)]
    if first:
        got += [(24, 3072), (24, 3072)]
    return pl.pallas_call(
        functools.partial(forward_kernel, first),
        out_shape=[
            out((128, 768), BF),
            out((4, 192, 128), BF),
            out((4, 4, 384, 128), BF),
            out((8, 512), F32),
            out((192, 512), F32),
            out((128, 768), BF),
            out((128, 768), F32),
            out((128, 768), BF),
            out((128, 3072), F32),
            out((128, 3072), BF),
            out((128, 768), F32),
        ]
        + ([out((2, 8, 768), F32), out((2, 8, 3072), F32)] if first else [])
        + [out((4, 2, 2, 2, *s), BF) for s in got],
        in_specs=[vmem, pl.BlockSpec(memory_space=pltpu.SMEM)]
        + ([vmem] * 9 if first else [vmem, vmem, anyspace])
        + [anyspace] * len(shards),
        out_specs=[vmem, vmem, anyspace]
        + [vmem] * (10 if first else 8)
        + [anyspace] * len(got),
        scratch_shapes=[
            pltpu.VMEM((4, 2, 2, 2, 24, 3072), BF),
            pltpu.VMEM((4, 2, 2, 2, 24, 3072), BF),
            pltpu.VMEM((4, 2, 2, 2, 96, 768), BF),
            pltpu.VMEM((4, 576, 128), BF),
            pltpu.VMEM((4, 192, 128), BF),
            pltpu.VMEM((4, 4, 384, 128), BF),
            pltpu.VMEM((3, 1024, 512), F32),
            pltpu.VMEM((3, 64, 512), F32),
            pltpu.VMEM((4, 192, 128), BF),
            pltpu.VMEM((4, 192, 128), BF),
            pltpu.VMEM((4, 2, 2, 2, 32, 256), BF),
            pltpu.VMEM((2, 8, 896), F32),
            pltpu.VMEM((2, 8, 3200), F32),
            dma((4,)),
            dma,
            dma((3,)),
            dma((3,)),
            dma((3,)),
            dma((3,)),
            dma((4,)),
            dma((4,)),
            dma((4,)),
            dma((4,)),
            dma((4,)),
            dma((4,)),
            dma((3,)),
            dma((3,)),
            pltpu.VMEM((32, 256), F32),
            pltpu.VMEM((32, 256), BF),
            dma((n, 3, 4)),
            dma((n, 3, 4)),
            dma((n, 4, 3)),
            dma((n, 4, 3)),
            dma((n,)),
        ],
        compiler_params=pltpu.CompilerParams(
            collective_id=2 if first else 0,
            has_side_effects=True,
            vmem_limit_bytes=60 * 1024 * 1024,
        ),
        name="forward_first" if first else "forward_second",
    )(hidden, lengths, *known, *shards)


def backward_kernel(layer, *refs):
    refs = list(refs)

    def take(count):
        out = refs[:count]
        del refs[:count]
        return out

    beside = layer == 0
    dy, rows, up, before2, before1, qb, kvb, logs, att, lens, wj, wu, wd = take(13)
    operands = take(5) if beside else None
    dh_out, dj_out, db_out, du_out, df_out, vec_out = take(6)
    sums_out = take(1)[0] if beside else None
    vj, vu, vd, das, dab, dkv, rx, ry, rl, py, dq, sb, dj = take(13)
    wsem, asend, arecv, csend, crecv, jsend, jrecv = take(7)
    rows = rows.at[layer]
    me = my_place()
    x, c = me["x"], me["c"]
    yh = me["y"] // 2
    partner, across = peer_of(me, "c", 1), peer_of(me, "y", 2)
    loads = []
    for q in range(4):
        at = slice(768 * q, 768 * q + 768)
        for a, b in ((wd.at[at], vd.at[at]), (wu.at[:, at], vu.at[:, at])):
            loads.append(pltpu.make_async_copy(a, b, wsem.at[len(loads)]))
    loads.append(pltpu.make_async_copy(wj, vj, wsem.at[8]))
    for copy in loads:
        copy.start()
    if beside:
        reducer = Reducer(me, operands, refs[:8], sums_out, refs[8:])
        greet_all(me)
        reducer.exchange()
    else:
        greet_sequence(me)
    sends = []

    def send(src, dst, s, r, place):
        copy = remote(src, dst, s, r, place)
        copy.start()
        sends.append(copy)

    def arrived(slot, s, r, place):
        remote(slot, slot, s, r, place).wait_recv()

    def column_sum(a):
        return jnp.sum(a.astype(F32), axis=0, keepdims=True)

    vec_out[...] = jnp.zeros_like(vec_out)
    d_second, gain_grad, shift_grad = norm_backward(before2[...], rows[6:7], dy[...].astype(F32))
    vec_out[6:7] = gain_grad
    vec_out[7:8] = shift_grad
    df = d_second.astype(BF)
    df_out[...] = df
    vec_out[5:6] = column_sum(df)
    d_first = d_second
    for q in range(4):
        loads[2 * q].wait()
        loads[2 * q + 1].wait()
        at = slice(768 * q, 768 * q + 768)
        u = up[:, at]
        slope = normal_cdf(u) + u * (0.3989422804014327 * jnp.exp(-0.5 * u * u))
        du = (mxu(df, vd[at, :], FAR) * slope).astype(BF)
        du_out[:, at] = du
        vec_out[8 + q : 9 + q] = column_sum(du)
        d_first = d_first + mxu(du, vu[:, at], FAR)
    d_sum, gain_grad, shift_grad = norm_backward(before1[...], rows[3:4], d_first)
    vec_out[3:4] = gain_grad
    vec_out[4:5] = shift_grad
    db = d_sum.astype(BF)
    db_out[...] = db
    vec_out[2:3] = column_sum(db)
    dh_out[...] = d_sum
    loads[8].wait()
    da = mxu(db, vj[:, 2304:3072], FAR).T.astype(BF)
    for g in range(4):
        das[g] = da[192 * g : 192 * g + 192]
    dab[x] = das[x]
    for s in (2, 1, 3):
        peer = peer_of(me, "x", s)
        send(das.at[peer["x"]], dab.at[x], asend.at[s - 1], arecv.at[s - 1], peer)
    if beside:
        for third in range(3):
            reducer.products(third)
    for s in (1, 3, 2):
        source = peer_of(me, "x", 4 - s)
        arrived(dab.at[source["x"]], asend.at[s - 1], arecv.at[s - 1], source)
    length = lens[0]

    def by_head(ref, n):
        return jnp.concatenate([ref[xs, 64 * n : 64 * n + 64] for xs in range(4)], axis=1)

    inner = []
    for n in range(3):
        dq[n] = jnp.zeros((64, 512), F32)
        inner.append(
            jnp.sum(
                by_head(dab, n).astype(F32) * att[64 * n : 64 * n + 64, :], axis=0, keepdims=True
            )
        )

    def half(which, base):
        def step(i, carry):
            core, xs = i // 4, i % 4
            b = base + core
            bias = key_bias(length, b, xs)
            bias = jnp.concatenate([bias] * 2, axis=1)
            for n in range(3):
                own = slice(64 * n, 64 * n + 64)
                keys = kvb[b, xs, own, :]
                values = kvb[b, xs, slice(192 + 64 * n, 256 + 64 * n), :]
                dk = dv = None
                for h in range(2):
                    at = slice(256 * h, 256 * h + 256)
                    q_n = jnp.concatenate([qb[2 * h, own], qb[2 * h + 1, own]], axis=1)
                    da_n = jnp.concatenate([dab[2 * h, own], dab[2 * h + 1, own]], axis=1)
                    p = jnp.exp(mxu(keys, q_n, NEAR) + bias - logs[n : n + 1, at])
                    dp = mxu(values, da_n, NEAR)
                    ds = (p * (dp - inner[n][:, at])).astype(BF)
                    dq[n, :, at] += mxu(keys, ds)
                    k_term = mxu(q_n, ds, FAR)
                    v_term = mxu(da_n, p.astype(BF), FAR)
                    dk = k_term if dk is None else dk + k_term
                    dv = v_term if dv is None else dv + v_term
                dkv[which, core, xs, 64 * n : 64 * n + 64, :] = dk.astype(BF)
                dkv[which, core, xs, 192 + 64 * n : 256 + 64 * n, :] = dv.astype(BF)
            return carry

        lax.fori_loop(0, 8, step, 0)

    half(0, (1 - yh) * 2)
    send(dkv.at[0, 1 - c], rx, csend.at[0], crecv.at[0], partner)
    arrived(rx, csend.at[0], crecv.at[0], partner)
    for xs in range(4):
        py[xs] = (dkv[0, c, xs].astype(F32) + rx[xs].astype(F32)).astype(BF)
    send(py, ry, csend.at[1], crecv.at[1], across)
    if beside:
        for third in range(3):
            reducer.middle(0, third)
    half(1, yh * 2)
    send(dkv.at[1, 1 - c], rl, csend.at[2], crecv.at[2], partner)
    if beside:
        for third in range(3):
            reducer.finish(0, third)
    for xs in range(4):
        for n in range(3):
            part = dq[n, :, 128 * xs : 128 * xs + 128] * 0.125
            sb[xs, 64 * n : 64 * n + 64, :] = part.astype(BF)
    arrived(rl, csend.at[2], crecv.at[2], partner)
    arrived(ry, csend.at[1], crecv.at[1], across)
    for xs in range(4):
        total = dkv[1, c, xs].astype(F32) + rl[xs].astype(F32) + ry[xs].astype(F32)
        sb[xs, 192:576, :] = total.astype(BF)
    dj[x] = sb[x]
    for s in (2, 1, 3):
        peer = peer_of(me, "x", s)
        send(sb.at[peer["x"]], dj.at[x], jsend.at[s - 1], jrecv.at[s - 1], peer)
    if beside:
        for third in range(3):
            reducer.middle(1, third)
    for s in (1, 3, 2):
        source = peer_of(me, "x", 4 - s)
        arrived(dj.at[source["x"]], jsend.at[s - 1], jrecv.at[s - 1], source)
    dh = dh_out[...]
    for j in range(3):
        at = slice(768 * j, 768 * j + 768)
        t = jnp.concatenate([dj[g, 192 * j : 192 * j + 192] for g in range(4)], axis=0)
        t = t.astype(F32).T.astype(BF)
        dj_out[:, at] = t
        if j != 1:
            row = 0 if j == 0 else 1
            vec_out[row : row + 1] = column_sum(t)
        dh = dh + mxu(t, vj[:, at], FAR)
    dh_out[...] = dh
    if beside:
        for third in range(3):
            reducer.finish(1, third)
        reducer.end()
    for copy in sends:
        copy.wait_send()


def backward_layer(layer, dy, rows, up, before2, before1, q, kv, logs, att, lengths, wj, wu, wd, later):
    vmem = pl.BlockSpec(memory_space=pltpu.VMEM)
    anyspace = pl.BlockSpec(memory_space=pl.ANY)
    dma = pltpu.SemaphoreType.DMA
    out = jax.ShapeDtypeStruct
    return pl.pallas_call(
        functools.partial(backward_kernel, layer),
        out_shape=[
            out((128, 768), F32),
            out((128, 2304), BF),
            out((128, 768), BF),
            out((128, 3072), BF),
            out((128, 768), BF),
            out((16, 768), F32),
        ]
        + ([out((3, 4, 24, 768), BF)] if layer == 0 else []),
        in_specs=[vmem] * 9
        + [pl.BlockSpec(memory_space=pltpu.SMEM)]
        + [anyspace] * (3 + len(later)),
        out_specs=[vmem] * (7 if layer == 0 else 6),
        scratch_shapes=[
            pltpu.VMEM((768, 3072), BF),
            pltpu.VMEM((768, 3072), BF),
            pltpu.VMEM((3072, 768), BF),
            pltpu.VMEM((4, 192, 128), BF),
            pltpu.VMEM((4, 192, 128), BF),
            pltpu.VMEM((2, 2, 4, 384, 128), BF),
            pltpu.VMEM((4, 384, 128), BF),
            pltpu.VMEM((4, 384, 128), BF),
            pltpu.VMEM((4, 384, 128), BF),
            pltpu.VMEM((4, 384, 128), BF),
            pltpu.VMEM((3, 64, 512), F32),
            pltpu.VMEM((4, 576, 128), BF),
            pltpu.VMEM((4, 576, 128), BF),
            dma((9,)),
            dma((3,)),
            dma((3,)),
            dma((3,)),
            dma((3,)),
            dma((3,)),
            dma((3,)),
        ]
        + (reducer_buffers() + reducer_semaphores() if layer == 0 else []),
        compiler_params=pltpu.CompilerParams(
            collective_id=3 + layer, has_side_effects=True, vmem_limit_bytes=60 * 1024 * 1024
        ),
        name="backward_layer",
    )(dy, rows, up, before2, before1, q, kv, logs, att, lengths, wj, wu, wd, *later)


def body(
    inputs,
    lengths,
    joint_weight,
    query_bias,
    value_bias,
    output_weight,
    output_bias,
    first_gain,
    first_shift,
    up_weight,
    up_bias,
    down_weight,
    down_bias,
    second_gain,
    second_shift,
    cotangent,
):
    small = (
        query_bias,
        value_bias,
        output_bias,
        first_gain,
        first_shift,
        down_bias,
        second_gain,
        second_shift,
        up_bias,
    )
    joint_and_out = jnp.concatenate([joint_weight, output_weight], axis=-1)
    hidden0 = inputs.reshape(128, 768)
    got = forward_layer(
        True,
        hidden0,
        lengths,
        small,
        (up_weight, down_weight, joint_and_out),
    )
    rows_all, up_adds, up0, down0, joint0, joint1 = got[11:]
    more = forward_layer(
        False, got[0], lengths, (rows_all, up_adds, joint1), (up_weight, down_weight)
    )
    up1, down1 = more[11:]
    weights_of = [
        (j.reshape(768, 3072), u.reshape(768, 3072), d.reshape(3072, 768))
        for j, u, d in ((joint0, up0, down0), (joint1, up1, down1))
    ]
    kept = [(hidden0, *got[1:11]), (got[0], *more[1:11])]
    outputs = [got[0].reshape(1, 128, 768), more[0].reshape(1, 128, 768)]
    grad_rows = cotangent.reshape(128, 768)
    vector_grads = [None] * LAYERS
    later = ()
    for l in reversed(range(LAYERS)):
        hidden, q, kv, logs, att, mixed, before1, low, up, acts, before2 = kept[l]
        grad_rows, d_joint, d_branch, d_up, d_down, vector_grads[l], *sums = backward_layer(
            l,
            grad_rows,
            rows_all,
            up,
            before2,
            before1,
            q,
            kv,
            logs,
            att,
            lengths,
            *weights_of[l],
            later,
        )
        later = reducer_operands(hidden, mixed, low, acts, d_joint, d_branch, d_up, d_down)
    joint_grad, out_grad, up_grad, down_grad, vectors = reduce_grads(
        later, sums[0], vector_grads
    )
    vectors = vectors.reshape(LAYERS, 16, 768)
    owner = lax.axis_index("batch") * 4 + lax.axis_index("blk")
    own_rows = lax.dynamic_slice_in_dim(vectors[:, :8], owner * 24, 24, axis=2)
    own_up = lax.dynamic_slice_in_dim(vectors[:, 8:12].reshape(LAYERS, 3072), owner * 96, 96, axis=1)
    stacked = (
        joint_grad,
        own_rows[:, 0],
        own_rows[:, 1],
        out_grad,
        own_rows[:, 2],
        own_rows[:, 3],
        own_rows[:, 4],
        up_grad,
        own_up,
        down_grad,
        own_rows[:, 5],
        own_rows[:, 6],
        own_rows[:, 7],
    )
    activations = jnp.stack(outputs)
    input_grad = grad_rows.reshape(1, 128, 768)
    return (
        activations,
        input_grad,
        stacked[0],
        stacked[1],
        stacked[2],
        stacked[3],
        stacked[4],
        stacked[5],
        stacked[6],
        stacked[7],
        stacked[8],
        stacked[9],
        stacked[10],
        stacked[11],
        stacked[12],
    )


def solution(mesh):
    placed = (
        P("batch", ("head", "blk"), None),
        P("batch"),
        P(None, ("batch", "blk"), None),
        P(None, ("batch", "blk")),
        P(None, ("batch", "blk")),
        P(None, ("batch", "blk"), None),
        P(None, ("batch", "blk")),
        P(None, ("batch", "blk")),
        P(None, ("batch", "blk")),
        P(None, ("batch", "blk"), None),
        P(None, ("batch", "blk")),
        P(None, ("batch", "blk"), None),
        P(None, ("batch", "blk")),
        P(None, ("batch", "blk")),
        P(None, ("batch", "blk")),
        P("batch", ("head", "blk"), None),
    )
    return jax.shard_map(
        body,
        mesh=mesh,
        in_specs=placed,
        out_specs=(
            P(None, "batch", ("head", "blk"), None),
            P("batch", ("head", "blk"), None),
            P(None, ("batch", "blk"), None),
            P(None, ("batch", "blk")),
            P(None, ("batch", "blk")),
            P(None, ("batch", "blk"), None),
            P(None, ("batch", "blk")),
            P(None, ("batch", "blk")),
            P(None, ("batch", "blk")),
            P(None, ("batch", "blk"), None),
            P(None, ("batch", "blk")),
            P(None, ("batch", "blk"), None),
            P(None, ("batch", "blk")),
            P(None, ("batch", "blk")),
            P(None, ("batch", "blk")),
        ),
        check_vma=False,
    )
```
